32 devices in a mesh: grp: 2 (over x), head: 8 (over z, y), ctx: 2 (over core).
Axes of the slice: x: 2, y: 2, z: 4, core: 2. Of those that a mesh axis runs over, the one named last changes fastest.
Arguments:
- x_seq: bfloat16 [4096, 4096], P(('grp', 'ctx', 'head')), parts along dimension 0, may hold values from -6 to 6
- dy_seq: bfloat16 [4096, 4096], P(('grp', 'ctx', 'head')), parts along dimension 0, may hold values from -0.59765625 to 0.59765625
- dt_seq: bfloat16 [4096, 64], P(('grp', 'ctx', 'head')), parts along dimension 0, may hold values from 0.5 to 2
- a_log: float32 [64], replicated, may hold values from -13 to -2.9
- b_seq: bfloat16 [4096, 8, 128], P(('grp', 'ctx', 'head')), parts along dimension 0, may hold values from -0.5 to 0.5
- c_seq: bfloat16 [4096, 8, 128], P(('grp', 'ctx', 'head')), parts along dimension 0, may hold values from -0.5 to 0.5
Outputs:
- dx_seq: bfloat16 [4096, 4096], P(('grp', 'ctx', 'head')), parts along dimension 0
- ddt_seq: bfloat16 [4096, 64], P(('grp', 'ctx', 'head')), parts along dimension 0
- db_seq: bfloat16 [4096, 8, 128], P(('grp', 'ctx', 'head')), parts along dimension 0
- dc_seq: bfloat16 [4096, 8, 128], P(('grp', 'ctx', 'head')), parts along dimension 0
The draws below stay inside these ranges and needn't reach their ends.
There are 2 independent parts, one for each index of `grp`. The reference program is written for one: setup_inputs(seed, part) draws one part's arguments, and reference() takes and returns one part's arrays. A program takes and returns all parts, laid end to end along the dimension named above; an argument that names none is the same for every part. Nothing has to cross between parts.
All inputs are finite; a program needn't handle non-finite values.
Results may differ from the reference program's by a relative error of at most 0.001.
Values may be sent and summed in bfloat16 or wider, within the bound.
No kernel may reach another device: no remote copies, remote signals or barrier semaphores. Data moves between devices by JAX's collectives and lax.ppermute only.
A program may use at most 128 MiB of HBM per device.

```python
import math
import jax
import jax.numpy as jnp
from jax import lax

HEADS = 64
HEAD_DIM = 64
STATE = 128
GROUPS = 8
STRETCH = 256
TOKENS = 2048
N_HEAD = 8


def draw_a_log(key, part):
    key = jax.random.fold_in(key, 11)
    key_pick, key_slow, key_fast = jax.random.split(key, 3)
    share = 0.5
    slow_pick = jax.random.uniform(key_pick, (HEADS,)) < share
    slow_log = jnp.log(0.1 / TOKENS) + jax.random.uniform(key_slow, (HEADS,)) * jnp.log(20.0)
    fast_log = jnp.log(0.02) + jax.random.uniform(key_fast, (HEADS,)) * jnp.log(2.5)
    return jnp.where(slow_pick, slow_log, fast_log).astype(jnp.float32)


def block_levels(own_key, shape, cuts, smallest, top_value):
    factor_of, own = 1.0, jax.random.fold_in(own_key, 6)
    for axis_at, parts in cuts:
        steps = jnp.exp(jax.random.uniform(jax.random.fold_in(own, axis_at), (parts,), jnp.float32, smallest / len(cuts), top_value / len(cuts)))
        factor_of = factor_of * jnp.repeat(steps, shape[axis_at] // parts).reshape([-1 if axis == axis_at else 1 for axis in range(len(shape))])
    return factor_of


def normal_values(own_key, shape, deviation, limit, cuts=(), kind=jnp.bfloat16):
    values = deviation * jax.random.normal(own_key, shape, jnp.float32)
    if cuts:
        values = values * block_levels(own_key, shape, cuts, -0.22, 0.18)
    return jnp.clip(values, -limit, limit).astype(kind)


def setup_inputs(seed: int = 0, part: int = 0) -> dict:
    seeds = jax.random.split(jax.random.key(seed), 7)
    part_splits = jax.random.split(jax.random.fold_in(seeds[6], part), 7)
    return {
        "x_seq": normal_values(part_splits[0], (TOKENS, HEADS * HEAD_DIM), 1.0, 6.0, ((0, 16),)),
        "dy_seq": normal_values(part_splits[1], (TOKENS, HEADS * HEAD_DIM), 0.1, 0.59765625, ((0, 16),)),
        "dt_seq": jnp.clip(jnp.exp(math.log(2.0) - 1.3862944 * jax.random.uniform(part_splits[2], (TOKENS, HEADS), jnp.float32) ** block_levels(part_splits[2], (TOKENS, HEADS), ((0, 16),), -0.2, 0.2)), 0.5, 2.0).astype(jnp.bfloat16),
        "a_log": draw_a_log(jax.random.fold_in(seeds[6], 71), part),
        "b_seq": normal_values(part_splits[4], (TOKENS, GROUPS, STATE), STATE ** -0.5, 0.5, ((0, 16),)),
        "c_seq": normal_values(part_splits[5], (TOKENS, GROUPS, STATE), STATE ** -0.5, 0.5, ((0, 16),)),
    }


highest = lax.Precision.HIGHEST


def stretch_local(x_head, dy_head, dt_head, b_head, c_head, decay_rate):
    dt_full = dt_head.astype(jnp.float32)
    cum_log = jnp.cumsum(dt_full * decay_rate, axis=1)
    end_log = cum_log[:, -1]
    to_end = jnp.exp(end_log[:, None] - cum_log)
    from_start = jnp.exp(cum_log)
    x_scaled = dt_full[..., None] * x_head.astype(jnp.float32)
    states_loc = jnp.einsum("cqp,cqn->cpn", x_scaled * to_end[..., None], b_head.astype(jnp.float32), precision=highest)
    grads_loc = jnp.einsum("cqp,cqn->cpn", dy_head.astype(jnp.float32) * from_start[..., None], c_head.astype(jnp.float32), precision=highest)
    return cum_log, states_loc, grads_loc


def chains(end_log, states_loc, grads_loc):
    factor = jnp.exp(end_log)
    zero_state = jnp.zeros(states_loc.shape[1:], jnp.float32)

    def forward(carry, item):
        return item[0] * carry + item[1], carry

    def backward(carry, item):
        return item[0] * carry + item[1], carry

    state_out, state_in = lax.scan(forward, zero_state, (factor, states_loc))
    grad_out, grad_in = lax.scan(backward, zero_state, (factor, grads_loc), reverse=True)
    return state_in, grad_in, state_out, grad_out


def stretch_grads(x_head, dy_head, dt_head, b_head, c_head, decay_rate, cum_log, state_in, grad_in):
    dt_full = dt_head.astype(jnp.float32)
    x_wide = x_head.astype(jnp.float32)
    dy_wide = dy_head.astype(jnp.float32)
    b_wide = b_head.astype(jnp.float32)
    c_wide = c_head.astype(jnp.float32)
    x_scaled = dt_full[..., None] * x_wide
    end_log = cum_log[:, -1]
    to_end = jnp.exp(end_log[:, None] - cum_log)
    from_start = jnp.exp(cum_log)
    span = cum_log.shape[1]
    lower_mask = jnp.arange(span)[:, None] >= jnp.arange(span)[None, :]
    log_gap = cum_log[:, :, None] - cum_log[:, None, :]
    decay_mat = jnp.where(lower_mask, jnp.exp(jnp.minimum(log_gap, 0.0)), 0.0)
    k_one = jnp.einsum("cip,cjp->cij", dy_wide, x_wide, precision=highest) * dt_full[:, None, :]
    k_two = jnp.einsum("cin,cjn->cij", c_wide, b_wide, precision=highest)
    a_one = decay_mat * k_one
    a_two = decay_mat * k_two
    b_state = jnp.einsum("cin,cpn->cip", b_wide, grad_in, precision=highest)
    c_state = jnp.einsum("cin,cpn->cip", c_wide, state_in, precision=highest)
    dxbar = jnp.einsum("cki,ckp->cip", a_two, dy_wide, precision=highest) + to_end[..., None] * b_state
    dcol = from_start[..., None] * jnp.einsum("cip,cpn->cin", dy_wide, state_in, precision=highest)
    dcol = dcol + jnp.einsum("cij,cjn->cin", a_one, b_wide, precision=highest)
    drow = jnp.einsum("cki,ckn->cin", a_one, c_wide, precision=highest)
    drow = drow + to_end[..., None] * jnp.einsum("cip,cpn->cin", x_scaled, grad_in, precision=highest)
    box_terms = a_one * k_two
    col_sums = jnp.sum(box_terms, axis=1)
    row_sums = jnp.sum(box_terms, axis=2)
    box_sum = jnp.cumsum(col_sums, axis=1) - jnp.cumsum(row_sums, axis=1) + row_sums
    later_terms = from_start * jnp.sum(dy_wide * c_state, axis=-1)
    early_terms = to_end * jnp.sum(x_scaled * b_state, axis=-1)
    suffix_sum = jnp.flip(jnp.cumsum(jnp.flip(later_terms, 1), axis=1), 1)
    head_sum = jnp.cumsum(early_terms, axis=1)
    corner = jnp.exp(end_log) * jnp.sum(grad_in * state_in, axis=(1, 2))
    dlog_step = box_sum + suffix_sum + head_sum + corner[:, None] - jnp.sum(dxbar * x_scaled, axis=-1)
    grad_dt = jnp.sum(dxbar * x_wide, axis=-1) + decay_rate * dlog_step
    return dt_full[..., None] * dxbar, grad_dt, drow, dcol


def rounded(value):
    return lax.optimization_barrier(value.astype(jnp.bfloat16)).astype(jnp.float32)


def reference(x_seq, dy_seq, dt_seq, a_log, b_seq, c_seq):
    length = x_seq.shape[0]
    count = length // STRETCH
    per_group = HEADS // GROUPS
    block_size = min(HEADS // N_HEAD, HEADS // GROUPS)
    x_split = x_seq.reshape(count, STRETCH, HEADS, HEAD_DIM)
    dy_split = dy_seq.reshape(count, STRETCH, HEADS, HEAD_DIM)
    dt_split = dt_seq.reshape(count, STRETCH, HEADS)
    b_split = b_seq.reshape(count, STRETCH, GROUPS, STATE)
    c_split = c_seq.reshape(count, STRETCH, GROUPS, STATE)
    rates = -jnp.exp(a_log)

    def one_group(group):
        b_head = lax.dynamic_index_in_dim(b_split, group, 2, keepdims=False)
        c_head = lax.dynamic_index_in_dim(c_split, group, 2, keepdims=False)

        def one_head(carry, member):
            head_id = (group * per_group + member).astype(jnp.int32)
            x_head = lax.dynamic_index_in_dim(x_split, head_id, 2, keepdims=False)
            dy_head = lax.dynamic_index_in_dim(dy_split, head_id, 2, keepdims=False)
            dt_head = lax.dynamic_index_in_dim(dt_split, head_id, 2, keepdims=False)
            decay_rate = lax.dynamic_index_in_dim(rates, head_id, 0, keepdims=False)
            cum_log, states_loc, grads_loc = stretch_local(x_head, dy_head, dt_head, b_head, c_head, decay_rate)
            state_in, grad_in, unused_state, unused_grad = chains(cum_log[:, -1], states_loc, grads_loc)
            dx_head, ddt_head, db_head, dc_head = stretch_grads(x_head, dy_head, dt_head, b_head, c_head, decay_rate, cum_log, state_in, grad_in)
            db_part = carry[2] + db_head
            dc_part = carry[3] + dc_head
            closing = (member + 1) % block_size == 0
            db_total = jnp.where(closing, carry[0] + rounded(db_part), carry[0])
            dc_total = jnp.where(closing, carry[1] + rounded(dc_part), carry[1])
            db_part = jnp.where(closing, jnp.zeros_like(db_part), db_part)
            dc_part = jnp.where(closing, jnp.zeros_like(dc_part), dc_part)
            return (db_total, dc_total, db_part, dc_part), (dx_head.astype(jnp.bfloat16), ddt_head.astype(jnp.bfloat16))

        zero_sum = jnp.zeros((count, STRETCH, STATE), jnp.float32)
        sums, pieces = lax.scan(one_head, (zero_sum, zero_sum, zero_sum, zero_sum), jnp.arange(per_group).astype(jnp.int32))
        return sums[0], sums[1], pieces[0], pieces[1]

    db_all, dc_all, dx_all, ddt_all = lax.map(one_group, jnp.arange(GROUPS).astype(jnp.int32))
    db_out = db_all.transpose(1, 2, 0, 3).reshape(length, GROUPS, STATE).astype(jnp.bfloat16)
    dc_out = dc_all.transpose(1, 2, 0, 3).reshape(length, GROUPS, STATE).astype(jnp.bfloat16)
    dx_out = dx_all.transpose(2, 3, 0, 1, 4).reshape(length, HEADS * HEAD_DIM)
    ddt_out = ddt_all.transpose(2, 3, 0, 1).reshape(length, HEADS)
    return dx_out, ddt_out, db_out, dc_out
```

```python
import functools

import jax
import jax.numpy as jnp
from jax import lax
from jax.experimental import pallas as pl
from jax.experimental.pallas import tpu as pltpu
from jax.sharding import PartitionSpec as P

HEADS = 64
HEAD_DIM = 64
STATE = 128
GROUPS = 8
LANES = 128
ROWS = 8
DT_ROWS = 16
LOG2E = 1.4426950408889634
F32 = jnp.float32
BF16 = jnp.bfloat16


def split2(value):
    hi = value.astype(BF16)
    return hi, (value - hi.astype(F32)).astype(BF16)


def split3(value):
    hi = value.astype(BF16)
    rest = value - hi.astype(F32)
    mid = rest.astype(BF16)
    return hi, mid, (rest - mid.astype(F32)).astype(BF16)


def dot(a, b):
    return lax.dot_general(a, b, (((1,), (0,)), ((), ())), preferred_element_type=F32)


def dot_nt(a, b):
    return lax.dot_general(a, b, (((1,), (1,)), ((), ())), preferred_element_type=F32)


def dot_tn(a, b):
    return lax.dot_general(a, b, (((0,), (0,)), ((), ())), preferred_element_type=F32)


def cat(parts, axis):
    return jnp.concatenate(parts, axis=axis)


def upper(size, strict):
    row = lax.broadcasted_iota(jnp.int32, (size, size), 0)
    col = lax.broadcasted_iota(jnp.int32, (size, size), 1)
    return row < col if strict else row <= col


def cumulate(rows, strict):
    tri = upper(rows.shape[1], strict).astype(F32).astype(BF16)
    sums = dot(cat([part.astype(F32) for part in split3(rows)], 0).astype(BF16), tri)
    return sums[:ROWS] + sums[ROWS : 2 * ROWS] + sums[2 * ROWS :]


def spread_matrix(terms, width):
    row = lax.broadcasted_iota(jnp.int32, (terms * ROWS, width), 0)
    col = lax.broadcasted_iota(jnp.int32, (terms * ROWS, width), 1)
    return (row % ROWS == col // HEAD_DIM).astype(F32).astype(BF16)


def spread(cols, width):
    hi, lo = split2(cols)
    return dot(cat([hi.astype(F32), lo.astype(F32)], 1).astype(BF16), spread_matrix(2, width))


def steps_of(buf, first, rate):
    dt = buf[0, first : first + DT_ROWS, :].astype(F32)[:ROWS]
    return dt, cumulate(dt * rate, False)


def wide(buf, first, blocks, tokens):
    return cat([buf[0, first + i * tokens : first + (i + 1) * tokens, :] for i in range(blocks)], 1)


def states_kernel(blocks, tokens, width, flag_ref, rate_ref, buf_s, buf_g, s_ref, g_ref, before_ref, after_ref, send_ref, s_now, g_now, s_log, g_log):
    step, last = pl.program_id(0), pl.num_programs(0) - 1
    rate = rate_ref[...]
    b_row, c_row, dt_row = 2 * blocks * tokens, (2 * blocks + 1) * tokens, (2 * blocks + 2) * tokens

    @pl.when(step == 0)
    def _():
        s_now[...] = jnp.zeros_like(s_now)
        g_now[...] = jnp.zeros_like(g_now)
        s_log[...] = jnp.full_like(s_log, flag_ref[0])
        g_log[...] = jnp.full_like(g_log, flag_ref[1])

    dt, cum = steps_of(buf_s, dt_row, rate)
    end = cum[:, tokens - 1 :]
    cols = jnp.transpose(cat([dt * jnp.exp(end - cum), jnp.broadcast_to(jnp.exp(end), dt.shape)], 0))
    scale = spread(cols[:, :ROWS], width)
    through = spread(cols[:ROWS, ROWS:], width)
    hi, lo = split2(scale * wide(buf_s, 0, blocks, tokens).astype(F32))
    b_here = buf_s[0, b_row : b_row + tokens, :]
    s_ref[0] = s_now[...]
    before_ref[0] = s_log[...]
    s_now[...] = through[:1] * s_now[...] + dot_tn(cat([b_here, b_here], 0), cat([hi, lo], 0))
    s_log[...] = through * s_log[...]

    dt, cum = steps_of(buf_g, dt_row, rate)
    end = cum[:, tokens - 1 :]
    cols = jnp.transpose(cat([jnp.exp(cum), jnp.broadcast_to(jnp.exp(end), dt.shape)], 0))
    scale = spread(cols[:, :ROWS], width)
    through = spread(cols[:ROWS, ROWS:], width)
    hi, lo = split2(scale * wide(buf_g, blocks * tokens, blocks, tokens).astype(F32))
    c_here = buf_g[0, c_row : c_row + tokens, :]
    g_ref[0] = g_now[...]
    after_ref[0] = g_log[...]
    g_now[...] = through[:1] * g_now[...] + dot_tn(cat([c_here, c_here], 0), cat([hi, lo], 0))
    g_log[...] = through * g_log[...]

    @pl.when(step == last)
    def _():
        send_ref[...] = jnp.where(flag_ref[0] > 0.5, g_now[...], s_now[...])


def inner_kernel(blocks, tokens, width, rate_ref, buf, dxbar_ref, row_ref, db_ref, dc_ref):
    b_row, c_row, dt_row = 2 * blocks * tokens, (2 * blocks + 1) * tokens, (2 * blocks + 2) * tokens
    dt, cum = steps_of(buf, dt_row, rate_ref[...])
    cum = cum * LOG2E
    cols = jnp.transpose(cat([cum, dt], 0))
    dt_wide = spread(cols[:, ROWS:], width)
    b_here, c_here = buf[0, b_row : b_row + tokens, :], buf[0, c_row : c_row + tokens, :]
    k_two = dot_nt(b_here, c_here)
    mask = upper(tokens, False)
    left = lax.broadcasted_iota(jnp.int32, (tokens, LANES), 1) < HEAD_DIM
    none = jnp.zeros((tokens, LANES), F32)
    one_sum = jnp.zeros((tokens, tokens), F32)
    rows = []
    for block in range(blocks):
        x_here = buf[0, block * tokens : (block + 1) * tokens, :].astype(F32)
        dy_here = buf[0, (blocks + block) * tokens : (blocks + block + 1) * tokens, :]
        dy_f32 = dy_here.astype(F32)
        scaled = x_here * dt_wide[:, block * LANES : (block + 1) * LANES]
        hi = scaled.astype(BF16).astype(F32)
        lo = scaled - hi
        pair = cat(
            [
                cat([jnp.where(left, hi, none), jnp.where(left, lo, none)], 1),
                cat([jnp.where(left, none, hi), jnp.where(left, none, lo)], 1),
            ],
            0,
        ).astype(BF16)
        k_one = dot_nt(pair, cat([dy_here, dy_here], 1))
        tops, bottoms = [], []
        for side in range(2):
            head = 2 * block + side
            gap = jnp.where(mask, cum[head : head + 1, :] - cols[:, head : head + 1], -1e30)
            decay = jnp.exp2(gap)
            a_one = decay * k_one[side * tokens : (side + 1) * tokens]
            a_two = decay * k_two
            one_sum = one_sum + a_one
            rows.append(jnp.sum(a_one * k_two, axis=0, keepdims=True))
            hi_two, lo_two = split2(a_two)
            tops.append(hi_two)
            bottoms.append(lo_two)
        sides = cat([jnp.where(left, dy_f32, none), jnp.where(left, none, dy_f32)], 0).astype(BF16)
        both = dot(cat([cat(tops, 1), cat(bottoms, 1)], 0), sides)
        dxbar_ref[0, :, block * LANES : (block + 1) * LANES] = both[:tokens] + both[tokens:]
    if len(rows) < ROWS:
        rows.append(jnp.zeros((ROWS - len(rows), tokens), F32))
    row_ref[0] = cat(rows, 0)
    db_ref[0] = dot(cat(list(split2(one_sum)), 1), cat([c_here, c_here], 0))
    dc_ref[0] = dot(cat(list(split2(jnp.transpose(one_sum))), 1), cat([b_here, b_here], 0))


def outer_kernel(blocks, tokens, width, rate_ref, buf, state0, grad0, before, after, carried, dxbar_in, row_in, db_in, dc_in, out):
    b_row, c_row, dt_row = 2 * blocks * tokens, (2 * blocks + 1) * tokens, (2 * blocks + 2) * tokens
    rate = rate_ref[...]
    dt, cum = steps_of(buf, dt_row, rate)
    end = cum[:, tokens - 1 :]
    to_end, from_start = jnp.exp(end - cum), jnp.exp(cum)
    cols = jnp.transpose(cat([dt, to_end, from_start], 0))
    dt_wide = spread(cols[:, :ROWS], width)
    end_wide = spread(cols[:, ROWS : 2 * ROWS], width)
    start_wide = spread(cols[:, 2 * ROWS : 3 * ROWS], width)
    x_here = wide(buf, 0, blocks, tokens).astype(F32)
    dy_here = wide(buf, blocks * tokens, blocks, tokens).astype(F32)
    b_here, c_here = buf[0, b_row : b_row + tokens, :], buf[0, c_row : c_row + tokens, :]
    state = state0[0] + before[0, :1] * carried[...]
    grad = grad0[0] + after[0, :1] * carried[...]
    s_hi, s_lo = split2(state)
    g_hi, g_lo = split2(grad)
    b_grad = dot(cat([b_here, b_here], 1), cat([g_hi, g_lo], 0))
    c_state = dot(cat([c_here, c_here], 1), cat([s_hi, s_lo], 0))
    dxbar = dxbar_in[0] + end_wide * b_grad
    dx = (dt_wide * dxbar).astype(BF16)
    for block in range(blocks):
        out[0, block * tokens : (block + 1) * tokens, :] = dx[:, block * LANES : (block + 1) * LANES]
    u_hi, u_lo = split2(end_wide * (dt_wide * x_here))
    v_hi, v_lo = split2(start_wide * dy_here)
    db = db_in[0] + (dot_nt(u_hi, g_hi) + (dot_nt(u_hi, g_lo) + dot_nt(u_lo, g_hi)))
    dc = dc_in[0] + (dot_nt(v_hi, s_hi) + (dot_nt(v_hi, s_lo) + dot_nt(v_lo, s_hi)))
    out[0, blocks * tokens : (blocks + 1) * tokens, :] = db.astype(BF16)
    out[0, (blocks + 1) * tokens : (blocks + 2) * tokens, :] = dc.astype(BF16)
    both = grad * state
    corner = both[:ROWS]
    for i in range(1, STATE // ROWS):
        corner = corner + both[i * ROWS : (i + 1) * ROWS]
    parts = split3(cat([dxbar * x_here, dy_here * c_state, corner], 0))
    picker = spread_matrix(2, width)
    sums = dot_nt(picker, parts[0]) + (dot_nt(picker, parts[1]) + dot_nt(picker, parts[2]))
    along = sums[:ROWS, :tokens]
    later = from_start * sums[:ROWS, tokens : 2 * tokens]
    corner = jnp.sum(sums[:ROWS, 2 * tokens :], axis=1, keepdims=True)
    flow = dt * along - row_in[0] - later
    dlog = jnp.exp(end) * corner + jnp.sum(later, axis=1, keepdims=True) + cumulate(flow, True)
    ddt = along + rate * dlog
    out[0, (blocks + 2) * tokens : (blocks + 2) * tokens + DT_ROWS, :] = cat([ddt, jnp.zeros_like(ddt)], 0).astype(BF16)


def on_device(x_seq, dy_seq, dt_seq, a_log, b_seq, c_seq):
    tokens = x_seq.shape[0]
    count = lax.axis_size("head")
    heads = HEADS // count
    width = heads * HEAD_DIM
    blocks = width // LANES
    copies = count // GROUPS
    rows_in = (2 * blocks + 2) * tokens + DT_ROWS
    rows_out = (blocks + 2) * tokens + DT_ROWS

    def by_owner(value):
        return value.reshape(tokens, count, blocks, LANES).transpose(1, 2, 0, 3).reshape(count, blocks * tokens, LANES)

    def by_group(value):
        return jnp.repeat(value.transpose(1, 0, 2), copies, axis=0)

    dt_rows = jnp.pad(dt_seq.T.reshape(count, heads, tokens), ((0, 0), (0, DT_ROWS - heads), (0, 0)))
    sent = cat([by_owner(x_seq), by_owner(dy_seq), by_group(b_seq), by_group(c_seq), dt_rows], 1)
    buf = lax.all_to_all(sent, "head", split_axis=0, concat_axis=0, tiled=True)

    rates = -jnp.exp(lax.dynamic_slice_in_dim(a_log, lax.axis_index("head") * heads, heads))
    rate = jnp.broadcast_to(jnp.pad(rates, (0, ROWS - heads))[:, None], (ROWS, LANES))
    second = lax.axis_index("ctx").astype(F32)
    flags = jnp.stack([second, 1.0 - second])

    def whole(*shape):
        return pl.BlockSpec(shape, lambda k: (0,) * len(shape))

    def at(*shape):
        return pl.BlockSpec((1,) + shape, lambda k: (k, 0, 0))

    def back(*shape):
        return pl.BlockSpec((1,) + shape, lambda k: (count - 1 - k, 0, 0))

    def f32(*shape):
        return jax.ShapeDtypeStruct(shape, F32)

    params = pltpu.CompilerParams(vmem_limit_bytes=40 * 1024 * 1024)
    state0, grad0, before, after, send = pl.pallas_call(
        functools.partial(states_kernel, blocks, tokens, width),
        grid=(count,),
        in_specs=[pl.BlockSpec(memory_space=pltpu.SMEM), whole(ROWS, LANES), at(rows_in, LANES), back(rows_in, LANES)],
        out_specs=[at(STATE, width), back(STATE, width), at(ROWS, width), back(ROWS, width), whole(STATE, width)],
        out_shape=[f32(count, STATE, width), f32(count, STATE, width), f32(count, ROWS, width), f32(count, ROWS, width), f32(STATE, width)],
        scratch_shapes=[pltpu.VMEM((STATE, width), F32), pltpu.VMEM((STATE, width), F32), pltpu.VMEM((ROWS, width), F32), pltpu.VMEM((ROWS, width), F32)],
        compiler_params=params,
        name="states",
    )(flags, rate, buf, buf)
    carried = lax.ppermute(send, "ctx", [(0, 1), (1, 0)])
    dxbar, row_sums, db_in, dc_in = pl.pallas_call(
        functools.partial(inner_kernel, blocks, tokens, width),
        grid=(count,),
        in_specs=[whole(ROWS, LANES), at(rows_in, LANES)],
        out_specs=[at(tokens, width), at(ROWS, tokens), at(tokens, STATE), at(tokens, STATE)],
        out_shape=[f32(count, tokens, width), f32(count, ROWS, tokens), f32(count, tokens, STATE), f32(count, tokens, STATE)],
        compiler_params=params,
        cost_estimate=pl.CostEstimate(flops=2_000_000_000, bytes_accessed=6_000_000, transcendentals=1_000_000),
        name="inner",
    )(rate, buf)
    out = pl.pallas_call(
        functools.partial(outer_kernel, blocks, tokens, width),
        grid=(count,),
        in_specs=[
            whole(ROWS, LANES),
            at(rows_in, LANES),
            at(STATE, width),
            at(STATE, width),
            at(ROWS, width),
            at(ROWS, width),
            whole(STATE, width),
            at(tokens, width),
            at(ROWS, tokens),
            at(tokens, STATE),
            at(tokens, STATE),
        ],
        out_specs=at(rows_out, LANES),
        out_shape=jax.ShapeDtypeStruct((count, rows_out, LANES), BF16),
        compiler_params=params,
        name="outer",
    )(rate, buf, state0, grad0, before, after, carried, dxbar, row_sums, db_in, dc_in)

    home = lax.all_to_all(out, "head", split_axis=0, concat_axis=0, tiled=True)
    dx = home[:, : blocks * tokens].reshape(count, blocks, tokens, LANES).transpose(2, 0, 1, 3).reshape(tokens, HEADS * HEAD_DIM)

    def total(first):
        part = home[:, first : first + tokens]
        if copies > 1:
            part = part.astype(F32).reshape(GROUPS, copies, tokens, STATE).sum(1).astype(BF16)
        return part.transpose(1, 0, 2)

    db = total(blocks * tokens)
    dc = total((blocks + 1) * tokens)
    first = (blocks + 2) * tokens
    ddt = home[:, first : first + heads].reshape(HEADS, tokens).T
    return dx, ddt, db, dc


def solution(mesh):
    spec2 = P(("grp", "ctx", "head"), None)
    spec3 = P(("grp", "ctx", "head"), None, None)
    return jax.shard_map(
        on_device,
        mesh=mesh,
        in_specs=(spec2, spec2, spec2, P(), spec3, spec3),
        out_specs=(spec2, spec2, spec3, spec3),
        check_vma=False,
    )
```

```python
import functools
from typing import NamedTuple

import jax
import jax.numpy as jnp
from jax import lax
from jax.experimental import pallas as pl
from jax.experimental.pallas import tpu as pltpu
from jax.sharding import PartitionSpec as P

HEADS = 64
HEAD_DIM = 64
STATE = 128
GROUPS = 8
LANES = 128
ROWS = 8
TILE = 16
LOG2E = 1.4426950408889634
F32 = jnp.float32
BF16 = jnp.bfloat16
PIECES = 1


def split2(value):
    hi = value.astype(BF16)
    return hi, (value - hi.astype(F32)).astype(BF16)


def split3(value):
    hi = value.astype(BF16)
    rest = value - hi.astype(F32)
    mid = rest.astype(BF16)
    return hi, mid, (rest - mid.astype(F32)).astype(BF16)


def dot(a, b):
    return lax.dot_general(a, b, (((1,), (0,)), ((), ())), preferred_element_type=F32)


def dot_nt(a, b):
    return lax.dot_general(a, b, (((1,), (1,)), ((), ())), preferred_element_type=F32)


def dot_tn(a, b):
    return lax.dot_general(a, b, (((0,), (0,)), ((), ())), preferred_element_type=F32)


def cat(parts, axis):
    return jnp.concatenate(parts, axis=axis)


def upper(size, strict):
    row = lax.broadcasted_iota(jnp.int32, (size, size), 0)
    col = lax.broadcasted_iota(jnp.int32, (size, size), 1)
    return row < col if strict else row <= col


def cumulate(rows, strict):
    tri = upper(rows.shape[1], strict).astype(F32).astype(BF16)
    sums = dot(cat([part.astype(F32) for part in split3(rows)], 0).astype(BF16), tri)
    return sums[:ROWS] + sums[ROWS : 2 * ROWS] + sums[2 * ROWS :]


def spread_matrix(terms, width):
    row = lax.broadcasted_iota(jnp.int32, (terms * ROWS, width), 0)
    col = lax.broadcasted_iota(jnp.int32, (terms * ROWS, width), 1)
    return (row % ROWS == col // HEAD_DIM).astype(F32).astype(BF16)


def spread(cols, width):
    hi, lo = split2(cols)
    return dot(cat([hi.astype(F32), lo.astype(F32)], 1).astype(BF16), spread_matrix(2, width))


class Place(NamedTuple):
    tokens: int
    blocks: int
    piece: int
    last: bool
    shared: bool
    bc: int
    dt: int
    dt_rows: int

    @property
    def width(self):
        return self.blocks * LANES

    def x(self, buf):
        return [buf[i * self.tokens : (i + 1) * self.tokens, :] for i in range(self.blocks)]

    def dy(self, buf):
        return [buf[i * self.tokens : (i + 1) * self.tokens, :] for i in range(self.blocks, 2 * self.blocks)]

    def b(self, buf):
        return buf[self.bc : self.bc + self.tokens, :]

    def c(self, buf):
        return buf[self.bc + self.tokens : self.bc + 2 * self.tokens, :]

    def steps(self, buf, rate):
        dt = buf[self.dt : self.dt + self.dt_rows, :].astype(F32)[self.piece * ROWS : (self.piece + 1) * ROWS]
        return dt, cumulate(dt * rate, False)


def states_kernel(place, flag_ref, rate_ref, *refs):
    bufs, refs = (refs[:2] * 2, refs[2:]) if place.shared else (refs[:4], refs[4:])
    xy_s, xy_g, bc_s, bc_g = bufs
    s_ref, g_ref, before_ref, after_ref, send_ref, now, log = refs
    step, last = pl.program_id(0), pl.num_programs(0) - 1
    rate, width, tokens = rate_ref[...], place.width, place.tokens

    @pl.when(step == 0)
    def _():
        now[...] = jnp.zeros_like(now)
        log[...] = jnp.ones_like(log)

    for seg in range(2):
        xy, bc = xy_s.at[seg, 0], bc_s.at[seg, 0]
        dt, cum = place.steps(bc, rate)
        end = cum[:, tokens - 1 :]
        cols = jnp.transpose(cat([dt * jnp.exp(end - cum), jnp.broadcast_to(jnp.exp(end), dt.shape)], 0))
        scale = spread(cols[:, :ROWS], width)
        through = spread(cols[:ROWS, ROWS:], width)
        hi, lo = split2(scale * cat(place.x(xy), 1).astype(F32))
        b_here = place.b(bc)
        s_ref[seg, 0] = now[seg]
        before_ref[seg, 0] = log[seg]
        now[seg] = through[:1] * now[seg] + dot_tn(cat([b_here, b_here], 0), cat([hi, lo], 0))
        log[seg] = through * log[seg]

        xy, bc = xy_g.at[seg, 0], bc_g.at[seg, 0]
        dt, cum = place.steps(bc, rate)
        end = cum[:, tokens - 1 :]
        cols = jnp.transpose(cat([jnp.exp(cum), jnp.broadcast_to(jnp.exp(end), dt.shape)], 0))
        scale = spread(cols[:, :ROWS], width)
        through = spread(cols[:ROWS, ROWS:], width)
        hi, lo = split2(scale * cat(place.dy(xy), 1).astype(F32))
        c_here = place.c(bc)
        g_ref[seg, 0] = now[2 + seg]
        after_ref[seg, 0] = log[2 + seg]
        now[2 + seg] = through[:1] * now[2 + seg] + dot_tn(cat([c_here, c_here], 0), cat([hi, lo], 0))
        log[2 + seg] = through * log[2 + seg]

    @pl.when(step == last)
    def _():
        front = flag_ref[0] > 0.5
        send_ref[:STATE] = now[0]
        send_ref[STATE : 2 * STATE] = jnp.where(front, now[1], now[2])
        send_ref[2 * STATE : 3 * STATE] = now[3]
        send_ref[3 * STATE :] = jnp.where(front, log[1], log[0])


def inner_kernel(place, rate_ref, *refs):
    refs = refs[:1] + refs if place.shared else refs
    xy_ref, bc_ref, dxbar_ref, row_ref, db_ref, dc_ref = refs
    xy, bc, tokens, width = xy_ref.at[0, 0], bc_ref.at[0, 0], place.tokens, place.width
    dt, cum = place.steps(bc, rate_ref[...])
    cum = cum * LOG2E
    cols = jnp.transpose(cat([cum, dt], 0))
    dt_wide = spread(cols[:, ROWS:], width)
    b_here, c_here = place.b(bc), place.c(bc)
    k_two = dot_nt(b_here, c_here)
    mask = upper(tokens, False)
    left = lax.broadcasted_iota(jnp.int32, (tokens, LANES), 1) < HEAD_DIM
    none = jnp.zeros((tokens, LANES), F32)
    one_sum = jnp.zeros((tokens, tokens), F32)
    rows = []
    for block, (x_here, dy_here) in enumerate(zip(place.x(xy), place.dy(xy))):
        dy_f32 = dy_here.astype(F32)
        scaled = x_here.astype(F32) * dt_wide[:, block * LANES : (block + 1) * LANES]
        hi = scaled.astype(BF16).astype(F32)
        lo = scaled - hi
        pair = cat(
            [
                cat([jnp.where(left, hi, none), jnp.where(left, lo, none)], 1),
                cat([jnp.where(left, none, hi), jnp.where(left, none, lo)], 1),
            ],
            0,
        ).astype(BF16)
        k_one = dot_nt(pair, cat([dy_here, dy_here], 1))
        tops, bottoms = [], []
        for side in range(2):
            head = 2 * block + side
            gap = jnp.where(mask, cum[head : head + 1, :] - cols[:, head : head + 1], -1e30)
            decay = jnp.exp2(gap)
            a_one = decay * k_one[side * tokens : (side + 1) * tokens]
            a_two = decay * k_two
            one_sum = one_sum + a_one
            rows.append(jnp.sum(a_one * k_two, axis=0, keepdims=True))
            hi_two, lo_two = split2(a_two)
            tops.append(hi_two)
            bottoms.append(lo_two)
        sides = cat([jnp.where(left, dy_f32, none), jnp.where(left, none, dy_f32)], 0).astype(BF16)
        both = dot(cat([cat(tops, 1), cat(bottoms, 1)], 0), sides)
        dxbar_ref[0, 0, :, block * LANES : (block + 1) * LANES] = both[:tokens] + both[tokens:]
    if len(rows) < ROWS:
        rows.append(jnp.zeros((ROWS - len(rows), tokens), F32))
    row_ref[0, 0] = cat(rows, 0)
    db_ref[0, 0] = dot(cat(list(split2(one_sum)), 1), cat([c_here, c_here], 0))
    dc_ref[0, 0] = dot(cat(list(split2(jnp.transpose(one_sum))), 1), cat([b_here, b_here], 0))


def outer_kernel(place, flag_ref, rate_ref, *refs):
    refs = refs[:1] + refs if place.shared else refs
    xy_ref, bc_ref, state0, grad0, before, after, sent, got, dxbar_in, row_in, db_in, dc_in, *refs = refs
    if place.piece > 0:
        db_old, dc_old, *refs = refs
    out, *refs = refs
    if not place.last:
        db_new, dc_new, *refs = refs
    (carried,) = refs
    xy, bc, tokens, width = xy_ref.at[0, 0], bc_ref.at[0, 0], place.tokens, place.width
    seg = pl.program_id(0)

    @pl.when((seg == 0) & (pl.program_id(1) == 0))
    def _():
        front = flag_ref[0] > 0.5
        sent0, sent2 = sent[:STATE], sent[2 * STATE : 3 * STATE]
        got0, got1, got2 = got[:STATE], got[STATE : 2 * STATE], got[2 * STATE : 3 * STATE]
        mine, other = sent[3 * STATE : 3 * STATE + 1], got[3 * STATE : 3 * STATE + 1]
        far = got1 + other * (jnp.where(front, sent2, sent0) + mine * jnp.where(front, got2, got0))
        near = jnp.where(front, got0, got2) + other * jnp.where(front, sent0, sent2)
        none = jnp.zeros_like(far)
        carried[0] = jnp.where(front, none, got0)
        carried[1] = jnp.where(front, near, far)
        carried[2] = jnp.where(front, far, near)
        carried[3] = jnp.where(front, got2, none)

    rate = rate_ref[...]
    dt, cum = place.steps(bc, rate)
    end = cum[:, tokens - 1 :]
    to_end, from_start = jnp.exp(end - cum), jnp.exp(cum)
    cols = jnp.transpose(cat([dt, to_end, from_start], 0))
    dt_wide = spread(cols[:, :ROWS], width)
    end_wide = spread(cols[:, ROWS : 2 * ROWS], width)
    start_wide = spread(cols[:, 2 * ROWS : 3 * ROWS], width)
    x_here = cat(place.x(xy), 1).astype(F32)
    dy_here = cat(place.dy(xy), 1).astype(F32)
    b_here, c_here = place.b(bc), place.c(bc)
    state = state0[0, 0] + before[0, 0, :1] * carried[seg]
    grad = grad0[0, 0] + after[0, 0, :1] * carried[2 + seg]
    s_hi, s_lo = split2(state)
    g_hi, g_lo = split2(grad)
    b_grad = dot(cat([b_here, b_here], 1), cat([g_hi, g_lo], 0))
    c_state = dot(cat([c_here, c_here], 1), cat([s_hi, s_lo], 0))
    dxbar = dxbar_in[0, 0] + end_wide * b_grad
    dx = (dt_wide * dxbar).astype(BF16)
    for block in range(place.blocks):
        out[0, 0, block * tokens : (block + 1) * tokens, :] = dx[:, block * LANES : (block + 1) * LANES]
    u_hi, u_lo = split2(end_wide * (dt_wide * x_here))
    v_hi, v_lo = split2(start_wide * dy_here)
    db = db_in[0, 0] + (dot_nt(u_hi, g_hi) + (dot_nt(u_hi, g_lo) + dot_nt(u_lo, g_hi)))
    dc = dc_in[0, 0] + (dot_nt(v_hi, s_hi) + (dot_nt(v_hi, s_lo) + dot_nt(v_lo, s_hi)))
    if place.piece > 0:
        db, dc = db + db_old[0, 0], dc + dc_old[0, 0]
    first = place.blocks * tokens
    if place.last:
        out[0, 0, first : first + tokens, :] = db.astype(BF16)
        out[0, 0, first + tokens : first + 2 * tokens, :] = dc.astype(BF16)
        first = first + 2 * tokens
    else:
        db_new[0, 0], dc_new[0, 0] = db, dc
    both = grad * state
    corner = both[:ROWS]
    for i in range(1, STATE // ROWS):
        corner = corner + both[i * ROWS : (i + 1) * ROWS]
    parts = split3(cat([dxbar * x_here, dy_here * c_state, corner], 0))
    picker = spread_matrix(2, width)
    sums = dot_nt(picker, parts[0]) + (dot_nt(picker, parts[1]) + dot_nt(picker, parts[2]))
    along = sums[:ROWS, :tokens]
    later = from_start * sums[:ROWS, tokens : 2 * tokens]
    corner = jnp.sum(sums[:ROWS, 2 * tokens :], axis=1, keepdims=True)
    flow = dt * along - row_in[0, 0] - later
    dlog = jnp.exp(end) * corner + jnp.sum(later, axis=1, keepdims=True) + cumulate(flow, True)
    ddt = along + rate * dlog
    out[0, 0, first : first + TILE, :] = cat([ddt, jnp.zeros_like(ddt)], 0).astype(BF16)


def on_device(x_seq, dy_seq, dt_seq, a_log, b_seq, c_seq):
    tokens = x_seq.shape[0]
    half = lax.axis_size("lo")
    count = 2 * half
    heads = HEADS // count
    width = heads * HEAD_DIM
    copies = count // GROUPS
    pieces = PIECES if width % (PIECES * LANES) == 0 else 1
    blocks = width // LANES // pieces
    piece_heads = heads // pieces
    dt_rows = -(-pieces * ROWS // TILE) * TILE
    member = lax.axis_index(("ctx", "lo"))
    front = 1.0 - lax.axis_index("hi").astype(F32)
    flags = jnp.stack([front, 1.0 - front])

    def swap(value):
        return lax.all_to_all(value, ("ctx", "lo"), split_axis=0, concat_axis=0, tiled=True)

    def by_owner(value):
        parts = value.reshape(tokens, count, pieces, blocks, LANES).transpose(2, 1, 3, 0, 4)
        return parts.reshape(pieces, count, blocks * tokens, LANES)

    def by_group(value):
        return jnp.repeat(value.transpose(1, 0, 2), copies, axis=0)

    def padded(value, rows):
        return jnp.pad(value, ((0, 0),) * (value.ndim - 2) + ((0, rows - value.shape[-2]), (0, 0)))

    dt_sent = padded(dt_seq.T.reshape(count, pieces, piece_heads, tokens), ROWS).reshape(count, pieces * ROWS, tokens)
    x_sent, dy_sent = by_owner(x_seq), by_owner(dy_seq)
    rates = -jnp.exp(lax.dynamic_slice_in_dim(a_log, member * heads, heads)).reshape(pieces, piece_heads)
    rates = jnp.broadcast_to(jnp.pad(rates, ((0, 0), (0, ROWS - piece_heads)))[:, :, None], (pieces, ROWS, LANES))

    def f32(*shape):
        return jax.ShapeDtypeStruct((2, half) + shape, F32)

    smem = pl.BlockSpec(memory_space=pltpu.SMEM)
    params = pltpu.CompilerParams(vmem_limit_bytes=40 * 1024 * 1024)

    def whole(*shape):
        return pl.BlockSpec(shape, lambda *k: (0,) * len(shape))

    def at(*shape):
        return pl.BlockSpec((1, 1) + shape, lambda s, k: (s, k) + (0,) * len(shape))

    homes = []
    shared_buf = db_old = dc_old = None
    for piece in range(pieces):
        sent = [x_sent[piece], dy_sent[piece]]
        if piece == 0:
            sent += [by_group(b_seq), by_group(c_seq), padded(dt_sent, dt_rows)]
        buf = swap(cat(sent, 1)).reshape(2, half, -1, LANES)
        shared_buf = buf if piece == 0 else shared_buf
        place = Place(tokens, blocks, piece, piece == pieces - 1, piece == 0, 2 * blocks * tokens, (2 * blocks + 2) * tokens, dt_rows)
        bufs = [buf] if place.shared else [buf, shared_buf]
        rate, wide = rates[piece], place.width

        def both(*shape):
            return pl.BlockSpec((2, 1) + shape, lambda k: (0, k) + (0,) * len(shape))

        def back(*shape):
            return pl.BlockSpec((2, 1) + shape, lambda k: (0, half - 1 - k) + (0,) * len(shape))

        total = (3 * STATE + ROWS, wide)
        state0, grad0, before, after, send = pl.pallas_call(
            functools.partial(states_kernel, place),
            grid=(half,),
            in_specs=[smem, whole(ROWS, LANES)] + [spec(*b.shape[2:]) for b in bufs for spec in (both, back)],
            out_specs=[both(STATE, wide), back(STATE, wide), both(ROWS, wide), back(ROWS, wide), whole(*total)],
            out_shape=[f32(STATE, wide), f32(STATE, wide), f32(ROWS, wide), f32(ROWS, wide), jax.ShapeDtypeStruct(total, F32)],
            scratch_shapes=[pltpu.VMEM((4, STATE, wide), F32), pltpu.VMEM((4, ROWS, wide), F32)],
            compiler_params=params,
            name="states",
        )(flags, rate, *[b for b in bufs for _ in range(2)])
        got = lax.ppermute(send, "hi", [(0, 1), (1, 0)])
        buf_specs = [at(*b.shape[2:]) for b in bufs]
        dxbar, row_sums, db_in, dc_in = pl.pallas_call(
            functools.partial(inner_kernel, place),
            grid=(2, half),
            in_specs=[whole(ROWS, LANES)] + buf_specs,
            out_specs=[at(tokens, wide), at(ROWS, tokens), at(tokens, STATE), at(tokens, STATE)],
            out_shape=[f32(tokens, wide), f32(ROWS, tokens), f32(tokens, STATE), f32(tokens, STATE)],
            compiler_params=params,
            cost_estimate=pl.CostEstimate(flops=2_000_000_000, bytes_accessed=6_000_000, transcendentals=1_000_000),
            name="inner",
        )(rate, *bufs)
        rows_out = blocks * tokens + (2 * tokens if place.last else 0) + TILE
        old = [] if piece == 0 else [db_old, dc_old]
        new = [] if place.last else [f32(tokens, STATE)] * 2
        out, *olds = pl.pallas_call(
            functools.partial(outer_kernel, place),
            grid=(2, half),
            in_specs=[smem, whole(ROWS, LANES)]
            + buf_specs
            + [at(STATE, wide), at(STATE, wide), at(ROWS, wide), at(ROWS, wide), whole(*total), whole(*total)]
            + [at(tokens, wide), at(ROWS, tokens), at(tokens, STATE), at(tokens, STATE)]
            + [at(tokens, STATE) for _ in old],
            out_specs=[at(rows_out, LANES)] + [at(tokens, STATE) for _ in new],
            out_shape=[jax.ShapeDtypeStruct((2, half, rows_out, LANES), BF16)] + new,
            scratch_shapes=[pltpu.VMEM((4, STATE, wide), F32)],
            compiler_params=params,
            name="outer",
        )(flags, rate, *bufs, state0, grad0, before, after, send, got, dxbar, row_sums, db_in, dc_in, *old)
        if olds:
            db_old, dc_old = olds
        homes.append(swap(out.reshape(count, rows_out, LANES)))

    def columns(home):
        return home[:, : blocks * tokens].reshape(count, blocks, tokens, LANES)

    dx = cat([columns(home) for home in homes], 1).transpose(2, 0, 1, 3).reshape(tokens, HEADS * HEAD_DIM)
    steps = [home[:, -TILE:][:, :piece_heads] for home in homes]
    ddt = cat(steps, 1).reshape(HEADS, tokens).T

    def summed(first):
        part = homes[-1][:, first : first + tokens]
        if copies > 1:
            part = part.astype(F32).reshape(GROUPS, copies, tokens, STATE).sum(1).astype(BF16)
        return part.transpose(1, 0, 2)

    return dx, ddt, summed(blocks * tokens), summed((blocks + 1) * tokens)


def solution(mesh):
    parts, head, ctx = (mesh.shape[name] for name in ("grp", "head", "ctx"))
    split = jax.sharding.Mesh(mesh.devices.reshape(parts, 2, head // 2, ctx), ("grp", "hi", "lo", "ctx"))
    spec = P(("grp", "ctx", "hi", "lo"))
    return jax.shard_map(
        on_device,
        mesh=split,
        in_specs=(spec, spec, spec, P(), spec, spec),
        out_specs=(spec, spec, spec, spec),
        check_vma=False,
    )
```

```python
import functools
from typing import NamedTuple

import jax
import jax.numpy as jnp
from jax import lax
from jax.experimental import pallas as pl
from jax.experimental.pallas import tpu as pltpu
from jax.sharding import PartitionSpec as P

HEADS = 64
HEAD_DIM = 64
STATE = 128
GROUPS = 8
LANES = 128
ROWS = 8
TILE = 16
LOG2E = 1.4426950408889634
CODE_SPAN = 250.0
F32 = jnp.float32
BF16 = jnp.bfloat16


def split2(value):
    hi = value.astype(BF16)
    return hi, (value - hi.astype(F32)).astype(BF16)


def split3(value):
    hi = value.astype(BF16)
    rest = value - hi.astype(F32)
    mid = rest.astype(BF16)
    return hi, mid, (rest - mid.astype(F32)).astype(BF16)


def dot(a, b):
    return lax.dot_general(a, b, (((1,), (0,)), ((), ())), preferred_element_type=F32)


def dot_nt(a, b):
    return lax.dot_general(a, b, (((1,), (1,)), ((), ())), preferred_element_type=F32)


def dot_tn(a, b):
    return lax.dot_general(a, b, (((0,), (0,)), ((), ())), preferred_element_type=F32)


def cat(parts, axis):
    return jnp.concatenate(parts, axis=axis)


def upper(size, strict):
    row = lax.broadcasted_iota(jnp.int32, (size, size), 0)
    col = lax.broadcasted_iota(jnp.int32, (size, size), 1)
    return row < col if strict else row <= col


def cumulate(rows, strict):
    tri = upper(rows.shape[1], strict).astype(F32).astype(BF16)
    sums = dot(cat([part.astype(F32) for part in split3(rows)], 0).astype(BF16), tri)
    size = rows.shape[0]
    return sums[:size] + sums[size : 2 * size] + sums[2 * size :]


def spread_matrix(terms, width):
    row = lax.broadcasted_iota(jnp.int32, (terms * ROWS, width), 0)
    col = lax.broadcasted_iota(jnp.int32, (terms * ROWS, width), 1)
    return (row % ROWS == col // HEAD_DIM).astype(F32).astype(BF16)


def spread_rows(rows, width):
    return dot_tn(rows, spread_matrix(2, width))


def two_terms(rows):
    hi, lo = split2(rows)
    return cat([hi.astype(F32), lo.astype(F32)], 0).astype(BF16)


def spread(cols, width):
    hi, lo = split2(cols)
    return dot(cat([hi.astype(F32), lo.astype(F32)], 1).astype(BF16), spread_matrix(2, width))


class Place(NamedTuple):
    tokens: int
    blocks: int

    @property
    def width(self):
        return self.blocks * LANES

    @property
    def b_row(self):
        return 2 * self.blocks * self.tokens

    @property
    def dt_row(self):
        return self.b_row + 2 * self.tokens

    @property
    def rows_in(self):
        return self.dt_row + TILE

    @property
    def rows_out(self):
        return (self.blocks + 2) * self.tokens + TILE

    def x(self, buf):
        return [buf[i * self.tokens : (i + 1) * self.tokens, :] for i in range(self.blocks)]

    def dy(self, buf):
        return [buf[i * self.tokens : (i + 1) * self.tokens, :] for i in range(self.blocks, 2 * self.blocks)]

    def b(self, buf):
        return buf[self.b_row : self.b_row + self.tokens, :]

    def c(self, buf):
        return buf[self.b_row + self.tokens : self.b_row + 2 * self.tokens, :]

    def dt(self, buf):
        return buf[self.dt_row : self.dt_row + TILE, :].astype(F32)[:ROWS]

    def steps(self, buf, rate):
        dt = self.dt(buf)
        return dt, cumulate(dt * rate, False)


def pack_kernel(place, count, copies, x_hbm, dy_hbm, b_hbm, c_hbm, dt_hbm, out, x_ref, dy_ref, b_ref, c_ref, dt_ref, b_wide, c_wide, dt_wide, sems):
    tokens, blocks, width = place.tokens, place.blocks, place.width
    heads = HEADS // count
    parts = [(b_hbm, b_ref), (c_hbm, c_ref), (dt_hbm, dt_ref), (x_hbm, x_ref), (dy_hbm, dy_ref)]
    moves = [pltpu.make_async_copy(source, target, sems.at[i]) for i, (source, target) in enumerate(parts)]
    for move in moves:
        move.start()
    for move in moves[:3]:
        move.wait()
    b_wide[...] = b_ref[...].astype(F32).reshape(b_wide.shape)
    c_wide[...] = c_ref[...].astype(F32).reshape(c_wide.shape)
    dt_wide[...] = dt_ref[...].astype(F32)
    for dest in range(count):
        mine = pl.ds(dest // copies, tokens, stride=GROUPS)
        out[dest, place.b_row : place.b_row + tokens, :] = b_wide[mine, :].astype(BF16)
        out[dest, place.b_row + tokens : place.dt_row, :] = c_wide[mine, :].astype(BF16)
        dt = dt_wide[dest * heads : (dest + 1) * heads, :]
        out[dest, place.dt_row :, :] = cat([dt, jnp.zeros((TILE - heads, tokens), F32)], 0).astype(BF16)
    for move, ref, first in ((moves[3], x_ref, 0), (moves[4], dy_ref, blocks * tokens)):
        move.wait()
        for dest in range(count):
            for i in range(blocks):
                at = dest * width + i * LANES
                out[dest, first + i * tokens : first + (i + 1) * tokens, :] = ref[:, at : at + LANES]


def unpack_kernel(place, count, copies, home, dx_hbm, ddt_hbm, db_hbm, dc_hbm, dx_ref, db_ref, dc_ref, ddt_ref, db_wide, dc_wide, ddt_wide, sems):
    tokens, blocks, width = place.tokens, place.blocks, place.width
    heads = HEADS // count
    moves = []
    step = max(count // 4, 1)
    for source in range(count):
        for i in range(blocks):
            at = source * width + i * LANES
            dx_ref[:, at : at + LANES] = home[source, i * tokens : (i + 1) * tokens, :]
        if (source + 1) % step == 0:
            columns = slice((source + 1 - step) * width, (source + 1) * width)
            moves.append(pltpu.make_async_copy(dx_ref.at[:, columns], dx_hbm.at[:, columns], sems.at[len(moves)]))
            moves[-1].start()
    first = blocks * tokens
    for to, at in ((db_wide, first), (dc_wide, first + tokens)):
        for group in range(GROUPS):
            part = home[group * copies, at : at + tokens, :].astype(F32)
            for copy in range(1, copies):
                part = part + home[group * copies + copy, at : at + tokens, :].astype(F32)
            to[pl.ds(group, tokens, stride=GROUPS), :] = part
    for source in range(count):
        ddt_wide[source * heads : (source + 1) * heads, :] = home[source, first + 2 * tokens :, :].astype(F32)[:heads]
    db_ref[...] = db_wide[...].reshape(db_ref.shape).astype(BF16)
    dc_ref[...] = dc_wide[...].reshape(dc_ref.shape).astype(BF16)
    ddt_ref[...] = ddt_wide[...].astype(BF16)
    for source, target in ((db_ref, db_hbm), (dc_ref, dc_hbm), (ddt_ref, ddt_hbm)):
        moves.append(pltpu.make_async_copy(source, target, sems.at[len(moves)]))
        moves[-1].start()
    for move in moves:
        move.wait()


def segment_decays(place, bufs, rate):
    dts = [place.dt(buf) for buf in bufs]
    cums = cumulate(cat([dt * rate for dt in dts], 0), False)
    cums = [cums[i * ROWS : (i + 1) * ROWS] for i in range(len(bufs))]
    starts, start = [], jnp.zeros((ROWS, 1), F32)
    for cum in cums:
        starts.append(start + cum)
        start = start + cum[:, place.tokens - 1 :]
    return dts, [start - one for one in starts], starts, start


def encode(value, scale):
    size = jnp.exp2(jnp.abs(value) * (CODE_SPAN / scale) - CODE_SPAN / 2)
    return jnp.where(value < 0.0, -size, size).astype(BF16)


def decode(code, scale):
    code = code.astype(F32)
    size = (jnp.log(jnp.abs(code)) * LOG2E + CODE_SPAN / 2) * (scale / CODE_SPAN)
    return jnp.where(code < 0.0, -size, size)


def totals_kernel(place, flag_ref, rate_ref, buf, u_ref, v_ref, own_ref, send_ref, now, log):
    seg, width = pl.program_id(0), place.width
    chunks = [buf.at[0, i] for i in range(buf.shape[1])]
    dts, ends, starts, total = segment_decays(place, chunks, rate_ref[...])
    x_hi, x_lo, dy_hi, dy_lo, b_all, c_all = [], [], [], [], [], []
    for i, chunk in enumerate(chunks):
        to_end, from_start = two_terms(dts[i] * jnp.exp(ends[i])), two_terms(jnp.exp(starts[i]))
        u_ref[0, i], v_ref[0, i] = to_end, from_start
        hi, lo = split2(spread_rows(to_end, width) * cat(place.x(chunk), 1).astype(F32))
        x_hi.append(hi)
        x_lo.append(lo)
        hi, lo = split2(spread_rows(from_start, width) * cat(place.dy(chunk), 1).astype(F32))
        dy_hi.append(hi)
        dy_lo.append(lo)
        b_all.append(place.b(chunk))
        c_all.append(place.c(chunk))
    b_turned = jnp.transpose(cat(b_all, 0).astype(F32)).astype(BF16)
    c_turned = jnp.transpose(cat(c_all, 0).astype(F32)).astype(BF16)
    now[seg] = dot(b_turned, cat(x_hi, 0)) + dot(b_turned, cat(x_lo, 0))
    now[2 + seg] = dot(c_turned, cat(dy_hi, 0)) + dot(c_turned, cat(dy_lo, 0))
    log[seg] = spread_rows(two_terms(jnp.broadcast_to(jnp.exp(total), (ROWS, LANES))), width)[:ROWS]

    @pl.when(seg == 1)
    def _():
        front = flag_ref[0] > 0.5
        values = [now[0], jnp.where(front, now[1], now[2]), now[3]]
        tops = [jnp.maximum(jnp.max(jnp.abs(value), axis=0, keepdims=True), 1e-30) for value in values]
        scales = [(top * 1.01).astype(BF16).astype(F32) for top in tops]
        for i, (value, scale) in enumerate(zip(values, scales)):
            send_ref[i * STATE : (i + 1) * STATE] = encode(value, scale)
        logs = [part.astype(F32) for i in range(2) for part in split2(log[i, :1])]
        notes = cat(scales + logs + [jnp.zeros((TILE - 7, width), F32)], 0)
        send_ref[3 * STATE :] = notes.astype(BF16)
        own_ref[:STATE] = values[0]
        own_ref[STATE : 2 * STATE] = values[2]
        own_ref[2 * STATE :] = cat([log[0], log[1]], 0)


def head_sums(values, width):
    hi, lo = split2(values)
    picker = spread_matrix(2, width)
    return (dot_nt(picker, hi) + dot_nt(picker, lo))[:ROWS]


def fold(value):
    total = value[:ROWS]
    for i in range(1, value.shape[0] // ROWS):
        total = total + value[i * ROWS : (i + 1) * ROWS]
    return total


def middle_kernel(place, rate_ref, buf, dx_ref, ddt_ref, db_ref, dc_ref):
    tokens, width, blocks = place.tokens, place.width, place.blocks
    rate = rate_ref[...]
    chunks = [buf.at[0, i] for i in range(buf.shape[1])]
    dts = [place.dt(chunk) for chunk in chunks]
    cums = cumulate(cat([dt * rate for dt in dts], 0), False)
    cums = [cums[i * ROWS : (i + 1) * ROWS] for i in range(len(chunks))]
    ends = [cum[:, tokens - 1 :] for cum in cums]
    starts = [jnp.exp(cum) for cum in cums]

    scaled, us, vs, end_wides, dt_wides, adds_s, adds_g, through = [], [], [], [], [], [], [], []
    for i, chunk in enumerate(chunks):
        dt_wide = spread_rows(two_terms(dts[i]), width)
        end_wide = spread_rows(two_terms(jnp.exp(ends[i] - cums[i])), width)
        start_wide = spread_rows(two_terms(starts[i]), width)
        xbar = dt_wide * cat(place.x(chunk), 1).astype(F32)
        u, v = split2(end_wide * xbar), split2(start_wide * cat(place.dy(chunk), 1).astype(F32))
        b_here, c_here = place.b(chunk), place.c(chunk)
        adds_s.append(dot_tn(cat([b_here, b_here], 0), cat(list(u), 0)))
        adds_g.append(dot_tn(cat([c_here, c_here], 0), cat(list(v), 0)))
        through.append(start_wide[tokens - 1 :, :])
        scaled.append(xbar)
        us.append(u)
        vs.append(v)
        end_wides.append(end_wide)
        dt_wides.append(dt_wide)
    states, grads = [jnp.zeros((STATE, width), F32)], [jnp.zeros((STATE, width), F32)]
    for i in range(len(chunks) - 1):
        states.append(through[i] * states[-1] + adds_s[i])
        grads.append(through[-1 - i] * grads[-1] + adds_g[-1 - i])
    grads = grads[::-1]
    corners = head_sums(cat([fold(through[i] * (states[i] * grads[i])) for i in range(len(chunks))], 0), width)

    mask = upper(tokens, False)
    left = lax.broadcasted_iota(jnp.int32, (tokens, LANES), 1) < HEAD_DIM
    none = jnp.zeros((tokens, LANES), F32)
    for i, chunk in enumerate(chunks):
        b_here, c_here = place.b(chunk), place.c(chunk)
        cum = cums[i] * LOG2E
        cols = jnp.transpose(cum)
        k_two = dot_nt(b_here, c_here)
        s_hi, s_lo = split2(states[i])
        g_hi, g_lo = split2(grads[i])
        b_grad = end_wides[i] * dot(cat([b_here, b_here], 1), cat([g_hi, g_lo], 0))
        c_state = dot(cat([c_here, c_here], 1), cat([s_hi, s_lo], 0))
        one_sum = jnp.zeros((tokens, tokens), F32)
        rows, alongs = [], []
        for block, (x_here, dy_here) in enumerate(zip(place.x(chunk), place.dy(chunk))):
            lanes = slice(block * LANES, (block + 1) * LANES)
            dy_f32 = dy_here.astype(F32)
            hi = scaled[i][:, lanes].astype(BF16).astype(F32)
            lo = scaled[i][:, lanes] - hi
            pair = cat(
                [
                    cat([jnp.where(left, hi, none), jnp.where(left, lo, none)], 1),
                    cat([jnp.where(left, none, hi), jnp.where(left, none, lo)], 1),
                ],
                0,
            ).astype(BF16)
            k_one = dot_nt(pair, cat([dy_here, dy_here], 1))
            tops, bottoms = [], []
            for side in range(2):
                head = 2 * block + side
                gap = jnp.where(mask, cum[head : head + 1, :] - cols[:, head : head + 1], -1e30)
                decay = jnp.exp2(gap)
                a_one = decay * k_one[side * tokens : (side + 1) * tokens]
                a_two = decay * k_two
                one_sum = one_sum + a_one
                rows.append(jnp.sum(a_one * k_two, axis=0, keepdims=True))
                hi_two, lo_two = split2(a_two)
                tops.append(hi_two)
                bottoms.append(lo_two)
            sides = cat([jnp.where(left, dy_f32, none), jnp.where(left, none, dy_f32)], 0).astype(BF16)
            both = dot(cat([cat(tops, 1), cat(bottoms, 1)], 0), sides)
            dxbar = both[:tokens] + both[tokens:] + b_grad[:, lanes]
            dx_ref[0, i, :, lanes] = dt_wides[i][:, lanes] * dxbar
            alongs.append(dxbar * x_here.astype(F32))
        if len(rows) < ROWS:
            rows.append(jnp.zeros((ROWS - len(rows), tokens), F32))
        (u_hi, u_lo), (v_hi, v_lo) = us[i], vs[i]
        db = dot(cat(list(split2(one_sum)), 1), cat([c_here, c_here], 0))
        dc = dot(cat(list(split2(jnp.transpose(one_sum))), 1), cat([b_here, b_here], 0))
        db_ref[0, i] = db + (dot_nt(u_hi, g_hi) + (dot_nt(u_hi, g_lo) + dot_nt(u_lo, g_hi)))
        dc_ref[0, i] = dc + (dot_nt(v_hi, s_hi) + (dot_nt(v_hi, s_lo) + dot_nt(v_lo, s_hi)))
        sums = head_sums(cat([cat(alongs, 1), cat(place.dy(chunk), 1).astype(F32) * c_state], 0), width)
        along = sums[:, :tokens]
        later = starts[i] * sums[:, tokens:]
        corner = jnp.sum(corners[:, i * ROWS : (i + 1) * ROWS], axis=1, keepdims=True)
        flow = dts[i] * along - cat(rows, 0) - later
        dlog = corner + jnp.sum(later, axis=1, keepdims=True) + cumulate(flow, True)
        ddt_ref[0, i] = along + rate * dlog


def finish_kernel(place, flag_ref, rate_ref, buf, u_ref, v_ref, own, got, dx_in, ddt_in, db_in, dc_in, out):
    seg, tokens, width = pl.program_id(0), place.tokens, place.width
    front, first = flag_ref[0], flag_ref[0] * (1 - seg) > 0.5
    final = (1.0 - flag_ref[0]) * seg > 0.5
    front = front > 0.5
    notes = got[3 * STATE :].astype(F32)
    sent0, sent2, logs = own[:STATE], own[STATE : 2 * STATE], (own[2 * STATE : 2 * STATE + 1], own[2 * STATE + ROWS : 2 * STATE + ROWS + 1])
    got0, got1, got2 = (decode(got[i * STATE : (i + 1) * STATE], notes[i : i + 1]) for i in range(3))
    mine = jnp.where(front, logs[1], logs[0])
    other = jnp.where(front, notes[3:4] + notes[4:5], notes[5:6] + notes[6:7])
    through = jnp.where(seg == 0, logs[0], logs[1])
    far = got1 + other * (jnp.where(front, sent2, sent0) + mine * jnp.where(front, got2, got0))
    near = jnp.where(front, got0, got2) + other * jnp.where(front, sent0, sent2)
    none = jnp.zeros_like(far)
    state = jnp.where(first, none, jnp.where(front, near, jnp.where(seg == 0, got0, far)))
    grad = jnp.where(final, none, jnp.where(front, jnp.where(seg == 0, far, got2), near))
    s_hi, s_lo = split2(state)
    g_hi, g_lo = split2(grad)
    s_both, g_both = cat([s_hi, s_lo], 0), cat([g_hi, g_lo], 0)
    corner = jnp.sum(head_sums(fold(through * (grad * state)), width), axis=1, keepdims=True)
    chunks = [buf.at[0, i] for i in range(buf.shape[1])]
    before, after = jnp.zeros((ROWS, 1), F32), jnp.zeros((ROWS, 1), F32)
    ins, laters, dts = [], [], []
    first_row = place.blocks * tokens
    for i, chunk in enumerate(chunks):
        u_wide, v_wide = spread_rows(u_ref[0, i], width), spread_rows(v_ref[0, i], width)
        b_here, c_here = place.b(chunk), place.c(chunk)
        b_grad = dot(cat([b_here, b_here], 1), g_both)
        c_state = dot(cat([c_here, c_here], 1), s_both)
        dx = (dx_in[0, i] + u_wide * b_grad).astype(BF16)
        for block in range(place.blocks):
            out[0, i, block * tokens : (block + 1) * tokens, :] = dx[:, block * LANES : (block + 1) * LANES]
        u = u_wide * cat(place.x(chunk), 1).astype(F32)
        v = v_wide * cat(place.dy(chunk), 1).astype(F32)
        u_hi, u_lo = split2(u)
        v_hi, v_lo = split2(v)
        db = db_in[0, i] + (dot_nt(u_hi, g_hi) + (dot_nt(u_hi, g_lo) + dot_nt(u_lo, g_hi)))
        dc = dc_in[0, i] + (dot_nt(v_hi, s_hi) + (dot_nt(v_hi, s_lo) + dot_nt(v_lo, s_hi)))
        out[0, i, first_row : first_row + tokens, :] = db.astype(BF16)
        out[0, i, first_row + tokens : first_row + 2 * tokens, :] = dc.astype(BF16)
        ins.append(head_sums(u * b_grad, width))
        laters.append(head_sums(v * c_state, width))
        dts.append(place.dt(chunk))
    into = cumulate(cat(ins, 0), True)
    over = cumulate(cat(laters, 0), True)
    tails = [jnp.sum(later, axis=1, keepdims=True) for later in laters]
    for i in range(len(chunks)):
        rows = slice(i * ROWS, (i + 1) * ROWS)
        rest = corner + before
        for tail in tails[i:]:
            rest = rest + tail
        dlog = rest + (into[rows] - over[rows])
        before = before + jnp.sum(ins[i], axis=1, keepdims=True)
        safe = jnp.where(dts[i] > 0.0, dts[i], 1.0)
        ddt = ddt_in[0, i] + ins[i] / safe + rate_ref[...] * dlog
        out[0, i, first_row + 2 * tokens :, :] = cat([ddt, jnp.zeros_like(ddt)], 0).astype(BF16)


def on_device(x_seq, dy_seq, dt_seq, a_log, b_seq, c_seq):
    tokens = x_seq.shape[0]
    half = lax.axis_size("lo")
    count = 2 * half
    heads = HEADS // count
    width = heads * HEAD_DIM
    copies = count // GROUPS
    place = Place(tokens, width // LANES)
    front = 1.0 - lax.axis_index("hi").astype(F32)
    flags = jnp.stack([front, 1.0 - front])

    def swap(value):
        return lax.all_to_all(value, ("ctx", "lo"), split_axis=0, concat_axis=0, tiled=True)

    rates = -jnp.exp(lax.dynamic_slice_in_dim(a_log, lax.axis_index(("ctx", "lo")) * heads, heads))
    rate = jnp.broadcast_to(jnp.pad(rates, (0, ROWS - heads))[:, None], (ROWS, LANES))

    def f32(*shape):
        return jax.ShapeDtypeStruct((2, half) + shape, F32)

    def bf16(*shape):
        return jax.ShapeDtypeStruct(shape, BF16)

    smem = pl.BlockSpec(memory_space=pltpu.SMEM)
    params = pltpu.CompilerParams(vmem_limit_bytes=40 * 1024 * 1024)

    def whole(*shape):
        return pl.BlockSpec(shape, lambda *k: (0,) * len(shape))

    def segment(*shape):
        return pl.BlockSpec((1, half) + shape, lambda s: (s, 0) + (0,) * len(shape))

    hbm, vmem = pl.BlockSpec(memory_space=pl.ANY), pl.BlockSpec(memory_space=pltpu.VMEM)
    seqs = (x_seq, dy_seq, b_seq, c_seq)
    wides = [pltpu.VMEM((tokens * GROUPS, STATE), F32), pltpu.VMEM((tokens * GROUPS, STATE), F32), pltpu.VMEM((HEADS, tokens), F32)]
    sent = pl.pallas_call(
        functools.partial(pack_kernel, place, count, copies),
        in_specs=[hbm] * 5,
        out_specs=vmem,
        out_shape=bf16(count, place.rows_in, LANES),
        scratch_shapes=[pltpu.VMEM(seq.shape, BF16) for seq in seqs]
        + [pltpu.VMEM((HEADS, tokens), BF16)]
        + wides
        + [pltpu.SemaphoreType.DMA((5,))],
        compiler_params=pltpu.CompilerParams(vmem_limit_bytes=58 * 1024 * 1024),
        name="pack",
    )(x_seq, dy_seq, b_seq, c_seq, dt_seq.T)
    buf = swap(sent).reshape(2, half, place.rows_in, LANES)

    owned, coded = (2 * STATE + 2 * ROWS, width), (3 * STATE + TILE, width)
    u_rows, v_rows, own, send = pl.pallas_call(
        functools.partial(totals_kernel, place),
        grid=(2,),
        in_specs=[smem, whole(ROWS, LANES), segment(place.rows_in, LANES)],
        out_specs=[segment(TILE, tokens), segment(TILE, tokens), whole(*owned), whole(*coded)],
        out_shape=[bf16(2, half, TILE, tokens), bf16(2, half, TILE, tokens), jax.ShapeDtypeStruct(owned, F32), bf16(*coded)],
        scratch_shapes=[pltpu.VMEM((4, STATE, width), F32), pltpu.VMEM((2, ROWS, width), F32)],
        compiler_params=params,
        name="totals",
    )(flags, rate, buf)
    got = lax.ppermute(send, "hi", [(0, 1), (1, 0)])

    within = [f32(tokens, width), f32(ROWS, tokens), f32(tokens, STATE), f32(tokens, STATE)]
    within_specs = [segment(tokens, width), segment(ROWS, tokens), segment(tokens, STATE), segment(tokens, STATE)]
    parts = pl.pallas_call(
        functools.partial(middle_kernel, place),
        grid=(2,),
        in_specs=[whole(ROWS, LANES), segment(place.rows_in, LANES)],
        out_specs=within_specs,
        out_shape=within,
        compiler_params=params,
        cost_estimate=pl.CostEstimate(flops=6_000_000_000, bytes_accessed=20_000_000, transcendentals=2_000_000),
        name="middle",
    )(rate, buf)
    out = pl.pallas_call(
        functools.partial(finish_kernel, place),
        grid=(2,),
        in_specs=[smem, whole(ROWS, LANES), segment(place.rows_in, LANES), segment(TILE, tokens), segment(TILE, tokens)]
        + [whole(*owned), whole(*coded)]
        + within_specs,
        out_specs=segment(place.rows_out, LANES),
        out_shape=bf16(2, half, place.rows_out, LANES),
        compiler_params=params,
        name="finish",
    )(flags, rate, buf, u_rows, v_rows, own, got, *parts)

    home = swap(out.reshape(count, place.rows_out, LANES))
    dx, ddt, db, dc = pl.pallas_call(
        functools.partial(unpack_kernel, place, count, copies),
        in_specs=[vmem],
        out_specs=[hbm] * 4,
        out_shape=[bf16(*x_seq.shape), bf16(HEADS, tokens), bf16(*b_seq.shape), bf16(*c_seq.shape)],
        scratch_shapes=[pltpu.VMEM(x_seq.shape, BF16), pltpu.VMEM(b_seq.shape, BF16), pltpu.VMEM(c_seq.shape, BF16), pltpu.VMEM((HEADS, tokens), BF16)]
        + wides
        + [pltpu.SemaphoreType.DMA((7,))],
        compiler_params=params,
        name="unpack",
    )(home)
    return dx, ddt.T, db, dc


def solution(mesh):
    parts, head, ctx = (mesh.shape[name] for name in ("grp", "head", "ctx"))
    split = jax.sharding.Mesh(mesh.devices.reshape(parts, 2, head // 2, ctx), ("grp", "hi", "lo", "ctx"))
    spec = P(("grp", "ctx", "hi", "lo"))
    return jax.shard_map(
        on_device,
        mesh=split,
        in_specs=(spec, spec, spec, P(), spec, spec),
        out_specs=(spec, spec, spec, spec),
        check_vma=False,
    )
```

```python
import functools
from typing import NamedTuple

import jax
import jax.numpy as jnp
from jax import lax
from jax.experimental import pallas as pl
from jax.experimental.pallas import tpu as pltpu
from jax.sharding import PartitionSpec as P

HEADS = 64
HEAD_DIM = 64
STATE = 128
GROUPS = 8
LANES = 128
ROWS = 8
TILE = 16
LOG2E = 1.4426950408889634
CODE_SPAN = 250.0
PIECES = 1
F32 = jnp.float32
BF16 = jnp.bfloat16


def split2(value):
    hi = value.astype(BF16)
    return hi, (value - hi.astype(F32)).astype(BF16)


def split3(value):
    hi = value.astype(BF16)
    rest = value - hi.astype(F32)
    mid = rest.astype(BF16)
    return hi, mid, (rest - mid.astype(F32)).astype(BF16)


def dot(a, b):
    return lax.dot_general(a, b, (((1,), (0,)), ((), ())), preferred_element_type=F32)


def dot_nt(a, b):
    return lax.dot_general(a, b, (((1,), (1,)), ((), ())), preferred_element_type=F32)


def dot_tn(a, b):
    return lax.dot_general(a, b, (((0,), (0,)), ((), ())), preferred_element_type=F32)


def cat(parts, axis):
    return jnp.concatenate(parts, axis=axis)


def upper(size, strict):
    row = lax.broadcasted_iota(jnp.int32, (size, size), 0)
    col = lax.broadcasted_iota(jnp.int32, (size, size), 1)
    return row < col if strict else row <= col


def cumulate(rows, strict):
    tri = upper(rows.shape[1], strict).astype(F32).astype(BF16)
    sums = dot(cat([part.astype(F32) for part in split3(rows)], 0).astype(BF16), tri)
    size = rows.shape[0]
    return sums[:size] + sums[size : 2 * size] + sums[2 * size :]


def spread_matrix(terms, width):
    row = lax.broadcasted_iota(jnp.int32, (terms * ROWS, width), 0)
    col = lax.broadcasted_iota(jnp.int32, (terms * ROWS, width), 1)
    return (row % ROWS == col // HEAD_DIM).astype(F32).astype(BF16)


def spread_rows(rows, width):
    hi, lo = split2(rows)
    terms = cat([hi.astype(F32), lo.astype(F32)], 0).astype(BF16)
    return dot_tn(terms, spread_matrix(2, width))


def columns(rows):
    return jnp.transpose(cat([rows, jnp.zeros((LANES - rows.shape[0], rows.shape[1]), F32)], 0))


def widen(cols, first, width):
    lane = lax.broadcasted_iota(jnp.int32, cols.shape, 1)
    heads = [first + lane // HEAD_DIM + 2 * block for block in range(width // LANES)]
    return cat([jnp.take_along_axis(cols, head, axis=1) for head in heads], 1)


def head_products(values, factors):
    rows = values[0].shape[0]
    both = dot_nt(cat(list(values), 0), cat(list(factors), 0))
    size = factors[0].shape[0]
    return (both[:rows, :size] + (both[:rows, size:] + both[rows:, :size])) + both[rows:, size:]


class Place(NamedTuple):
    tokens: int
    half: int
    blocks: int
    pieces: int
    piece: int

    @property
    def width(self):
        return self.blocks * LANES

    @property
    def last(self):
        return self.piece == self.pieces - 1

    @property
    def b_row(self):
        return 2 * self.blocks * self.tokens

    @property
    def dt_row(self):
        return self.b_row + 2 * self.tokens

    @property
    def dt_rows(self):
        return -(-self.pieces * ROWS // TILE) * TILE

    @property
    def rows_in(self):
        return self.dt_row + self.dt_rows if self.piece == 0 else self.b_row

    @property
    def rows_out(self):
        return (self.blocks + (2 if self.last else 0)) * self.tokens + TILE

    def x(self, buf):
        return [buf[i * self.tokens : (i + 1) * self.tokens, :] for i in range(self.blocks)]

    def dy(self, buf):
        return [buf[i * self.tokens : (i + 1) * self.tokens, :] for i in range(self.blocks, 2 * self.blocks)]

    def b(self, buf):
        return buf[self.b_row : self.b_row + self.tokens, :]

    def c(self, buf):
        return buf[self.b_row + self.tokens : self.b_row + 2 * self.tokens, :]

    def dt(self, buf):
        return buf[self.dt_row : self.dt_row + self.dt_rows, :].astype(F32)[self.piece * ROWS : (self.piece + 1) * ROWS]

    def bufs(self, refs):
        return (refs[0], refs[0], refs[1:]) if self.piece == 0 else (refs[0], refs[1], refs[2:])


def pack_kernel(place, count, copies, *refs):
    hbm, (out, *refs) = refs[:5], refs[5:]
    b_ref, c_ref, dt_ref, x_ref, dy_ref, b_wide, c_wide, dt_wide, sems = refs
    tokens, blocks, width = place.tokens, place.blocks, place.width
    heads = HEADS // count // place.pieces
    moves = [pltpu.make_async_copy(source, target, sems.at[i]) for i, (source, target) in enumerate(zip(hbm, refs))]
    for move in moves:
        move.start()
    for move in moves[:3]:
        move.wait()
    b_wide[...] = b_ref[...].astype(F32).reshape(b_wide.shape)
    c_wide[...] = c_ref[...].astype(F32).reshape(c_wide.shape)
    dt_wide[...] = dt_ref[...].astype(F32)
    for dest in range(count):
        mine = pl.ds(dest // copies, tokens, stride=GROUPS)
        out[dest, place.b_row : place.b_row + tokens, :] = b_wide[mine, :].astype(BF16)
        out[dest, place.b_row + tokens : place.dt_row, :] = c_wide[mine, :].astype(BF16)
        rows = []
        for piece in range(place.pieces):
            at = (dest * place.pieces + piece) * heads
            rows += [dt_wide[at : at + heads, :]] + [jnp.zeros((ROWS - heads, tokens), F32)] * (heads < ROWS)
        rows += [jnp.zeros((place.dt_rows - place.pieces * ROWS, tokens), F32)] * (place.dt_rows > place.pieces * ROWS)
        out[dest, place.dt_row :, :] = cat(rows, 0).astype(BF16)
    for move, ref, first in ((moves[3], x_ref, 0), (moves[4], dy_ref, blocks * tokens)):
        move.wait()
        for dest in range(count):
            for i in range(blocks):
                at = dest * place.pieces * width + i * LANES
                out[dest, first + i * tokens : first + (i + 1) * tokens, :] = ref[:, at : at + LANES]


def pack_more_kernel(place, count, x_hbm, dy_hbm, out, x_ref, dy_ref, sems):
    tokens, blocks, width = place.tokens, place.blocks, place.width
    moves = [pltpu.make_async_copy(x_hbm, x_ref, sems.at[0]), pltpu.make_async_copy(dy_hbm, dy_ref, sems.at[1])]
    for move in moves:
        move.start()
    for move, ref, first in ((moves[0], x_ref, 0), (moves[1], dy_ref, blocks * tokens)):
        move.wait()
        for dest in range(count):
            for i in range(blocks):
                at = (dest * place.pieces + place.piece) * width + i * LANES
                out[dest, first + i * tokens : first + (i + 1) * tokens, :] = ref[:, at : at + LANES]


def unpack_kernel(places, count, copies, *refs):
    pieces, last = len(places), places[-1]
    homes, (dx_hbm, ddt_hbm, db_hbm, dc_hbm, dx_ref, db_ref, dc_ref, ddt_ref, db_wide, dc_wide, ddt_wide, sems) = refs[:pieces], refs[pieces:]
    tokens, blocks, width = last.tokens, last.blocks, last.width
    heads = HEADS // count // pieces
    moves = []
    step = max(count // 4, 1)
    for source in range(count):
        for piece, home in enumerate(homes):
            for i in range(blocks):
                at = (source * pieces + piece) * width + i * LANES
                dx_ref[:, at : at + LANES] = home[source, i * tokens : (i + 1) * tokens, :]
        if (source + 1) % step == 0:
            columns = slice((source + 1 - step) * pieces * width, (source + 1) * pieces * width)
            moves.append(pltpu.make_async_copy(dx_ref.at[:, columns], dx_hbm.at[:, columns], sems.at[len(moves)]))
            moves[-1].start()
    first = blocks * tokens
    for to, at in ((db_wide, first), (dc_wide, first + tokens)):
        for group in range(GROUPS):
            part = homes[-1][group * copies, at : at + tokens, :].astype(F32)
            for copy in range(1, copies):
                part = part + homes[-1][group * copies + copy, at : at + tokens, :].astype(F32)
            to[pl.ds(group, tokens, stride=GROUPS), :] = part
    for source in range(count):
        for place, home in zip(places, homes):
            at = (source * pieces + place.piece) * heads
            ddt_wide[at : at + heads, :] = home[source, place.rows_out - TILE :, :].astype(F32)[:heads]
    db_ref[...] = db_wide[...].reshape(db_ref.shape).astype(BF16)
    dc_ref[...] = dc_wide[...].reshape(dc_ref.shape).astype(BF16)
    ddt_ref[...] = ddt_wide[...].astype(BF16)
    for source, target in ((db_ref, db_hbm), (dc_ref, dc_hbm), (ddt_ref, ddt_hbm)):
        moves.append(pltpu.make_async_copy(source, target, sems.at[len(moves)]))
        moves[-1].start()
    for move in moves:
        move.wait()


def segment_decays(place, bufs, rate):
    dts = [place.dt(buf) for buf in bufs]
    cums = cumulate(cat([dt * rate for dt in dts], 0), False)
    cums = [cums[i * ROWS : (i + 1) * ROWS] for i in range(len(bufs))]
    starts, start = [], jnp.zeros((ROWS, 1), F32)
    for cum in cums:
        starts.append(start + cum)
        start = start + cum[:, place.tokens - 1 :]
    return dts, [start - one for one in starts], starts


def encode(value, scale):
    size = jnp.exp2(jnp.abs(value) * (CODE_SPAN / scale) - CODE_SPAN / 2)
    return jnp.where(value < 0.0, -size, size).astype(BF16)


def decode(code, scale):
    code = code.astype(F32)
    size = (jnp.log(jnp.abs(code)) * LOG2E + CODE_SPAN / 2) * (scale / CODE_SPAN)
    return jnp.where(code < 0.0, -size, size)


def totals_kernel(place, flag_ref, rate_ref, *refs):
    xy_ref, bc_ref, (u_rows, u_parts, v_parts, own_ref, send_ref) = place.bufs(refs)
    width, tokens = place.width, place.tokens
    totals_s, totals_g, logs = [], [], []
    for seg in range(2):
        xys, bcs = ([ref.at[seg, i] for i in range(place.half)] for ref in (xy_ref, bc_ref))
        dts, ends, starts = segment_decays(place, bcs, rate_ref[...])
        for i, xy in enumerate(xys):
            u_rows[seg, i] = dts[i] * jnp.exp(ends[i])
            rows = slice(i * tokens, (i + 1) * tokens)
            hi, lo = split2(spread_rows(u_rows[seg, i], width) * cat(place.x(xy), 1).astype(F32))
            u_parts[seg, 0, rows], u_parts[seg, 1, rows] = hi, lo
            start_wide = spread_rows(jnp.exp(starts[i]), width)
            hi, lo = split2(start_wide * cat(place.dy(xy), 1).astype(F32))
            v_parts[seg, 0, rows], v_parts[seg, 1, rows] = hi, lo
        b_turned = jnp.transpose(cat([place.b(bc) for bc in bcs], 0).astype(F32)).astype(BF16)
        c_turned = jnp.transpose(cat([place.c(bc) for bc in bcs], 0).astype(F32)).astype(BF16)
        totals_s.append(dot(b_turned, u_parts[seg, 0]) + dot(b_turned, u_parts[seg, 1]))
        totals_g.append(dot(c_turned, v_parts[seg, 0]) + dot(c_turned, v_parts[seg, 1]))
        logs.append(jnp.broadcast_to(start_wide[tokens - 1 :, :], (ROWS, width)))
    front = flag_ref[0] > 0.5
    values = [totals_s[0], jnp.where(front, totals_s[1], totals_g[0]), totals_g[1]]
    tops = [jnp.maximum(jnp.max(jnp.abs(value), axis=0, keepdims=True), 1e-30) for value in values]
    scales = [(top * 1.01).astype(BF16).astype(F32) for top in tops]
    for i, (value, scale) in enumerate(zip(values, scales)):
        send_ref[i * STATE : (i + 1) * STATE] = encode(value, scale)
    notes = scales + [part.astype(F32) for log in logs for part in split2(log[:1])]
    send_ref[3 * STATE :] = cat(notes + [jnp.zeros((TILE - len(notes), width), F32)], 0).astype(BF16)
    own_ref[:STATE] = values[0]
    own_ref[STATE : 2 * STATE] = values[2]
    own_ref[2 * STATE :] = cat(logs, 0)


def head_sums(values, width):
    hi, lo = split2(values)
    picker = spread_matrix(2, width)
    return (dot_nt(picker, hi) + dot_nt(picker, lo))[:ROWS]


def fold(value):
    total = value[:ROWS]
    for i in range(1, value.shape[0] // ROWS):
        total = total + value[i * ROWS : (i + 1) * ROWS]
    return total


def middle_kernel(place, rate_ref, *refs):
    xy_ref, bc_ref, outs = place.bufs(refs)
    for seg in range(2):
        chunks = [ref.at[seg] for ref in (xy_ref, bc_ref)]
        middle_segment(place, rate_ref[...], *chunks, *[ref.at[seg] for ref in outs])


def middle_segment(place, rate, xy_ref, bc_ref, dx_ref, ddt_ref, db_ref, dc_ref):
    tokens, width = place.tokens, place.width
    chunks, xys = ([ref.at[i] for i in range(place.half)] for ref in (bc_ref, xy_ref))
    dts = [place.dt(chunk) for chunk in chunks]
    cums = cumulate(cat([dt * rate for dt in dts], 0), False)
    cums = [cums[i * ROWS : (i + 1) * ROWS] for i in range(len(chunks))]
    ends = [cum[:, tokens - 1 :] for cum in cums]
    starts = [jnp.exp(cum) for cum in cums]

    us, vs, end_wides, adds_s, adds_g, through = [], [], [], [], [], []
    for i, chunk in enumerate(chunks):
        cols = columns(cat([dts[i] * jnp.exp(ends[i] - cums[i]), starts[i]], 0))
        end_wide, start_wide = widen(cols, 0, width), widen(cols, ROWS, width)
        u, v = split2(end_wide * cat(place.x(xys[i]), 1).astype(F32)), split2(start_wide * cat(place.dy(xys[i]), 1).astype(F32))
        b_here, c_here = place.b(chunk), place.c(chunk)
        adds_s.append(dot_tn(cat([b_here, b_here], 0), cat(list(u), 0)))
        adds_g.append(dot_tn(cat([c_here, c_here], 0), cat(list(v), 0)))
        through.append(start_wide[tokens - 1 :, :])
        us.append(u)
        vs.append(v)
        end_wides.append(end_wide)
    states, grads = [jnp.zeros((STATE, width), F32)], [jnp.zeros((STATE, width), F32)]
    for i in range(len(chunks) - 1):
        states.append(through[i] * states[-1] + adds_s[i])
        grads.append(through[-1 - i] * grads[-1] + adds_g[-1 - i])
    grads = grads[::-1]
    corners = head_sums(cat([fold(through[i] * (states[i] * grads[i])) for i in range(len(chunks))], 0), width)

    mask = upper(tokens, False)
    left = lax.broadcasted_iota(jnp.int32, (tokens, LANES), 1) < HEAD_DIM
    left, right = left.astype(F32).astype(BF16), (~left).astype(F32).astype(BF16)
    for i, chunk in enumerate(chunks):
        b_here, c_here = place.b(chunk), place.c(chunk)
        cum = cums[i] * LOG2E
        cols = jnp.transpose(cum - jnp.log(jnp.where(dts[i] > 0.0, dts[i], 1.0)) * LOG2E)
        k_two = dot_nt(b_here, c_here)
        s_hi, s_lo = split2(states[i])
        g_hi, g_lo = split2(grads[i])
        b_grad = end_wides[i] * dot(cat([b_here, b_here], 1), cat([g_hi, g_lo], 0))
        c_state = dot(cat([c_here, c_here], 1), cat([s_hi, s_lo], 0))
        one_sum = jnp.zeros((tokens, tokens), F32)
        rows, alongs = [], []
        for block, (x_here, dy_here) in enumerate(zip(place.x(xys[i]), place.dy(xys[i]))):
            lanes = slice(block * LANES, (block + 1) * LANES)
            sides = cat([dy_here * left, dy_here * right], 0)
            k_one = dot_nt(x_here, sides)
            tops, bottoms = [], []
            for side in range(2):
                head = 2 * block + side
                gap = jnp.where(mask, cum[head : head + 1, :] - cols[:, head : head + 1], -1e30)
                decay = jnp.exp2(gap)
                a_one = decay * k_one[:, side * tokens : (side + 1) * tokens]
                a_two = decay * k_two
                one_sum = one_sum + a_one
                rows.append(jnp.sum(a_one * k_two, axis=0, keepdims=True))
                hi_two, lo_two = split2(a_two)
                tops.append(hi_two)
                bottoms.append(lo_two)
            both = dot(cat([cat(tops, 1), cat(bottoms, 1)], 0), sides)
            dx = both[:tokens] + both[tokens:] + b_grad[:, lanes]
            dx_ref[i, :, lanes] = dx
            alongs.append(dx * x_here.astype(F32))
        if len(rows) < ROWS:
            rows.append(jnp.zeros((ROWS - len(rows), tokens), F32))
        db = dot(cat(list(split2(one_sum)), 1), cat([c_here, c_here], 0))
        dc = dot(cat(list(split2(jnp.transpose(one_sum))), 1), cat([b_here, b_here], 0))
        db_ref[i] = db + head_products(us[i], (g_hi, g_lo))
        dc_ref[i] = dc + head_products(vs[i], (s_hi, s_lo))
        sums = head_sums(cat([cat(alongs, 1), cat(place.dy(xys[i]), 1).astype(F32) * c_state], 0), width)
        along = sums[:, :tokens]
        later = starts[i] * sums[:, tokens:]
        corner = jnp.sum(corners[:, i * ROWS : (i + 1) * ROWS], axis=1, keepdims=True)
        flow = along - cat(rows, 0) - later
        dlog = corner + jnp.sum(later, axis=1, keepdims=True) + cumulate(flow, True)
        ddt_ref[i] = along / jnp.where(dts[i] > 0.0, dts[i], 1.0) + rate * dlog


def finish_kernel(place, flag_ref, rate_ref, *refs):
    xy_ref, bc_ref, (u_rows, u_parts, v_parts, own, got, dx_in, ddt_in, db_in, dc_in, *refs) = place.bufs(refs)
    old = [] if place.piece == 0 else [refs.pop(0), refs.pop(0)]
    out, *new = refs
    rate, tokens, width = rate_ref[...], place.tokens, place.width
    front = flag_ref[0] > 0.5
    notes = got[3 * STATE :].astype(F32)
    sent0, sent2, logs = own[:STATE], own[STATE : 2 * STATE], (own[2 * STATE : 2 * STATE + 1], own[2 * STATE + ROWS : 2 * STATE + ROWS + 1])
    got0, got1, got2 = (decode(got[i * STATE : (i + 1) * STATE], notes[i : i + 1]) for i in range(3))
    mine = jnp.where(front, logs[1], logs[0])
    other = jnp.where(front, notes[3:4] + notes[4:5], notes[5:6] + notes[6:7])
    far = got1 + other * (jnp.where(front, sent2, sent0) + mine * jnp.where(front, got2, got0))
    near = jnp.where(front, got0, got2) + other * jnp.where(front, sent0, sent2)
    none = jnp.zeros_like(far)
    states = [jnp.where(front, none, got0), jnp.where(front, near, far)]
    grads = [jnp.where(front, far, near), jnp.where(front, got2, none)]
    for seg, (state, grad, through) in enumerate(zip(states, grads, logs)):
        s_hi, s_lo = split2(state)
        g_hi, g_lo = split2(grad)
        corner = jnp.sum(head_sums(fold(through * (grad * state)), width), axis=1, keepdims=True)
        xys, bcs = ([ref.at[seg, i] for i in range(place.half)] for ref in (xy_ref, bc_ref))
        b_all, c_all = cat([place.b(bc) for bc in bcs], 0), cat([place.c(bc) for bc in bcs], 0)
        b_grad = dot(cat([b_all, b_all], 1), cat([g_hi, g_lo], 0))
        c_state = dot(cat([c_all, c_all], 1), cat([s_hi, s_lo], 0))
        u_hi, u_lo, v_hi, v_lo = u_parts[seg, 0], u_parts[seg, 1], v_parts[seg, 0], v_parts[seg, 1]
        db = head_products((u_hi, u_lo), (g_hi, g_lo))
        dc = head_products((v_hi, v_lo), (s_hi, s_lo))
        ins = []
        for i, xy in enumerate(xys):
            rows = slice(i * tokens, (i + 1) * tokens)
            extra = widen(columns(u_rows[seg, i]), 0, width) * b_grad[rows]
            dx = (dx_in[seg, i] + extra).astype(BF16)
            for block in range(place.blocks):
                out[seg, i, block * tokens : (block + 1) * tokens, :] = dx[:, block * LANES : (block + 1) * LANES]
            ins.append(extra * cat(place.x(xy), 1).astype(F32))
            db_here, dc_here = db_in[seg, i] + db[rows], dc_in[seg, i] + dc[rows]
            if old:
                db_here, dc_here = db_here + old[0][seg, i], dc_here + old[1][seg, i]
            if place.last:
                first = place.blocks * tokens
                out[seg, i, first : first + tokens, :] = db_here.astype(BF16)
                out[seg, i, first + tokens : first + 2 * tokens, :] = dc_here.astype(BF16)
            else:
                new[0][seg, i], new[1][seg, i] = db_here, dc_here
        ins = head_sums(cat(ins, 0), width)
        laters = head_sums((v_hi.astype(F32) + v_lo.astype(F32)) * c_state, width)
        ins, laters = ([sums[:, i * tokens : (i + 1) * tokens] for i in range(place.half)] for sums in (ins, laters))
        over = cumulate(cat([one - other for one, other in zip(ins, laters)], 0), True)
        rest = corner
        for later in laters:
            rest = rest + jnp.sum(later, axis=1, keepdims=True)
        for i, bc in enumerate(bcs):
            dlog = rest + over[i * ROWS : (i + 1) * ROWS]
            rest = rest + jnp.sum(ins[i] - laters[i], axis=1, keepdims=True)
            dt = place.dt(bc)
            ddt = ddt_in[seg, i] + ins[i] / jnp.where(dt > 0.0, dt, 1.0) + rate * dlog
            out[seg, i, place.rows_out - TILE :, :] = cat([ddt, jnp.zeros_like(ddt)], 0).astype(BF16)


def on_device(x_seq, dy_seq, dt_seq, a_log, b_seq, c_seq):
    tokens = x_seq.shape[0]
    half = lax.axis_size("lo")
    count = 2 * half
    heads = HEADS // count
    blocks = heads * HEAD_DIM // LANES
    copies = count // GROUPS
    pieces = PIECES if blocks % PIECES == 0 else 1
    places = [Place(tokens, half, blocks // pieces, pieces, piece) for piece in range(pieces)]
    width = places[0].width
    front = 1.0 - lax.axis_index("hi").astype(F32)
    flags = jnp.stack([front, 1.0 - front])

    def swap(value):
        return lax.all_to_all(value, ("ctx", "lo"), split_axis=0, concat_axis=0, tiled=True)

    rates = -jnp.exp(lax.dynamic_slice_in_dim(a_log, lax.axis_index(("ctx", "lo")) * heads, heads)).reshape(pieces, -1)
    rates = jnp.pad(rates, ((0, 0), (0, ROWS - heads // pieces)))
    rates = jnp.broadcast_to(rates[:, :, None], (pieces, ROWS, LANES))

    def f32(*shape):
        return jax.ShapeDtypeStruct((2, half) + shape, F32)

    def bf16(*shape):
        return jax.ShapeDtypeStruct(shape, BF16)

    smem = pl.BlockSpec(memory_space=pltpu.SMEM)
    hbm, vmem = pl.BlockSpec(memory_space=pl.ANY), pl.BlockSpec(memory_space=pltpu.VMEM)
    params = pltpu.CompilerParams(vmem_limit_bytes=24 * 1024 * 1024)
    alone = pltpu.CompilerParams(vmem_limit_bytes=58 * 1024 * 1024)
    wides = [pltpu.VMEM((tokens * GROUPS, STATE), F32), pltpu.VMEM((tokens * GROUPS, STATE), F32), pltpu.VMEM((HEADS, tokens), F32)]
    seqs = (b_seq, c_seq, dt_seq.T, x_seq, dy_seq)

    def packed(place):
        if place.piece == 0:
            return pl.pallas_call(
                functools.partial(pack_kernel, place, count, copies),
                in_specs=[hbm] * 5,
                out_specs=vmem,
                out_shape=bf16(count, place.rows_in, LANES),
                scratch_shapes=[pltpu.VMEM(seq.shape, BF16) for seq in seqs] + wides + [pltpu.SemaphoreType.DMA((5,))],
                compiler_params=alone,
                name="pack",
            )(*seqs)
        return pl.pallas_call(
            functools.partial(pack_more_kernel, place, count),
            in_specs=[hbm] * 2,
            out_specs=vmem,
            out_shape=bf16(count, place.rows_in, LANES),
            scratch_shapes=[pltpu.VMEM(x_seq.shape, BF16), pltpu.VMEM(x_seq.shape, BF16), pltpu.SemaphoreType.DMA((2,))],
            compiler_params=params,
            name="pack_more",
        )(x_seq, dy_seq)

    bufs = [swap(packed(place)).reshape(2, half, place.rows_in, LANES) for place in places]
    owned, coded = (2 * STATE + 2 * ROWS, width), (3 * STATE + TILE, width)
    within = [f32(tokens, width), f32(ROWS, tokens), f32(tokens, STATE), f32(tokens, STATE)]
    parts_shape = bf16(2, 2, half * tokens, width)
    def data_of(place):
        return [bufs[0]] if place.piece == 0 else [bufs[place.piece], bufs[0]]

    def totals_of(place):
        data = data_of(place)
        return pl.pallas_call(
            functools.partial(totals_kernel, place),
            in_specs=[smem] + [vmem] * (1 + len(data)),
            out_specs=[vmem] * 5,
            out_shape=[f32(ROWS, tokens), parts_shape, parts_shape, jax.ShapeDtypeStruct(owned, F32), bf16(*coded)],
            compiler_params=params,
            name="totals",
        )(flags, rates[place.piece], *data)

    def middle_of(place, rate):
        data = data_of(place)
        return pl.pallas_call(
            functools.partial(middle_kernel, place),
            in_specs=[vmem] * (1 + len(data)),
            out_specs=[vmem] * 4,
            out_shape=within,
            compiler_params=params,
            cost_estimate=pl.CostEstimate(flops=6_000_000_000, bytes_accessed=20_000_000, transcendentals=2_000_000),
            name="middle",
        )(rate, *data)

    def finish_of(place, passed, got, parts, sums):
        data = data_of(place)
        new = [] if place.last else [f32(tokens, STATE)] * 2
        return pl.pallas_call(
            functools.partial(finish_kernel, place),
            in_specs=[smem] + [vmem] * (10 + len(data) + len(sums)),
            out_specs=[vmem] * (1 + len(new)),
            out_shape=[bf16(2, half, place.rows_out, LANES)] + new,
            compiler_params=params,
            name="finish",
        )(flags, rates[place.piece], *data, *passed, got, *parts, *sums)

    def after(value, *others):
        return lax.optimization_barrier((value, *others))[0]

    homes, sums, pending = [], [], []
    for place in places:
        *passed, send = totals_of(place)
        pending.append((place, passed, lax.ppermute(send, "hi", [(0, 1), (1, 0)]), send))
    rate = rates[0]
    for i, (place, passed, got, _) in enumerate(pending):
        parts = middle_of(place, rate)
        if not place.last:
            got = after(got, pending[i + 1][3])
        out, *sums = finish_of(place, passed, got, parts, sums)
        homes.append(swap(out.reshape(count, place.rows_out, LANES)))
        if not place.last:
            rate = after(rates[i + 1], out)

    dx, ddt, db, dc = pl.pallas_call(
        functools.partial(unpack_kernel, places, count, copies),
        in_specs=[vmem] * pieces,
        out_specs=[hbm] * 4,
        out_shape=[bf16(*x_seq.shape), bf16(HEADS, tokens), bf16(*b_seq.shape), bf16(*c_seq.shape)],
        scratch_shapes=[pltpu.VMEM(x_seq.shape, BF16), pltpu.VMEM(b_seq.shape, BF16), pltpu.VMEM(c_seq.shape, BF16), pltpu.VMEM((HEADS, tokens), BF16)]
        + wides
        + [pltpu.SemaphoreType.DMA((7,))],
        compiler_params=params,
        name="unpack",
    )(*homes)
    return dx, ddt.T, db, dc


def solution(mesh):
    parts, head, ctx = (mesh.shape[name] for name in ("grp", "head", "ctx"))
    split = jax.sharding.Mesh(mesh.devices.reshape(parts, 2, head // 2, ctx), ("grp", "hi", "lo", "ctx"))
    spec = P(("grp", "ctx", "hi", "lo"))
    return jax.shard_map(
        on_device,
        mesh=split,
        in_specs=(spec, spec, spec, P(), spec, spec),
        out_specs=(spec, spec, spec, spec),
        check_vma=False,
    )
```

```python
import functools
from typing import NamedTuple

import jax
import jax.numpy as jnp
from jax import lax
from jax.experimental import pallas as pl
from jax.experimental.pallas import tpu as pltpu
from jax.sharding import PartitionSpec as P

HEADS = 64
HEAD_DIM = 64
STATE = 128
GROUPS = 8
LANES = 128
ROWS = 8
TILE = 16
LOG2E = 1.4426950408889634
CODE_SPAN = 250.0
IN_FLIGHT = 5
F32 = jnp.float32
BF16 = jnp.bfloat16


def split2(value):
    hi = value.astype(BF16)
    return hi, (value - hi.astype(F32)).astype(BF16)


def split3(value):
    hi = value.astype(BF16)
    rest = value - hi.astype(F32)
    mid = rest.astype(BF16)
    return hi, mid, (rest - mid.astype(F32)).astype(BF16)


def dot(a, b):
    return lax.dot_general(a, b, (((1,), (0,)), ((), ())), preferred_element_type=F32)


def dot_nt(a, b):
    return lax.dot_general(a, b, (((1,), (1,)), ((), ())), preferred_element_type=F32)


def dot_tn(a, b):
    return lax.dot_general(a, b, (((0,), (0,)), ((), ())), preferred_element_type=F32)


def cat(parts, axis):
    return jnp.concatenate(parts, axis=axis)


def upper(size, strict):
    row = lax.broadcasted_iota(jnp.int32, (size, size), 0)
    col = lax.broadcasted_iota(jnp.int32, (size, size), 1)
    return row < col if strict else row <= col


def cumulate(rows, strict):
    tri = upper(rows.shape[1], strict).astype(F32).astype(BF16)
    sums = dot(cat([part.astype(F32) for part in split3(rows)], 0).astype(BF16), tri)
    size = rows.shape[0]
    return sums[:size] + sums[size : 2 * size] + sums[2 * size :]


def spread_matrix(terms, width):
    row = lax.broadcasted_iota(jnp.int32, (terms * ROWS, width), 0)
    col = lax.broadcasted_iota(jnp.int32, (terms * ROWS, width), 1)
    return (row % ROWS == col // HEAD_DIM).astype(F32).astype(BF16)


def spread_rows(rows, width):
    hi, lo = split2(rows)
    terms = cat([hi.astype(F32), lo.astype(F32)], 0).astype(BF16)
    return dot_tn(terms, spread_matrix(2, width))


def columns(rows):
    return jnp.transpose(cat([rows, jnp.zeros((LANES - rows.shape[0], rows.shape[1]), F32)], 0))


def widen(cols, first, width):
    lane = lax.broadcasted_iota(jnp.int32, cols.shape, 1)
    heads = [first + lane // HEAD_DIM + 2 * block for block in range(width // LANES)]
    return cat([jnp.take_along_axis(cols, head, axis=1) for head in heads], 1)


def head_products(values, factors):
    rows = values[0].shape[0]
    both = dot_nt(cat(list(values), 0), cat(list(factors), 0))
    size = factors[0].shape[0]
    return (both[:rows, :size] + (both[:rows, size:] + both[rows:, :size])) + both[rows:, size:]


class Place(NamedTuple):
    tokens: int
    half: int
    blocks: int

    @property
    def width(self):
        return self.blocks * LANES

    @property
    def b_row(self):
        return 2 * self.blocks * self.tokens

    @property
    def dt_row(self):
        return self.b_row + 2 * self.tokens

    @property
    def rows_in(self):
        return self.dt_row + TILE

    @property
    def rows_out(self):
        return (self.blocks + 2) * self.tokens + TILE

    def x(self, buf):
        return [buf[i * self.tokens : (i + 1) * self.tokens, :] for i in range(self.blocks)]

    def dy(self, buf):
        return [buf[i * self.tokens : (i + 1) * self.tokens, :] for i in range(self.blocks, 2 * self.blocks)]

    def b(self, buf):
        return buf[self.b_row : self.b_row + self.tokens, :]

    def c(self, buf):
        return buf[self.b_row + self.tokens : self.b_row + 2 * self.tokens, :]

    def dt(self, buf):
        return buf[self.dt_row : self.dt_row + TILE, :].astype(F32)[:ROWS]


def partner(place, k):
    return (lax.axis_index("ctx") ^ (k // place.half)) * place.half + (lax.axis_index("lo") ^ (k % place.half))


def pack_kernel(place, count, copies, *refs):
    (b_hbm, c_hbm, dt_hbm, x_hbm, dy_hbm), outs, refs = refs[:5], refs[5 : 5 + count], refs[5 + count :]
    b_ref, c_ref, dt_ref, b_wide, c_wide, dt_wide, x_ref, dy_ref, ready, sems, out_sems = refs
    tokens, blocks, width = place.tokens, place.blocks, place.width
    heads = HEADS // count
    dests = [partner(place, k) for k in range(count)]
    loads = [(b_hbm, b_ref), (c_hbm, c_ref), (dt_hbm, dt_ref)]
    for k, dest in enumerate(dests):
        columns = pl.ds(pl.multiple_of(dest * width, LANES), width)
        loads += [(x_hbm.at[:, columns], x_ref.at[k]), (dy_hbm.at[:, columns], dy_ref.at[k])]
    loads = [pltpu.make_async_copy(source, target, sems.at[i]) for i, (source, target) in enumerate(loads)]
    for load in loads:
        load.start()
    for load in loads[:3]:
        load.wait()
    every = tokens * GROUPS
    b_wide[:every] = b_ref[...].astype(F32).reshape(every, STATE)
    c_wide[:every] = c_ref[...].astype(F32).reshape(every, STATE)
    dt_wide[...] = dt_ref[...].astype(F32)
    stores = []
    for k, (dest, out) in enumerate(zip(dests, outs)):
        mine = pl.ds(lax.div(dest, copies), tokens, stride=GROUPS)
        ready[k, place.b_row : place.b_row + tokens] = b_wide[mine, :].astype(BF16)
        ready[k, place.b_row + tokens : place.dt_row] = c_wide[mine, :].astype(BF16)
        dt = dt_wide[pl.ds(dest * heads, heads), :]
        ready[k, place.dt_row :] = cat([dt, jnp.zeros((TILE - heads, tokens), F32)], 0).astype(BF16)
        for load in loads[3 + 2 * k : 5 + 2 * k]:
            load.wait()
        for part, ref in enumerate((x_ref, dy_ref)):
            for i in range(blocks):
                row = (part * blocks + i) * tokens
                ready[k, row : row + tokens] = ref[k, :, i * LANES : (i + 1) * LANES]
        stores.append(pltpu.make_async_copy(ready.at[k], out, out_sems.at[k]))
        stores[-1].start()
    for store in stores:
        store.wait()


def unpack_kernel(place, count, copies, *refs):
    homes, refs = refs[:count], refs[count:]
    dx_hbm, ddt_hbm, db_hbm, dc_hbm, dx_ref, db_ref, dc_ref, ddt_ref, db_wide, dc_wide, ddt_wide, sems = refs
    tokens, blocks, width = place.tokens, place.blocks, place.width
    heads = HEADS // count
    first = blocks * tokens
    moves = []

    def move(source, target):
        moves.append(pltpu.make_async_copy(source, target, sems.at[len(moves)]))
        moves[-1].start()

    if copies > 1:
        db_wide[...] = jnp.zeros_like(db_wide)
        dc_wide[...] = jnp.zeros_like(dc_wide)
    for k, home in enumerate(homes):
        source = partner(place, k)
        mine = pl.ds(lax.div(source, copies), tokens, stride=GROUPS)
        for to, at in ((db_wide, first), (dc_wide, first + tokens)):
            part = home[at : at + tokens, :].astype(F32)
            to[mine, :] = part if copies == 1 else to[mine, :] + part
        ddt_wide[pl.ds(source * heads, heads), :] = home[place.rows_out - TILE :, :].astype(F32)[:heads]
        for i in range(blocks):
            dx_ref[k, :, i * LANES : (i + 1) * LANES] = home[i * tokens : (i + 1) * tokens, :]
        move(dx_ref.at[k], dx_hbm.at[:, pl.ds(pl.multiple_of(source * width, LANES), width)])
    every = tokens * GROUPS
    db_ref[...] = db_wide[:every].reshape(db_ref.shape).astype(BF16)
    dc_ref[...] = dc_wide[:every].reshape(dc_ref.shape).astype(BF16)
    ddt_ref[...] = ddt_wide[...].astype(BF16)
    for source, target in ((db_ref, db_hbm), (dc_ref, dc_hbm), (ddt_ref, ddt_hbm)):
        move(source, target)
    for one in moves:
        one.wait()


def segment_decays(place, bufs, rate):
    dts = [place.dt(buf) for buf in bufs]
    cums = cumulate(cat([dt * rate for dt in dts], 0), False)
    cums = [cums[i * ROWS : (i + 1) * ROWS] for i in range(len(bufs))]
    starts, start = [], jnp.zeros((ROWS, 1), F32)
    for cum in cums:
        starts.append(start + cum)
        start = start + cum[:, place.tokens - 1 :]
    return dts, [start - one for one in starts], starts


def encode(value, scale):
    size = jnp.exp2(jnp.abs(value) * (CODE_SPAN / scale) - CODE_SPAN / 2)
    return jnp.where(value < 0.0, -size, size).astype(BF16)


def decode(code, scale):
    code = code.astype(F32)
    size = (jnp.log(jnp.abs(code)) * LOG2E + CODE_SPAN / 2) * (scale / CODE_SPAN)
    return jnp.where(code < 0.0, -size, size)


def totals_kernel(place, turn, rate_ref, *refs):
    blocks, refs = refs[: place.half], refs[place.half :]
    others, refs = ([], refs) if turn else (refs[:3], refs[3:])
    buf, u_rows, u_parts, v_parts, *refs = refs
    width, tokens = place.width, place.tokens
    for k, block in enumerate(blocks):
        lo = lax.axis_index("lo") ^ k
        for at in range(0, place.rows_in, tokens):
            rows = slice(at, min(at + tokens, place.rows_in))
            buf[lo, rows] = block[rows]
    chunks = [buf.at[i] for i in range(place.half)]
    dts, ends, starts = segment_decays(place, chunks, rate_ref[...])
    for i, chunk in enumerate(chunks):
        u_rows[i] = dts[i] * jnp.exp(ends[i])
        rows = slice(i * tokens, (i + 1) * tokens)
        hi, lo = split2(spread_rows(u_rows[i], width) * cat(place.x(chunk), 1).astype(F32))
        u_parts[0, rows], u_parts[1, rows] = hi, lo
        start_wide = spread_rows(jnp.exp(starts[i]), width)
        hi, lo = split2(start_wide * cat(place.dy(chunk), 1).astype(F32))
        v_parts[0, rows], v_parts[1, rows] = hi, lo
    b_turned = jnp.transpose(cat([place.b(chunk) for chunk in chunks], 0).astype(F32)).astype(BF16)
    c_turned = jnp.transpose(cat([place.c(chunk) for chunk in chunks], 0).astype(F32)).astype(BF16)
    total_s = dot(b_turned, u_parts[0]) + dot(b_turned, u_parts[1])
    total_g = dot(c_turned, v_parts[0]) + dot(c_turned, v_parts[1])
    log = jnp.broadcast_to(start_wide[tokens - 1 :, :], (ROWS, width))
    if turn:
        for ref, value in zip(refs, (total_s, total_g, log)):
            ref[...] = value
        return
    own_ref, send_ref = refs
    front, early = lax.axis_index("hi") == 0, lax.axis_index("ctx") == 0
    other_s, other_g, other_log = (ref[...] for ref in others)
    logs = [jnp.where(early, log, other_log), jnp.where(early, other_log, log)]
    middle = jnp.where(front, jnp.where(early, other_s, total_s), jnp.where(early, total_g, other_g))
    values = [jnp.where(early, total_s, other_s), middle, jnp.where(early, other_g, total_g)]
    tops = [jnp.maximum(jnp.max(jnp.abs(value), axis=0, keepdims=True), 1e-30) for value in values]
    scales = [(top * 1.01).astype(BF16).astype(F32) for top in tops]
    for i, (value, scale) in enumerate(zip(values, scales)):
        send_ref[i * STATE : (i + 1) * STATE] = encode(value, scale)
    notes = scales + [part.astype(F32) for log in logs for part in split2(log[:1])]
    send_ref[3 * STATE :] = cat(notes + [jnp.zeros((TILE - len(notes), width), F32)], 0).astype(BF16)
    own_ref[:STATE] = values[0]
    own_ref[STATE : 2 * STATE] = values[2]
    own_ref[2 * STATE :] = cat(logs, 0)


def head_sums(values, width):
    hi, lo = split2(values)
    picker = spread_matrix(2, width)
    return (dot_nt(picker, hi) + dot_nt(picker, lo))[:ROWS]


def fold(value):
    total = value[:ROWS]
    for i in range(1, value.shape[0] // ROWS):
        total = total + value[i * ROWS : (i + 1) * ROWS]
    return total


def middle_kernel(place, rate_ref, *refs):
    for turn in range(2):
        middle_segment(place, rate_ref[...], refs[turn], *refs[2 + 4 * turn : 6 + 4 * turn])


def middle_segment(place, rate, buf, dx_ref, ddt_ref, db_ref, dc_ref):
    tokens, width = place.tokens, place.width
    chunks = [buf.at[i] for i in range(place.half)]
    dts = [place.dt(chunk) for chunk in chunks]
    cums = cumulate(cat([dt * rate for dt in dts], 0), False)
    cums = [cums[i * ROWS : (i + 1) * ROWS] for i in range(len(chunks))]
    ends = [cum[:, tokens - 1 :] for cum in cums]
    starts = [jnp.exp(cum) for cum in cums]

    us, vs, end_wides, adds_s, adds_g, through = [], [], [], [], [], []
    for i, chunk in enumerate(chunks):
        cols = columns(cat([dts[i] * jnp.exp(ends[i] - cums[i]), starts[i]], 0))
        end_wide, start_wide = widen(cols, 0, width), widen(cols, ROWS, width)
        u, v = split2(end_wide * cat(place.x(chunk), 1).astype(F32)), split2(start_wide * cat(place.dy(chunk), 1).astype(F32))
        b_here, c_here = place.b(chunk), place.c(chunk)
        adds_s.append(dot_tn(cat([b_here, b_here], 0), cat(list(u), 0)))
        adds_g.append(dot_tn(cat([c_here, c_here], 0), cat(list(v), 0)))
        through.append(start_wide[tokens - 1 :, :])
        us.append(u)
        vs.append(v)
        end_wides.append(end_wide)
    states, grads = [jnp.zeros((STATE, width), F32)], [jnp.zeros((STATE, width), F32)]
    for i in range(len(chunks) - 1):
        states.append(through[i] * states[-1] + adds_s[i])
        grads.append(through[-1 - i] * grads[-1] + adds_g[-1 - i])
    grads = grads[::-1]
    corners = head_sums(cat([fold(through[i] * (states[i] * grads[i])) for i in range(len(chunks))], 0), width)

    mask = upper(tokens, False)
    left = lax.broadcasted_iota(jnp.int32, (tokens, LANES), 1) < HEAD_DIM
    left, right = left.astype(F32).astype(BF16), (~left).astype(F32).astype(BF16)
    for i, chunk in enumerate(chunks):
        b_here, c_here = place.b(chunk), place.c(chunk)
        cum = cums[i] * LOG2E
        cols = jnp.transpose(cum - jnp.log(jnp.where(dts[i] > 0.0, dts[i], 1.0)) * LOG2E)
        k_two = dot_nt(b_here, c_here)
        s_hi, s_lo = split2(states[i])
        g_hi, g_lo = split2(grads[i])
        b_grad = end_wides[i] * dot(cat([b_here, b_here], 1), cat([g_hi, g_lo], 0))
        c_state = dot(cat([c_here, c_here], 1), cat([s_hi, s_lo], 0))
        one_sum = jnp.zeros((tokens, tokens), F32)
        rows, alongs = [], []
        for block, (x_here, dy_here) in enumerate(zip(place.x(chunk), place.dy(chunk))):
            lanes = slice(block * LANES, (block + 1) * LANES)
            sides = cat([dy_here * left, dy_here * right], 0)
            k_one = dot_nt(x_here, sides)
            tops, bottoms = [], []
            for side in range(2):
                head = 2 * block + side
                gap = jnp.where(mask, cum[head : head + 1, :] - cols[:, head : head + 1], -1e30)
                decay = jnp.exp2(gap)
                a_one = decay * k_one[:, side * tokens : (side + 1) * tokens]
                a_two = decay * k_two
                one_sum = one_sum + a_one
                rows.append(jnp.sum(a_one * k_two, axis=0, keepdims=True))
                hi_two, lo_two = split2(a_two)
                tops.append(hi_two)
                bottoms.append(lo_two)
            both = dot(cat([cat(tops, 1), cat(bottoms, 1)], 0), sides)
            dx = both[:tokens] + both[tokens:] + b_grad[:, lanes]
            dx_ref[i, :, lanes] = dx
            alongs.append(dx * x_here.astype(F32))
        if len(rows) < ROWS:
            rows.append(jnp.zeros((ROWS - len(rows), tokens), F32))
        db = dot(cat(list(split2(one_sum)), 1), cat([c_here, c_here], 0))
        dc = dot(cat(list(split2(jnp.transpose(one_sum))), 1), cat([b_here, b_here], 0))
        db_ref[i] = db + head_products(us[i], (g_hi, g_lo))
        dc_ref[i] = dc + head_products(vs[i], (s_hi, s_lo))
        sums = head_sums(cat([cat(alongs, 1), cat(place.dy(chunk), 1).astype(F32) * c_state], 0), width)
        along = sums[:, :tokens]
        later = starts[i] * sums[:, tokens:]
        corner = jnp.sum(corners[:, i * ROWS : (i + 1) * ROWS], axis=1, keepdims=True)
        flow = along - cat(rows, 0) - later
        dlog = corner + jnp.sum(later, axis=1, keepdims=True) + cumulate(flow, True)
        ddt_ref[i] = along / jnp.where(dts[i] > 0.0, dts[i], 1.0) + rate * dlog


def carried_in(own, got, seg, front):
    notes = got[3 * STATE :].astype(F32)
    sent0, sent2, logs = own[:STATE], own[STATE : 2 * STATE], (own[2 * STATE : 2 * STATE + 1], own[2 * STATE + ROWS : 2 * STATE + ROWS + 1])
    got0, got1, got2 = (decode(got[i * STATE : (i + 1) * STATE], notes[i : i + 1]) for i in range(3))
    mine = jnp.where(front, logs[1], logs[0])
    other = jnp.where(front, notes[3:4] + notes[4:5], notes[5:6] + notes[6:7])
    far = got1 + other * (jnp.where(front, sent2, sent0) + mine * jnp.where(front, got2, got0))
    near = jnp.where(front, got0, got2) + other * jnp.where(front, sent0, sent2)
    none = jnp.zeros_like(far)
    states = [jnp.where(front, none, got0), jnp.where(front, near, far)]
    grads = [jnp.where(front, far, near), jnp.where(front, got2, none)]
    return [[jnp.where(here == 0, pair[0], pair[1]) for pair in (states, grads, logs)] for here in (seg, 1 - seg)]


def finish_kernel(place, turn, rate_ref, buf, u_rows, u_parts, v_parts, dx_in, ddt_in, db_in, dc_in, *refs):
    rate, tokens, width = rate_ref[...], place.tokens, place.width
    if turn == 0:
        (own, got), *refs = refs[:2], *refs[2:]
        (state, grad, through), rest = carried_in(own, got, lax.axis_index("ctx"), lax.axis_index("hi") == 0)
        for ref, value in zip(refs, rest):
            ref[...] = jnp.broadcast_to(value, ref.shape)
    else:
        state, grad, through = (ref[...] for ref in refs[:3])
        through = through[:1]
    *outs, out = refs[3:]
    s_hi, s_lo = split2(state)
    g_hi, g_lo = split2(grad)
    corner = jnp.sum(head_sums(fold(through * (grad * state)), width), axis=1, keepdims=True)
    chunks = [buf.at[i] for i in range(place.half)]
    b_all, c_all = cat([place.b(chunk) for chunk in chunks], 0), cat([place.c(chunk) for chunk in chunks], 0)
    b_grad = dot(cat([b_all, b_all], 1), cat([g_hi, g_lo], 0))
    c_state = dot(cat([c_all, c_all], 1), cat([s_hi, s_lo], 0))
    v_hi, v_lo = v_parts[0], v_parts[1]
    db = head_products((u_parts[0], u_parts[1]), (g_hi, g_lo))
    dc = head_products((v_hi, v_lo), (s_hi, s_lo))
    ins = []
    for i, chunk in enumerate(chunks):
        rows = slice(i * tokens, (i + 1) * tokens)
        extra = widen(columns(u_rows[i]), 0, width) * b_grad[rows]
        dx = (dx_in[i] + extra).astype(BF16)
        for block in range(place.blocks):
            out[i, block * tokens : (block + 1) * tokens, :] = dx[:, block * LANES : (block + 1) * LANES]
        ins.append(extra * cat(place.x(chunk), 1).astype(F32))
        first = place.blocks * tokens
        out[i, first : first + tokens, :] = (db_in[i] + db[rows]).astype(BF16)
        out[i, first + tokens : first + 2 * tokens, :] = (dc_in[i] + dc[rows]).astype(BF16)
    ins = head_sums(cat(ins, 0), width)
    laters = head_sums((v_hi.astype(F32) + v_lo.astype(F32)) * c_state, width)
    ins, laters = ([sums[:, i * tokens : (i + 1) * tokens] for i in range(place.half)] for sums in (ins, laters))
    over = cumulate(cat([one - other for one, other in zip(ins, laters)], 0), True)
    rest = corner
    for later in laters:
        rest = rest + jnp.sum(later, axis=1, keepdims=True)
    for i, chunk in enumerate(chunks):
        dlog = rest + over[i * ROWS : (i + 1) * ROWS]
        rest = rest + jnp.sum(ins[i] - laters[i], axis=1, keepdims=True)
        dt = place.dt(chunk)
        ddt = ddt_in[i] + ins[i] / jnp.where(dt > 0.0, dt, 1.0) + rate * dlog
        out[i, place.rows_out - TILE :, :] = cat([ddt, jnp.zeros_like(ddt)], 0).astype(BF16)
    for k, target in enumerate(outs):
        lo = lax.axis_index("lo") ^ k
        for at in range(0, place.rows_out, tokens):
            part = slice(at, min(at + tokens, place.rows_out))
            target[part] = out[lo, part]


def on_device(x_seq, dy_seq, dt_seq, a_log, b_seq, c_seq):
    tokens = x_seq.shape[0]
    half = lax.axis_size("lo")
    count = 2 * half
    heads = HEADS // count
    copies = count // GROUPS
    place = Place(tokens, half, heads * HEAD_DIM // LANES)
    width = place.width

    def after(value, *others):
        return lax.optimization_barrier((value, *others))[0]

    def swap(blocks, order):
        got, under_way = {0: blocks[0]}, []
        for k in order:
            turn = (k % half) * 2 + k // half
            block = blocks[k]
            if len(under_way) >= IN_FLIGHT:
                block = after(block, under_way[-IN_FLIGHT])
            got[k] = lax.ppermute(block, ("lo", "ctx"), [(i, i ^ turn) for i in range(count)])
            under_way.append(got[k])
        return [got[k] for k in range(count)]

    rates = -jnp.exp(lax.dynamic_slice_in_dim(a_log, lax.axis_index(("ctx", "lo")) * heads, heads))
    rate = jnp.broadcast_to(jnp.pad(rates, (0, ROWS - heads))[:, None], (ROWS, LANES))

    def f32(*shape):
        return jax.ShapeDtypeStruct(shape, F32)

    def bf16(*shape):
        return jax.ShapeDtypeStruct(shape, BF16)

    hbm, vmem = pl.BlockSpec(memory_space=pltpu.HBM), pl.BlockSpec(memory_space=pltpu.VMEM)
    params = pltpu.CompilerParams(vmem_limit_bytes=24 * 1024 * 1024)
    spaced = pltpu.VMEM((tokens * GROUPS + GROUPS, STATE), F32)
    wides = [spaced, spaced, pltpu.VMEM((HEADS, tokens), F32)]
    seqs = (b_seq, c_seq, dt_seq.T, x_seq, dy_seq)
    by_partner = [pltpu.VMEM((count, tokens, width), BF16)]

    sent = pl.pallas_call(
        functools.partial(pack_kernel, place, count, copies),
        in_specs=[hbm] * 5,
        out_specs=[hbm] * count,
        out_shape=[bf16(place.rows_in, LANES)] * count,
        scratch_shapes=[pltpu.VMEM(seq.shape, BF16) for seq in seqs[:3]]
        + wides
        + by_partner * 2
        + [pltpu.VMEM((count, place.rows_in, LANES), BF16), pltpu.SemaphoreType.DMA((3 + 2 * count,)), pltpu.SemaphoreType.DMA((count,))],
        compiler_params=pltpu.CompilerParams(vmem_limit_bytes=58 * 1024 * 1024),
        name="pack",
    )(*seqs)
    arrived = swap(sent, [*range(half, count), *range(1, half)])

    owned, coded = (2 * STATE + 2 * ROWS, width), (3 * STATE + TILE, width)
    data_shapes = [bf16(half, place.rows_in, LANES), f32(half, ROWS, tokens)] + [bf16(2, half * tokens, width)] * 2
    carry_shapes = [f32(STATE, width), f32(STATE, width), f32(ROWS, width)]

    def totals(turn, blocks, others, shapes):
        return pl.pallas_call(
            functools.partial(totals_kernel, place, turn),
            in_specs=[vmem] * (1 + half + len(others)),
            out_specs=[vmem] * (4 + len(shapes)),
            out_shape=data_shapes + shapes,
            compiler_params=params,
            name="totals",
        )(rate, *blocks, *others)

    *data1, other_s, other_g, other_log = totals(1, arrived[half:], [], carry_shapes)
    *data0, own, send = totals(0, arrived[:half], [other_s, other_g, other_log], [f32(*owned), bf16(*coded)])
    got = lax.ppermute(send, "hi", [(0, 1), (1, 0)])

    within = [f32(half, tokens, width), f32(half, ROWS, tokens), f32(half, tokens, STATE), f32(half, tokens, STATE)]
    parts = pl.pallas_call(
        functools.partial(middle_kernel, place),
        in_specs=[vmem] * 3,
        out_specs=[vmem] * 8,
        out_shape=within * 2,
        compiler_params=params,
        cost_estimate=pl.CostEstimate(flops=6_000_000_000, bytes_accessed=20_000_000, transcendentals=2_000_000),
        name="middle",
    )(rate, data0[0], data1[0])

    def finish(turn, data, parts, others, shapes):
        return pl.pallas_call(
            functools.partial(finish_kernel, place, turn),
            in_specs=[vmem] * (9 + len(others)),
            out_specs=[vmem] * (half + len(shapes)),
            out_shape=shapes + [bf16(place.rows_out, LANES)] * half,
            scratch_shapes=[pltpu.VMEM((half, place.rows_out, LANES), BF16)],
            compiler_params=params,
            name="finish",
        )(rate, *data, *parts, *others)

    state, grad, through, *outs0 = finish(0, data0, parts[:4], [own, got], carry_shapes)
    outs1 = finish(1, data1, parts[4:], [state, grad, through], [])
    homes = swap([*outs0, *outs1], range(1, count))

    dx, ddt, db, dc = pl.pallas_call(
        functools.partial(unpack_kernel, place, count, copies),
        in_specs=[vmem] * count,
        out_specs=[hbm] * 4,
        out_shape=[bf16(*x_seq.shape), bf16(HEADS, tokens), bf16(*b_seq.shape), bf16(*c_seq.shape)],
        scratch_shapes=by_partner
        + [pltpu.VMEM(b_seq.shape, BF16), pltpu.VMEM(c_seq.shape, BF16), pltpu.VMEM((HEADS, tokens), BF16)]
        + wides
        + [pltpu.SemaphoreType.DMA((count + 3,))],
        compiler_params=params,
        name="unpack",
    )(*homes)
    return dx, ddt.T, db, dc


def solution(mesh):
    parts, head, ctx = (mesh.shape[name] for name in ("grp", "head", "ctx"))
    split = jax.sharding.Mesh(mesh.devices.reshape(parts, 2, head // 2, ctx), ("grp", "hi", "lo", "ctx"))
    spec = P(("grp", "ctx", "hi", "lo"))
    return jax.shard_map(
        on_device,
        mesh=split,
        in_specs=(spec, spec, spec, P(), spec, spec),
        out_specs=(spec, spec, spec, spec),
        check_vma=False,
    )
```

```python
import functools
from typing import NamedTuple

import jax
import jax.numpy as jnp
from jax import lax
from jax.experimental import pallas as pl
from jax.experimental.pallas import tpu as pltpu
from jax.sharding import PartitionSpec as P

HEADS = 64
HEAD_DIM = 64
STATE = 128
GROUPS = 8
LANES = 128
ROWS = 8
TILE = 16
LOG2E = 1.4426950408889634
CODE_SPAN = 250.0
IN_FLIGHT = 5
F32 = jnp.float32
BF16 = jnp.bfloat16


def split2(value):
    hi = value.astype(BF16)
    return hi, (value - hi.astype(F32)).astype(BF16)


def split3(value):
    hi = value.astype(BF16)
    rest = value - hi.astype(F32)
    mid = rest.astype(BF16)
    return hi, mid, (rest - mid.astype(F32)).astype(BF16)


def dot(a, b):
    return lax.dot_general(a, b, (((1,), (0,)), ((), ())), preferred_element_type=F32)


def dot_nt(a, b):
    return lax.dot_general(a, b, (((1,), (1,)), ((), ())), preferred_element_type=F32)


def dot_tn(a, b):
    return lax.dot_general(a, b, (((0,), (0,)), ((), ())), preferred_element_type=F32)


def cat(parts, axis):
    return jnp.concatenate(parts, axis=axis)


def upper(size, strict):
    row = lax.broadcasted_iota(jnp.int32, (size, size), 0)
    col = lax.broadcasted_iota(jnp.int32, (size, size), 1)
    return row < col if strict else row <= col


def cumulate(rows, strict):
    tri = upper(rows.shape[1], strict).astype(F32).astype(BF16)
    sums = dot(cat([part.astype(F32) for part in split3(rows)], 0).astype(BF16), tri)
    size = rows.shape[0]
    return sums[:size] + sums[size : 2 * size] + sums[2 * size :]


def spread_matrix(terms, width):
    row = lax.broadcasted_iota(jnp.int32, (terms * ROWS, width), 0)
    col = lax.broadcasted_iota(jnp.int32, (terms * ROWS, width), 1)
    return (row % ROWS == col // HEAD_DIM).astype(F32).astype(BF16)


def spread_rows(rows, width):
    hi, lo = split2(rows)
    terms = cat([hi.astype(F32), lo.astype(F32)], 0).astype(BF16)
    return dot_tn(terms, spread_matrix(2, width))


def columns(rows):
    return jnp.transpose(cat([rows, jnp.zeros((LANES - rows.shape[0], rows.shape[1]), F32)], 0))


def widen(cols, first, width):
    lane = lax.broadcasted_iota(jnp.int32, cols.shape, 1)
    heads = [first + lane // HEAD_DIM + 2 * block for block in range(width // LANES)]
    return cat([jnp.take_along_axis(cols, head, axis=1) for head in heads], 1)


def head_products(values, factors):
    rows = values[0].shape[0]
    both = dot_nt(cat(list(values), 0), cat(list(factors), 0))
    size = factors[0].shape[0]
    return (both[:rows, :size] + (both[:rows, size:] + both[rows:, :size])) + both[rows:, size:]


class Place(NamedTuple):
    tokens: int
    half: int
    blocks: int

    @property
    def width(self):
        return self.blocks * LANES

    @property
    def b_row(self):
        return 2 * self.blocks * self.tokens

    @property
    def dt_row(self):
        return self.b_row + 2 * self.tokens

    @property
    def rows_in(self):
        return self.dt_row + TILE

    @property
    def rows_out(self):
        return (self.blocks + 2) * self.tokens + TILE

    def x(self, buf):
        return [buf[i * self.tokens : (i + 1) * self.tokens, :] for i in range(self.blocks)]

    def dy(self, buf):
        return [buf[i * self.tokens : (i + 1) * self.tokens, :] for i in range(self.blocks, 2 * self.blocks)]

    def b(self, buf):
        return buf[self.b_row : self.b_row + self.tokens, :]

    def c(self, buf):
        return buf[self.b_row + self.tokens : self.b_row + 2 * self.tokens, :]

    def dt(self, buf):
        return buf[self.dt_row : self.dt_row + TILE, :].astype(F32)[:ROWS]


def partner(place, k):
    return (lax.axis_index("ctx") ^ (k // place.half)) * place.half + (lax.axis_index("lo") ^ (k % place.half))


def pack_kernel(place, count, copies, *refs):
    (b_hbm, c_hbm, dt_hbm, x_hbm, dy_hbm), outs, refs = refs[:5], refs[5 : 5 + count], refs[5 + count :]
    b_ref, c_ref, dt_ref, b_wide, c_wide, dt_wide, x_ref, dy_ref, ready, sems, out_sems = refs
    tokens, blocks, width = place.tokens, place.blocks, place.width
    heads = HEADS // count
    dests = [partner(place, k) for k in range(count)]
    loads = [(b_hbm, b_ref), (c_hbm, c_ref), (dt_hbm, dt_ref)]
    for k, dest in enumerate(dests):
        columns = pl.ds(pl.multiple_of(dest * width, LANES), width)
        loads += [(x_hbm.at[:, columns], x_ref.at[k]), (dy_hbm.at[:, columns], dy_ref.at[k])]
    loads = [pltpu.make_async_copy(source, target, sems.at[i]) for i, (source, target) in enumerate(loads)]
    for load in loads:
        load.start()
    for load in loads[:3]:
        load.wait()
    every = tokens * GROUPS
    b_wide[:every] = b_ref[...].astype(F32).reshape(every, STATE)
    c_wide[:every] = c_ref[...].astype(F32).reshape(every, STATE)
    dt_wide[...] = dt_ref[...].astype(F32)
    stores = []
    for k, (dest, out) in enumerate(zip(dests, outs)):
        mine = pl.ds(lax.div(dest, copies), tokens, stride=GROUPS)
        ready[k, place.b_row : place.b_row + tokens] = b_wide[mine, :].astype(BF16)
        ready[k, place.b_row + tokens : place.dt_row] = c_wide[mine, :].astype(BF16)
        dt = dt_wide[pl.ds(dest * heads, heads), :]
        ready[k, place.dt_row :] = cat([dt, jnp.zeros((TILE - heads, tokens), F32)], 0).astype(BF16)
        for load in loads[3 + 2 * k : 5 + 2 * k]:
            load.wait()
        for part, ref in enumerate((x_ref, dy_ref)):
            for i in range(blocks):
                row = (part * blocks + i) * tokens
                ready[k, row : row + tokens] = ref[k, :, i * LANES : (i + 1) * LANES]
        stores.append(pltpu.make_async_copy(ready.at[k], out, out_sems.at[k]))
        stores[-1].start()
    for store in stores:
        store.wait()


def unpack_kernel(place, count, copies, *refs):
    homes, refs = refs[:count], refs[count:]
    dx_hbm, ddt_hbm, db_hbm, dc_hbm, dx_ref, db_ref, dc_ref, ddt_ref, db_wide, dc_wide, ddt_wide, sems = refs
    tokens, blocks, width = place.tokens, place.blocks, place.width
    heads = HEADS // count
    first = blocks * tokens
    moves = []

    def move(source, target):
        moves.append(pltpu.make_async_copy(source, target, sems.at[len(moves)]))
        moves[-1].start()

    if copies > 1:
        db_wide[...] = jnp.zeros_like(db_wide)
        dc_wide[...] = jnp.zeros_like(dc_wide)
    for k, home in enumerate(homes):
        source = partner(place, k)
        mine = pl.ds(lax.div(source, copies), tokens, stride=GROUPS)
        for to, at in ((db_wide, first), (dc_wide, first + tokens)):
            part = home[at : at + tokens, :].astype(F32)
            to[mine, :] = part if copies == 1 else to[mine, :] + part
        ddt_wide[pl.ds(source * heads, heads), :] = home[place.rows_out - TILE :, :].astype(F32)[:heads]
        for i in range(blocks):
            dx_ref[k, :, i * LANES : (i + 1) * LANES] = home[i * tokens : (i + 1) * tokens, :]
        move(dx_ref.at[k], dx_hbm.at[:, pl.ds(pl.multiple_of(source * width, LANES), width)])
    every = tokens * GROUPS
    db_ref[...] = db_wide[:every].reshape(db_ref.shape).astype(BF16)
    dc_ref[...] = dc_wide[:every].reshape(dc_ref.shape).astype(BF16)
    ddt_ref[...] = ddt_wide[...].astype(BF16)
    for source, target in ((db_ref, db_hbm), (dc_ref, dc_hbm), (ddt_ref, ddt_hbm)):
        move(source, target)
    for one in moves:
        one.wait()


def segment_decays(place, bufs, rate):
    dts = [place.dt(buf) for buf in bufs]
    cums = cumulate(cat([dt * rate for dt in dts], 0), False)
    cums = [cums[i * ROWS : (i + 1) * ROWS] for i in range(len(bufs))]
    starts, start = [], jnp.zeros((ROWS, 1), F32)
    for cum in cums:
        starts.append(start + cum)
        start = start + cum[:, place.tokens - 1 :]
    return dts, [start - one for one in starts], starts


def encode(value, scale):
    size = jnp.exp2(jnp.abs(value) * (CODE_SPAN / scale) - CODE_SPAN / 2)
    return jnp.where(value < 0.0, -size, size).astype(BF16)


def decode(code, scale):
    code = code.astype(F32)
    size = (jnp.log(jnp.abs(code)) * LOG2E + CODE_SPAN / 2) * (scale / CODE_SPAN)
    return jnp.where(code < 0.0, -size, size)


def encode_into(send_ref, value, logs):
    top = jnp.maximum(jnp.max(jnp.abs(value), axis=0, keepdims=True), 1e-30)
    scale = (top * 1.01).astype(BF16).astype(F32)
    send_ref[:STATE] = encode(value, scale)
    notes = [scale] + [part.astype(F32) for log in logs for part in split2(log[:1])]
    notes += [jnp.zeros((TILE - len(notes), value.shape[1]), F32)]
    send_ref[STATE:] = cat(notes, 0).astype(BF16)


def totals_kernel(place, turn, rate_ref, *refs):
    blocks, refs = refs[: place.half], refs[place.half :]
    others, refs = ([], refs) if turn else (refs[:3], refs[3:])
    buf, u_rows, u_parts, v_parts, *refs = refs
    width, tokens = place.width, place.tokens
    for k, block in enumerate(blocks):
        lo = lax.axis_index("lo") ^ k
        for at in range(0, place.rows_in, tokens):
            rows = slice(at, min(at + tokens, place.rows_in))
            buf[lo, rows] = block[rows]
    chunks = [buf.at[i] for i in range(place.half)]
    dts, ends, starts = segment_decays(place, chunks, rate_ref[...])
    for i, chunk in enumerate(chunks):
        u_rows[i] = dts[i] * jnp.exp(ends[i])
        rows = slice(i * tokens, (i + 1) * tokens)
        hi, lo = split2(spread_rows(u_rows[i], width) * cat(place.x(chunk), 1).astype(F32))
        u_parts[0, rows], u_parts[1, rows] = hi, lo
        start_wide = spread_rows(jnp.exp(starts[i]), width)
        hi, lo = split2(start_wide * cat(place.dy(chunk), 1).astype(F32))
        v_parts[0, rows], v_parts[1, rows] = hi, lo
    b_turned = jnp.transpose(cat([place.b(chunk) for chunk in chunks], 0).astype(F32)).astype(BF16)
    c_turned = jnp.transpose(cat([place.c(chunk) for chunk in chunks], 0).astype(F32)).astype(BF16)
    total_s = dot(b_turned, u_parts[0]) + dot(b_turned, u_parts[1])
    total_g = dot(c_turned, v_parts[0]) + dot(c_turned, v_parts[1])
    log = jnp.broadcast_to(start_wide[tokens - 1 :, :], (ROWS, width))
    front, early = lax.axis_index("hi") == 0, lax.axis_index("ctx") == 0
    middle = jnp.where(front, total_s, total_g)
    if turn:
        encode_into(refs[3], jnp.where(early, total_g, total_s), [])
        encode_into(refs[4], middle, [])
        for ref, value in zip(refs, (total_s, total_g, log)):
            ref[...] = value
        return
    own_ref, send_ref, middle_ref = refs
    other_s, other_g, other_log = (ref[...] for ref in others)
    logs = [jnp.where(early, log, other_log), jnp.where(early, other_log, log)]
    encode_into(send_ref, jnp.where(early, total_s, total_g), logs)
    encode_into(middle_ref, middle, [])
    own_ref[:STATE] = jnp.where(early, total_s, other_s)
    own_ref[STATE : 2 * STATE] = jnp.where(early, other_g, total_g)
    own_ref[2 * STATE :] = cat(logs, 0)


def head_sums(values, width):
    hi, lo = split2(values)
    picker = spread_matrix(2, width)
    return (dot_nt(picker, hi) + dot_nt(picker, lo))[:ROWS]


def fold(value):
    total = value[:ROWS]
    for i in range(1, value.shape[0] // ROWS):
        total = total + value[i * ROWS : (i + 1) * ROWS]
    return total


def middle_kernel(place, rate_ref, buf, dx_ref, ddt_ref, db_ref, dc_ref):
    rate, tokens, width = rate_ref[...], place.tokens, place.width
    chunks = [buf.at[i] for i in range(place.half)]
    dts = [place.dt(chunk) for chunk in chunks]
    cums = cumulate(cat([dt * rate for dt in dts], 0), False)
    cums = [cums[i * ROWS : (i + 1) * ROWS] for i in range(len(chunks))]
    ends = [cum[:, tokens - 1 :] for cum in cums]
    starts = [jnp.exp(cum) for cum in cums]

    us, vs, end_wides, adds_s, adds_g, through = [], [], [], [], [], []
    for i, chunk in enumerate(chunks):
        cols = columns(cat([dts[i] * jnp.exp(ends[i] - cums[i]), starts[i]], 0))
        end_wide, start_wide = widen(cols, 0, width), widen(cols, ROWS, width)
        u, v = split2(end_wide * cat(place.x(chunk), 1).astype(F32)), split2(start_wide * cat(place.dy(chunk), 1).astype(F32))
        b_here, c_here = place.b(chunk), place.c(chunk)
        adds_s.append(dot_tn(cat([b_here, b_here], 0), cat(list(u), 0)))
        adds_g.append(dot_tn(cat([c_here, c_here], 0), cat(list(v), 0)))
        through.append(start_wide[tokens - 1 :, :])
        us.append(u)
        vs.append(v)
        end_wides.append(end_wide)
    states, grads = [jnp.zeros((STATE, width), F32)], [jnp.zeros((STATE, width), F32)]
    for i in range(len(chunks) - 1):
        states.append(through[i] * states[-1] + adds_s[i])
        grads.append(through[-1 - i] * grads[-1] + adds_g[-1 - i])
    grads = grads[::-1]
    corners = head_sums(cat([fold(through[i] * (states[i] * grads[i])) for i in range(len(chunks))], 0), width)

    mask = upper(tokens, False)
    left = lax.broadcasted_iota(jnp.int32, (tokens, LANES), 1) < HEAD_DIM
    left, right = left.astype(F32).astype(BF16), (~left).astype(F32).astype(BF16)
    for i, chunk in enumerate(chunks):
        b_here, c_here = place.b(chunk), place.c(chunk)
        cum = cums[i] * LOG2E
        cols = jnp.transpose(cum - jnp.log(jnp.where(dts[i] > 0.0, dts[i], 1.0)) * LOG2E)
        k_two = dot_nt(b_here, c_here)
        s_hi, s_lo = split2(states[i])
        g_hi, g_lo = split2(grads[i])
        b_grad = end_wides[i] * dot(cat([b_here, b_here], 1), cat([g_hi, g_lo], 0))
        c_state = dot(cat([c_here, c_here], 1), cat([s_hi, s_lo], 0))
        one_sum = jnp.zeros((tokens, tokens), F32)
        rows, alongs = [], []
        for block, (x_here, dy_here) in enumerate(zip(place.x(chunk), place.dy(chunk))):
            lanes = slice(block * LANES, (block + 1) * LANES)
            sides = cat([dy_here * left, dy_here * right], 0)
            k_one = dot_nt(x_here, sides)
            tops, bottoms = [], []
            for side in range(2):
                head = 2 * block + side
                gap = jnp.where(mask, cum[head : head + 1, :] - cols[:, head : head + 1], -1e30)
                decay = jnp.exp2(gap)
                a_one = decay * k_one[:, side * tokens : (side + 1) * tokens]
                a_two = decay * k_two
                one_sum = one_sum + a_one
                rows.append(jnp.sum(a_one * k_two, axis=0, keepdims=True))
                hi_two, lo_two = split2(a_two)
                tops.append(hi_two)
                bottoms.append(lo_two)
            both = dot(cat([cat(tops, 1), cat(bottoms, 1)], 0), sides)
            dx = both[:tokens] + both[tokens:] + b_grad[:, lanes]
            dx_ref[i, :, lanes] = dx
            alongs.append(dx * x_here.astype(F32))
        if len(rows) < ROWS:
            rows.append(jnp.zeros((ROWS - len(rows), tokens), F32))
        db = dot(cat(list(split2(one_sum)), 1), cat([c_here, c_here], 0))
        dc = dot(cat(list(split2(jnp.transpose(one_sum))), 1), cat([b_here, b_here], 0))
        db_ref[i] = db + head_products(us[i], (g_hi, g_lo))
        dc_ref[i] = dc + head_products(vs[i], (s_hi, s_lo))
        sums = head_sums(cat([cat(alongs, 1), cat(place.dy(chunk), 1).astype(F32) * c_state], 0), width)
        along = sums[:, :tokens]
        later = starts[i] * sums[:, tokens:]
        corner = jnp.sum(corners[:, i * ROWS : (i + 1) * ROWS], axis=1, keepdims=True)
        flow = along - cat(rows, 0) - later
        dlog = corner + jnp.sum(later, axis=1, keepdims=True) + cumulate(flow, True)
        ddt_ref[i] = along / jnp.where(dts[i] > 0.0, dts[i], 1.0) + rate * dlog


def carried_in(own, first, first_middle, second, second_middle, seg, front):
    sent0, sent2, logs = own[:STATE], own[STATE : 2 * STATE], (own[2 * STATE : 2 * STATE + 1], own[2 * STATE + ROWS : 2 * STATE + ROWS + 1])
    early = lax.axis_index("ctx") == 0
    crossed, late = (decode(part[:STATE], part[STATE:].astype(F32)[:1]) for part in (first, second))
    got0, got2 = jnp.where(early, late, crossed), jnp.where(early, crossed, late)
    middle = jnp.where(front == early, second_middle[...].astype(F32), first_middle[...].astype(F32))
    got1 = decode(middle[:STATE], middle[STATE : STATE + 1])
    notes = second[STATE:].astype(F32)
    mine = jnp.where(front, logs[1], logs[0])
    other = jnp.where(front, notes[1:2] + notes[2:3], notes[3:4] + notes[4:5])
    far = got1 + other * (jnp.where(front, sent2, sent0) + mine * jnp.where(front, got2, got0))
    near = jnp.where(front, got0, got2) + other * jnp.where(front, sent0, sent2)
    none = jnp.zeros_like(far)
    states = [jnp.where(front, none, got0), jnp.where(front, near, far)]
    grads = [jnp.where(front, far, near), jnp.where(front, got2, none)]
    return [[jnp.where(here == 0, pair[0], pair[1]) for pair in (states, grads, logs)] for here in (seg, 1 - seg)]


def finish_kernel(place, turn, rate_ref, buf, u_rows, u_parts, v_parts, dx_in, ddt_in, db_in, dc_in, *refs):
    rate, tokens, width = rate_ref[...], place.tokens, place.width
    if turn == 0:
        got, refs = refs[:5], refs[5:]
        (state, grad, through), rest = carried_in(*got, lax.axis_index("ctx"), lax.axis_index("hi") == 0)
        for ref, value in zip(refs, rest):
            ref[...] = jnp.broadcast_to(value, ref.shape)
    else:
        state, grad, through = (ref[...] for ref in refs[:3])
        through = through[:1]
    *outs, out = refs[3:]
    s_hi, s_lo = split2(state)
    g_hi, g_lo = split2(grad)
    corner = jnp.sum(head_sums(fold(through * (grad * state)), width), axis=1, keepdims=True)
    chunks = [buf.at[i] for i in range(place.half)]
    b_all, c_all = cat([place.b(chunk) for chunk in chunks], 0), cat([place.c(chunk) for chunk in chunks], 0)
    b_grad = dot(cat([b_all, b_all], 1), cat([g_hi, g_lo], 0))
    c_state = dot(cat([c_all, c_all], 1), cat([s_hi, s_lo], 0))
    v_hi, v_lo = v_parts[0], v_parts[1]
    db = head_products((u_parts[0], u_parts[1]), (g_hi, g_lo))
    dc = head_products((v_hi, v_lo), (s_hi, s_lo))
    ins = []
    for i, chunk in enumerate(chunks):
        rows = slice(i * tokens, (i + 1) * tokens)
        extra = widen(columns(u_rows[i]), 0, width) * b_grad[rows]
        dx = (dx_in[i] + extra).astype(BF16)
        for block in range(place.blocks):
            out[i, block * tokens : (block + 1) * tokens, :] = dx[:, block * LANES : (block + 1) * LANES]
        ins.append(extra * cat(place.x(chunk), 1).astype(F32))
        first = place.blocks * tokens
        out[i, first : first + tokens, :] = (db_in[i] + db[rows]).astype(BF16)
        out[i, first + tokens : first + 2 * tokens, :] = (dc_in[i] + dc[rows]).astype(BF16)
    ins = head_sums(cat(ins, 0), width)
    laters = head_sums((v_hi.astype(F32) + v_lo.astype(F32)) * c_state, width)
    ins, laters = ([sums[:, i * tokens : (i + 1) * tokens] for i in range(place.half)] for sums in (ins, laters))
    over = cumulate(cat([one - other for one, other in zip(ins, laters)], 0), True)
    rest = corner
    for later in laters:
        rest = rest + jnp.sum(later, axis=1, keepdims=True)
    for i, chunk in enumerate(chunks):
        dlog = rest + over[i * ROWS : (i + 1) * ROWS]
        rest = rest + jnp.sum(ins[i] - laters[i], axis=1, keepdims=True)
        dt = place.dt(chunk)
        ddt = ddt_in[i] + ins[i] / jnp.where(dt > 0.0, dt, 1.0) + rate * dlog
        out[i, place.rows_out - TILE :, :] = cat([ddt, jnp.zeros_like(ddt)], 0).astype(BF16)
    for k, target in enumerate(outs):
        lo = lax.axis_index("lo") ^ k
        for at in range(0, place.rows_out, tokens):
            part = slice(at, min(at + tokens, place.rows_out))
            target[part] = out[lo, part]


def on_device(x_seq, dy_seq, dt_seq, a_log, b_seq, c_seq):
    tokens = x_seq.shape[0]
    half = lax.axis_size("lo")
    count = 2 * half
    heads = HEADS // count
    copies = count // GROUPS
    place = Place(tokens, half, heads * HEAD_DIM // LANES)
    width = place.width

    def after(value, *others):
        return lax.optimization_barrier((value, *others))[0]

    def swap(blocks, order):
        got, under_way = {0: blocks[0]}, []
        for k in order:
            turn = (k % half) * 2 + k // half
            block = blocks[k]
            if len(under_way) >= IN_FLIGHT:
                block = after(block, under_way[-IN_FLIGHT])
            got[k] = lax.ppermute(block, ("lo", "ctx"), [(i, i ^ turn) for i in range(count)])
            under_way.append(got[k])
        return [got[k] for k in range(count)]

    rates = -jnp.exp(lax.dynamic_slice_in_dim(a_log, lax.axis_index(("ctx", "lo")) * heads, heads))
    rate = jnp.broadcast_to(jnp.pad(rates, (0, ROWS - heads))[:, None], (ROWS, LANES))

    def f32(*shape):
        return jax.ShapeDtypeStruct(shape, F32)

    def bf16(*shape):
        return jax.ShapeDtypeStruct(shape, BF16)

    hbm, vmem = pl.BlockSpec(memory_space=pltpu.HBM), pl.BlockSpec(memory_space=pltpu.VMEM)
    params = pltpu.CompilerParams(vmem_limit_bytes=24 * 1024 * 1024)
    spaced = pltpu.VMEM((tokens * GROUPS + GROUPS, STATE), F32)
    wides = [spaced, spaced, pltpu.VMEM((HEADS, tokens), F32)]
    seqs = (b_seq, c_seq, dt_seq.T, x_seq, dy_seq)
    by_partner = [pltpu.VMEM((count, tokens, width), BF16)]

    sent = pl.pallas_call(
        functools.partial(pack_kernel, place, count, copies),
        in_specs=[hbm] * 5,
        out_specs=[hbm] * count,
        out_shape=[bf16(place.rows_in, LANES)] * count,
        scratch_shapes=[pltpu.VMEM(seq.shape, BF16) for seq in seqs[:3]]
        + wides
        + by_partner * 2
        + [pltpu.VMEM((count, place.rows_in, LANES), BF16), pltpu.SemaphoreType.DMA((3 + 2 * count,)), pltpu.SemaphoreType.DMA((count,))],
        compiler_params=pltpu.CompilerParams(vmem_limit_bytes=58 * 1024 * 1024),
        name="pack",
    )(*seqs)
    arrived = swap(sent, [*range(half + 1, count), half, *range(1, half)])

    owned, coded = (2 * STATE + 2 * ROWS, width), (STATE + TILE, width)
    data_shapes = [bf16(half, place.rows_in, LANES), f32(half, ROWS, tokens)] + [bf16(2, half * tokens, width)] * 2
    carry_shapes = [f32(STATE, width), f32(STATE, width), f32(ROWS, width)]

    def totals(turn, blocks, others, shapes):
        return pl.pallas_call(
            functools.partial(totals_kernel, place, turn),
            in_specs=[vmem] * (1 + half + len(others)),
            out_specs=[vmem] * (4 + len(shapes)),
            out_shape=data_shapes + shapes,
            compiler_params=params,
            name="totals",
        )(rate, *blocks, *others)

    def cross(send, middle, early):
        pairs = [(0, 2), (3, 1)] if early else [(1, 3), (2, 0)]
        return lax.ppermute(send, "hi", [(0, 1), (1, 0)]), lax.ppermute(middle, ("hi", "ctx"), pairs)

    sends = [bf16(*coded)] * 2
    *data1, other_s, other_g, other_log, send, middle_send = totals(1, arrived[half:], [], carry_shapes + sends)
    first_send = send
    first, first_middle = cross(send, middle_send, True)
    *data0, own, send, middle_send = totals(0, [after(block, first_send) for block in arrived[:half]], [other_s, other_g, other_log], [f32(*owned)] + sends)
    second, second_middle = cross(send, middle_send, False)

    within = [f32(half, tokens, width), f32(half, ROWS, tokens), f32(half, tokens, STATE), f32(half, tokens, STATE)]
    def middle(data):
        return pl.pallas_call(
            functools.partial(middle_kernel, place),
            in_specs=[vmem] * 2,
            out_specs=[vmem] * 4,
            out_shape=within,
            compiler_params=params,
            cost_estimate=pl.CostEstimate(flops=3_000_000_000, bytes_accessed=10_000_000, transcendentals=1_000_000),
            name="middle",
        )(rate, data[0])

    def finish(turn, data, parts, others, shapes):
        return pl.pallas_call(
            functools.partial(finish_kernel, place, turn),
            in_specs=[vmem] * (9 + len(others)),
            out_specs=[vmem] * (half + len(shapes)),
            out_shape=shapes + [bf16(place.rows_out, LANES)] * half,
            scratch_shapes=[pltpu.VMEM((half, place.rows_out, LANES), BF16)],
            compiler_params=params,
            name="finish",
        )(rate, *data, *parts, *others)

    parts1, parts0 = middle(data1), middle(data0)
    second = after(second, parts1[0])
    state, grad, through, *outs0 = finish(0, data0, parts0, [own, first, first_middle, second, second_middle], carry_shapes)
    outs1 = finish(1, data1, parts1, [state, grad, through], [])
    homes = swap([*outs0, *outs1], [*range(1, half), *range(half + 1, count), half])

    dx, ddt, db, dc = pl.pallas_call(
        functools.partial(unpack_kernel, place, count, copies),
        in_specs=[vmem] * count,
        out_specs=[hbm] * 4,
        out_shape=[bf16(*x_seq.shape), bf16(HEADS, tokens), bf16(*b_seq.shape), bf16(*c_seq.shape)],
        scratch_shapes=by_partner
        + [pltpu.VMEM(b_seq.shape, BF16), pltpu.VMEM(c_seq.shape, BF16), pltpu.VMEM((HEADS, tokens), BF16)]
        + wides
        + [pltpu.SemaphoreType.DMA((count + 3,))],
        compiler_params=params,
        name="unpack",
    )(*homes)
    return dx, ddt.T, db, dc


def solution(mesh):
    parts, head, ctx = (mesh.shape[name] for name in ("grp", "head", "ctx"))
    split = jax.sharding.Mesh(mesh.devices.reshape(parts, 2, head // 2, ctx), ("grp", "hi", "lo", "ctx"))
    spec = P(("grp", "ctx", "hi", "lo"))
    return jax.shard_map(
        on_device,
        mesh=split,
        in_specs=(spec, spec, spec, P(), spec, spec),
        out_specs=(spec, spec, spec, spec),
        check_vma=False,
    )
```

```python
import functools
from typing import NamedTuple

import jax
import jax.numpy as jnp
from jax import lax
from jax.experimental import pallas as pl
from jax.experimental.pallas import tpu as pltpu
from jax.sharding import PartitionSpec as P

HEADS = 64
HEAD_DIM = 64
STATE = 128
GROUPS = 8
LANES = 128
ROWS = 8
TILE = 16
LOG2E = 1.4426950408889634
CODE_SPAN = 250.0
IN_FLIGHT = 5
F32 = jnp.float32
BF16 = jnp.bfloat16


def split2(value):
    hi = value.astype(BF16)
    return hi, (value - hi.astype(F32)).astype(BF16)


def split3(value):
    hi = value.astype(BF16)
    rest = value - hi.astype(F32)
    mid = rest.astype(BF16)
    return hi, mid, (rest - mid.astype(F32)).astype(BF16)


def dot(a, b):
    return lax.dot_general(a, b, (((1,), (0,)), ((), ())), preferred_element_type=F32)


def dot_nt(a, b):
    return lax.dot_general(a, b, (((1,), (1,)), ((), ())), preferred_element_type=F32)


def dot_tn(a, b):
    return lax.dot_general(a, b, (((0,), (0,)), ((), ())), preferred_element_type=F32)


def cat(parts, axis):
    return jnp.concatenate(parts, axis=axis)


def upper(size, strict):
    row = lax.broadcasted_iota(jnp.int32, (size, size), 0)
    col = lax.broadcasted_iota(jnp.int32, (size, size), 1)
    return row < col if strict else row <= col


def cumulate(rows, strict):
    tri = upper(rows.shape[1], strict).astype(F32).astype(BF16)
    sums = dot(cat([part.astype(F32) for part in split3(rows)], 0).astype(BF16), tri)
    size = rows.shape[0]
    return sums[:size] + sums[size : 2 * size] + sums[2 * size :]


def spread_matrix(terms, width):
    row = lax.broadcasted_iota(jnp.int32, (terms * ROWS, width), 0)
    col = lax.broadcasted_iota(jnp.int32, (terms * ROWS, width), 1)
    return (row % ROWS == col // HEAD_DIM).astype(F32).astype(BF16)


def spread_rows(rows, width):
    hi, lo = split2(rows)
    terms = cat([hi.astype(F32), lo.astype(F32)], 0).astype(BF16)
    return dot_tn(terms, spread_matrix(2, width))


def columns(rows):
    return jnp.transpose(cat([rows, jnp.zeros((LANES - rows.shape[0], rows.shape[1]), F32)], 0))


def widen(cols, first, width):
    lane = lax.broadcasted_iota(jnp.int32, cols.shape, 1)
    heads = [first + lane // HEAD_DIM + 2 * block for block in range(width // LANES)]
    return cat([jnp.take_along_axis(cols, head, axis=1) for head in heads], 1)


def head_products(values, factors):
    rows = values[0].shape[0]
    both = dot_nt(cat(list(values), 0), cat(list(factors), 0))
    size = factors[0].shape[0]
    return (both[:rows, :size] + (both[:rows, size:] + both[rows:, :size])) + both[rows:, size:]


class Place(NamedTuple):
    tokens: int
    half: int
    blocks: int

    @property
    def width(self):
        return self.blocks * LANES

    @property
    def b_row(self):
        return 2 * self.blocks * self.tokens

    @property
    def dt_row(self):
        return self.b_row + 2 * self.tokens

    @property
    def rows_in(self):
        return self.dt_row + TILE

    @property
    def rows_out(self):
        return (self.blocks + 2) * self.tokens + TILE

    def x(self, buf):
        return [buf[i * self.tokens : (i + 1) * self.tokens, :] for i in range(self.blocks)]

    def dy(self, buf):
        return [buf[i * self.tokens : (i + 1) * self.tokens, :] for i in range(self.blocks, 2 * self.blocks)]

    def b(self, buf):
        return buf[self.b_row : self.b_row + self.tokens, :]

    def c(self, buf):
        return buf[self.b_row + self.tokens : self.b_row + 2 * self.tokens, :]

    def dt(self, buf):
        return buf[self.dt_row : self.dt_row + TILE, :].astype(F32)[:ROWS]


def partner(place, k):
    return (lax.axis_index("ctx") ^ (k // place.half)) * place.half + (lax.axis_index("lo") ^ (k % place.half))


def pack_kernel(place, count, copies, *refs):
    (b_hbm, c_hbm, dt_hbm, x_hbm, dy_hbm), outs, refs = refs[:5], refs[5 : 5 + count], refs[5 + count :]
    b_ref, c_ref, dt_ref, b_wide, c_wide, dt_wide, x_ref, dy_ref, ready, sems, out_sems = refs
    tokens, blocks, width = place.tokens, place.blocks, place.width
    heads = HEADS // count
    dests = [partner(place, k) for k in range(count)]
    loads = [(b_hbm, b_ref), (c_hbm, c_ref), (dt_hbm, dt_ref)]
    for k, dest in enumerate(dests):
        columns = pl.ds(pl.multiple_of(dest * width, LANES), width)
        loads += [(x_hbm.at[:, columns], x_ref.at[k]), (dy_hbm.at[:, columns], dy_ref.at[k])]
    loads = [pltpu.make_async_copy(source, target, sems.at[i]) for i, (source, target) in enumerate(loads)]
    for load in loads:
        load.start()
    for load in loads[:3]:
        load.wait()
    every = tokens * GROUPS
    b_wide[:every] = b_ref[...].astype(F32).reshape(every, STATE)
    c_wide[:every] = c_ref[...].astype(F32).reshape(every, STATE)
    dt_wide[...] = dt_ref[...].astype(F32)
    stores = []
    for k, (dest, out) in enumerate(zip(dests, outs)):
        mine = pl.ds(lax.div(dest, copies), tokens, stride=GROUPS)
        ready[k, place.b_row : place.b_row + tokens] = b_wide[mine, :].astype(BF16)
        ready[k, place.b_row + tokens : place.dt_row] = c_wide[mine, :].astype(BF16)
        dt = dt_wide[pl.ds(dest * heads, heads), :]
        ready[k, place.dt_row :] = cat([dt, jnp.zeros((TILE - heads, tokens), F32)], 0).astype(BF16)
        for load in loads[3 + 2 * k : 5 + 2 * k]:
            load.wait()
        for part, ref in enumerate((x_ref, dy_ref)):
            for i in range(blocks):
                row = (part * blocks + i) * tokens
                ready[k, row : row + tokens] = ref[k, :, i * LANES : (i + 1) * LANES]
        stores.append(pltpu.make_async_copy(ready.at[k], out, out_sems.at[k]))
        stores[-1].start()
    for store in stores:
        store.wait()


def unpack_kernel(place, count, copies, *refs):
    homes, refs = refs[:count], refs[count:]
    dx_hbm, ddt_hbm, db_hbm, dc_hbm, dx_ref, db_ref, dc_ref, ddt_ref, db_wide, dc_wide, ddt_wide, sems = refs
    tokens, blocks, width = place.tokens, place.blocks, place.width
    heads = HEADS // count
    first = blocks * tokens
    moves = []

    def move(source, target):
        moves.append(pltpu.make_async_copy(source, target, sems.at[len(moves)]))
        moves[-1].start()

    if copies > 1:
        db_wide[...] = jnp.zeros_like(db_wide)
        dc_wide[...] = jnp.zeros_like(dc_wide)
    for k, home in enumerate(homes):
        source = partner(place, k)
        mine = pl.ds(lax.div(source, copies), tokens, stride=GROUPS)
        for to, at in ((db_wide, first), (dc_wide, first + tokens)):
            part = home[at : at + tokens, :].astype(F32)
            to[mine, :] = part if copies == 1 else to[mine, :] + part
        ddt_wide[pl.ds(source * heads, heads), :] = home[place.rows_out - TILE :, :].astype(F32)[:heads]
        for i in range(blocks):
            dx_ref[k, :, i * LANES : (i + 1) * LANES] = home[i * tokens : (i + 1) * tokens, :]
        move(dx_ref.at[k], dx_hbm.at[:, pl.ds(pl.multiple_of(source * width, LANES), width)])
    every = tokens * GROUPS
    db_ref[...] = db_wide[:every].reshape(db_ref.shape).astype(BF16)
    dc_ref[...] = dc_wide[:every].reshape(dc_ref.shape).astype(BF16)
    ddt_ref[...] = ddt_wide[...].astype(BF16)
    for source, target in ((db_ref, db_hbm), (dc_ref, dc_hbm), (ddt_ref, ddt_hbm)):
        move(source, target)
    for one in moves:
        one.wait()


def segment_decays(place, bufs, rate):
    dts = [place.dt(buf) for buf in bufs]
    cums = cumulate(cat([dt * rate for dt in dts], 0), False)
    cums = [cums[i * ROWS : (i + 1) * ROWS] for i in range(len(bufs))]
    starts, start = [], jnp.zeros((ROWS, 1), F32)
    for cum in cums:
        starts.append(start + cum)
        start = start + cum[:, place.tokens - 1 :]
    return dts, [start - one for one in starts], starts


def encode(value, scale):
    size = jnp.exp2(jnp.abs(value) * (CODE_SPAN / scale) - CODE_SPAN / 2)
    return jnp.where(value < 0.0, -size, size).astype(BF16)


def decode(code, scale):
    code = code.astype(F32)
    size = (jnp.log(jnp.abs(code)) * LOG2E + CODE_SPAN / 2) * (scale / CODE_SPAN)
    return jnp.where(code < 0.0, -size, size)


def encode_into(send_ref, value, logs):
    top = jnp.maximum(jnp.max(jnp.abs(value), axis=0, keepdims=True), 1e-30)
    scale = (top * 1.01).astype(BF16).astype(F32)
    send_ref[:STATE] = encode(value, scale)
    notes = [scale] + [part.astype(F32) for log in logs for part in split2(log[:1])]
    notes += [jnp.zeros((TILE - len(notes), value.shape[1]), F32)]
    send_ref[STATE:] = cat(notes, 0).astype(BF16)


def totals_kernel(place, turn, rate_ref, *refs):
    blocks, refs = refs[: place.half], refs[place.half :]
    others, refs = ([], refs) if turn else (refs[:3], refs[3:])
    buf, u_rows, u_parts, v_parts, *refs = refs
    width, tokens = place.width, place.tokens
    for k, block in enumerate(blocks):
        lo = lax.axis_index("lo") ^ k
        for at in range(0, place.rows_in, tokens):
            rows = slice(at, min(at + tokens, place.rows_in))
            buf[lo, rows] = block[rows]
    chunks = [buf.at[i] for i in range(place.half)]
    dts, ends, starts = segment_decays(place, chunks, rate_ref[...])
    for i, chunk in enumerate(chunks):
        u_rows[i] = dts[i] * jnp.exp(ends[i])
        rows = slice(i * tokens, (i + 1) * tokens)
        hi, lo = split2(spread_rows(u_rows[i], width) * cat(place.x(chunk), 1).astype(F32))
        u_parts[0, rows], u_parts[1, rows] = hi, lo
        start_wide = spread_rows(jnp.exp(starts[i]), width)
        hi, lo = split2(start_wide * cat(place.dy(chunk), 1).astype(F32))
        v_parts[0, rows], v_parts[1, rows] = hi, lo
    b_turned = jnp.transpose(cat([place.b(chunk) for chunk in chunks], 0).astype(F32)).astype(BF16)
    c_turned = jnp.transpose(cat([place.c(chunk) for chunk in chunks], 0).astype(F32)).astype(BF16)
    total_s = dot(b_turned, u_parts[0]) + dot(b_turned, u_parts[1])
    total_g = dot(c_turned, v_parts[0]) + dot(c_turned, v_parts[1])
    log = jnp.broadcast_to(start_wide[tokens - 1 :, :], (ROWS, width))
    front, early = lax.axis_index("hi") == 0, lax.axis_index("ctx") == 0
    middle = jnp.where(front, total_s, total_g)
    if turn:
        encode_into(refs[3], jnp.where(early, total_g, total_s), [])
        encode_into(refs[4], middle, [])
        for ref, value in zip(refs, (total_s, total_g, log)):
            ref[...] = value
        return
    own_ref, send_ref, middle_ref = refs
    other_s, other_g, other_log = (ref[...] for ref in others)
    logs = [jnp.where(early, log, other_log), jnp.where(early, other_log, log)]
    encode_into(send_ref, jnp.where(early, total_s, total_g), logs)
    encode_into(middle_ref, middle, [])
    own_ref[:STATE] = jnp.where(early, total_s, other_s)
    own_ref[STATE : 2 * STATE] = jnp.where(early, other_g, total_g)
    own_ref[2 * STATE :] = cat(logs, 0)


def head_sums(values, width):
    hi, lo = split2(values)
    picker = spread_matrix(2, width)
    return (dot_nt(picker, hi) + dot_nt(picker, lo))[:ROWS]


def fold(value):
    total = value[:ROWS]
    for i in range(1, value.shape[0] // ROWS):
        total = total + value[i * ROWS : (i + 1) * ROWS]
    return total


def middle_kernel(place, rate_ref, buf, dx_ref, ddt_ref, db_ref, dc_ref):
    rate, tokens, width = rate_ref[...], place.tokens, place.width
    chunks = [buf.at[i] for i in range(place.half)]
    dts = [place.dt(chunk) for chunk in chunks]
    cums = cumulate(cat([dt * rate for dt in dts], 0), False)
    cums = [cums[i * ROWS : (i + 1) * ROWS] for i in range(len(chunks))]
    ends = [cum[:, tokens - 1 :] for cum in cums]
    starts = [jnp.exp(cum) for cum in cums]

    us, vs, end_wides, adds_s, adds_g, through = [], [], [], [], [], []
    for i, chunk in enumerate(chunks):
        cols = columns(cat([dts[i] * jnp.exp(ends[i] - cums[i]), starts[i]], 0))
        end_wide, start_wide = widen(cols, 0, width), widen(cols, ROWS, width)
        u, v = split2(end_wide * cat(place.x(chunk), 1).astype(F32)), split2(start_wide * cat(place.dy(chunk), 1).astype(F32))
        b_here, c_here = place.b(chunk), place.c(chunk)
        adds_s.append(dot_tn(cat([b_here, b_here], 0), cat(list(u), 0)))
        adds_g.append(dot_tn(cat([c_here, c_here], 0), cat(list(v), 0)))
        through.append(start_wide[tokens - 1 :, :])
        us.append(u)
        vs.append(v)
        end_wides.append(end_wide)
    states, grads = [jnp.zeros((STATE, width), F32)], [jnp.zeros((STATE, width), F32)]
    for i in range(len(chunks) - 1):
        states.append(through[i] * states[-1] + adds_s[i])
        grads.append(through[-1 - i] * grads[-1] + adds_g[-1 - i])
    grads = grads[::-1]
    corners = head_sums(cat([fold(through[i] * (states[i] * grads[i])) for i in range(len(chunks))], 0), width)

    mask = upper(tokens, False)
    left = lax.broadcasted_iota(jnp.int32, (tokens, LANES), 1) < HEAD_DIM
    left, right = left.astype(F32).astype(BF16), (~left).astype(F32).astype(BF16)
    for i, chunk in enumerate(chunks):
        b_here, c_here = place.b(chunk), place.c(chunk)
        cum = cums[i] * LOG2E
        cols = jnp.transpose(cum - jnp.log(jnp.where(dts[i] > 0.0, dts[i], 1.0)) * LOG2E)
        k_two = dot_nt(b_here, c_here)
        s_hi, s_lo = split2(states[i])
        g_hi, g_lo = split2(grads[i])
        b_grad = end_wides[i] * dot(cat([b_here, b_here], 1), cat([g_hi, g_lo], 0))
        c_state = dot(cat([c_here, c_here], 1), cat([s_hi, s_lo], 0))
        one_sum = jnp.zeros((tokens, tokens), F32)
        rows, alongs = [], []
        for block, (x_here, dy_here) in enumerate(zip(place.x(chunk), place.dy(chunk))):
            lanes = slice(block * LANES, (block + 1) * LANES)
            sides = cat([dy_here * left, dy_here * right], 0)
            k_one = dot_nt(x_here, sides)
            tops, bottoms = [], []
            for side in range(2):
                head = 2 * block + side
                gap = jnp.where(mask, cum[head : head + 1, :] - cols[:, head : head + 1], -1e30)
                decay = jnp.exp2(gap)
                a_one = decay * k_one[:, side * tokens : (side + 1) * tokens]
                a_two = decay * k_two
                one_sum = one_sum + a_one
                rows.append(jnp.sum(a_one * k_two, axis=0, keepdims=True))
                hi_two, lo_two = split2(a_two)
                tops.append(hi_two)
                bottoms.append(lo_two)
            both = dot(cat([cat(tops, 1), cat(bottoms, 1)], 0), sides)
            dx = both[:tokens] + both[tokens:] + b_grad[:, lanes]
            dx_ref[i, :, lanes] = dx
            alongs.append(dx * x_here.astype(F32))
        if len(rows) < ROWS:
            rows.append(jnp.zeros((ROWS - len(rows), tokens), F32))
        db = dot(cat(list(split2(one_sum)), 1), cat([c_here, c_here], 0))
        dc = dot(cat(list(split2(jnp.transpose(one_sum))), 1), cat([b_here, b_here], 0))
        db_ref[i] = db + head_products(us[i], (g_hi, g_lo))
        dc_ref[i] = dc + head_products(vs[i], (s_hi, s_lo))
        sums = head_sums(cat([cat(alongs, 1), cat(place.dy(chunk), 1).astype(F32) * c_state], 0), width)
        along = sums[:, :tokens]
        later = starts[i] * sums[:, tokens:]
        corner = jnp.sum(corners[:, i * ROWS : (i + 1) * ROWS], axis=1, keepdims=True)
        flow = along - cat(rows, 0) - later
        dlog = corner + jnp.sum(later, axis=1, keepdims=True) + cumulate(flow, True)
        ddt_ref[i] = along / jnp.where(dts[i] > 0.0, dts[i], 1.0) + rate * dlog


def carried_in(own, first, first_middle, second, second_middle, seg, front):
    sent0, sent2, logs = own[:STATE], own[STATE : 2 * STATE], (own[2 * STATE : 2 * STATE + 1], own[2 * STATE + ROWS : 2 * STATE + ROWS + 1])
    early = lax.axis_index("ctx") == 0
    crossed, late = (decode(part[:STATE], part[STATE:].astype(F32)[:1]) for part in (first, second))
    got0, got2 = jnp.where(early, late, crossed), jnp.where(early, crossed, late)
    middle = jnp.where(front == early, second_middle[...].astype(F32), first_middle[...].astype(F32))
    got1 = decode(middle[:STATE], middle[STATE : STATE + 1])
    notes = second[STATE:].astype(F32)
    mine = jnp.where(front, logs[1], logs[0])
    other = jnp.where(front, notes[1:2] + notes[2:3], notes[3:4] + notes[4:5])
    far = got1 + other * (jnp.where(front, sent2, sent0) + mine * jnp.where(front, got2, got0))
    near = jnp.where(front, got0, got2) + other * jnp.where(front, sent0, sent2)
    none = jnp.zeros_like(far)
    states = [jnp.where(front, none, got0), jnp.where(front, near, far)]
    grads = [jnp.where(front, far, near), jnp.where(front, got2, none)]
    return [[jnp.where(here == 0, pair[0], pair[1]) for pair in (states, grads, logs)] for here in (seg, 1 - seg)]


def finish_kernel(place, turn, rate_ref, buf, u_rows, u_parts, v_parts, dx_in, ddt_in, db_in, dc_in, *refs):
    rate, tokens, width = rate_ref[...], place.tokens, place.width
    if turn == 0:
        got, refs = refs[:5], refs[5:]
        (state, grad, through), rest = carried_in(*got, lax.axis_index("ctx"), lax.axis_index("hi") == 0)
        for ref, value in zip(refs, rest):
            ref[...] = jnp.broadcast_to(value, ref.shape)
    else:
        state, grad, through = (ref[...] for ref in refs[:3])
        through = through[:1]
    *outs, out = refs[3:]
    s_hi, s_lo = split2(state)
    g_hi, g_lo = split2(grad)
    corner = jnp.sum(head_sums(fold(through * (grad * state)), width), axis=1, keepdims=True)
    chunks = [buf.at[i] for i in range(place.half)]
    b_all, c_all = cat([place.b(chunk) for chunk in chunks], 0), cat([place.c(chunk) for chunk in chunks], 0)
    b_grad = dot(cat([b_all, b_all], 1), cat([g_hi, g_lo], 0))
    c_state = dot(cat([c_all, c_all], 1), cat([s_hi, s_lo], 0))
    v_hi, v_lo = v_parts[0], v_parts[1]
    db = head_products((u_parts[0], u_parts[1]), (g_hi, g_lo))
    dc = head_products((v_hi, v_lo), (s_hi, s_lo))
    ins = []
    for i, chunk in enumerate(chunks):
        rows = slice(i * tokens, (i + 1) * tokens)
        extra = widen(columns(u_rows[i]), 0, width) * b_grad[rows]
        dx = (dx_in[i] + extra).astype(BF16)
        for block in range(place.blocks):
            out[i, block * tokens : (block + 1) * tokens, :] = dx[:, block * LANES : (block + 1) * LANES]
        ins.append(extra * cat(place.x(chunk), 1).astype(F32))
        first = place.blocks * tokens
        out[i, first : first + tokens, :] = (db_in[i] + db[rows]).astype(BF16)
        out[i, first + tokens : first + 2 * tokens, :] = (dc_in[i] + dc[rows]).astype(BF16)
    ins = head_sums(cat(ins, 0), width)
    laters = head_sums((v_hi.astype(F32) + v_lo.astype(F32)) * c_state, width)
    ins, laters = ([sums[:, i * tokens : (i + 1) * tokens] for i in range(place.half)] for sums in (ins, laters))
    over = cumulate(cat([one - other for one, other in zip(ins, laters)], 0), True)
    rest = corner
    for later in laters:
        rest = rest + jnp.sum(later, axis=1, keepdims=True)
    for i, chunk in enumerate(chunks):
        dlog = rest + over[i * ROWS : (i + 1) * ROWS]
        rest = rest + jnp.sum(ins[i] - laters[i], axis=1, keepdims=True)
        dt = place.dt(chunk)
        ddt = ddt_in[i] + ins[i] / jnp.where(dt > 0.0, dt, 1.0) + rate * dlog
        out[i, place.rows_out - TILE :, :] = cat([ddt, jnp.zeros_like(ddt)], 0).astype(BF16)
    for k, target in enumerate(outs):
        lo = lax.axis_index("lo") ^ k
        for at in range(0, place.rows_out, tokens):
            part = slice(at, min(at + tokens, place.rows_out))
            target[part] = out[lo, part]


def on_device(x_seq, dy_seq, dt_seq, a_log, b_seq, c_seq):
    tokens = x_seq.shape[0]
    half = lax.axis_size("lo")
    count = 2 * half
    heads = HEADS // count
    copies = count // GROUPS
    place = Place(tokens, half, heads * HEAD_DIM // LANES)
    width = place.width

    def after(value, *others):
        return lax.optimization_barrier((value, *others))[0]

    def swap(blocks, order, done):
        got = {0: blocks[0]}
        for i, k in enumerate(order):
            turn = (k % half) * 2 + k // half
            block = blocks[k]
            if i >= IN_FLIGHT:
                block = after(block, got[done[i - IN_FLIGHT]])
            got[k] = lax.ppermute(block, ("lo", "ctx"), [(j, j ^ turn) for j in range(count)])
        return [got[k] for k in range(count)]

    rates = -jnp.exp(lax.dynamic_slice_in_dim(a_log, lax.axis_index(("ctx", "lo")) * heads, heads))
    rate = jnp.broadcast_to(jnp.pad(rates, (0, ROWS - heads))[:, None], (ROWS, LANES))

    def f32(*shape):
        return jax.ShapeDtypeStruct(shape, F32)

    def bf16(*shape):
        return jax.ShapeDtypeStruct(shape, BF16)

    hbm, vmem = pl.BlockSpec(memory_space=pltpu.HBM), pl.BlockSpec(memory_space=pltpu.VMEM)
    params = pltpu.CompilerParams(vmem_limit_bytes=24 * 1024 * 1024)
    spaced = pltpu.VMEM((tokens * GROUPS + GROUPS, STATE), F32)
    wides = [spaced, spaced, pltpu.VMEM((HEADS, tokens), F32)]
    seqs = (b_seq, c_seq, dt_seq.T, x_seq, dy_seq)
    by_partner = [pltpu.VMEM((count, tokens, width), BF16)]

    sent = pl.pallas_call(
        functools.partial(pack_kernel, place, count, copies),
        in_specs=[hbm] * 5,
        out_specs=[hbm] * count,
        out_shape=[bf16(place.rows_in, LANES)] * count,
        scratch_shapes=[pltpu.VMEM(seq.shape, BF16) for seq in seqs[:3]]
        + wides
        + by_partner * 2
        + [pltpu.VMEM((count, place.rows_in, LANES), BF16), pltpu.SemaphoreType.DMA((3 + 2 * count,)), pltpu.SemaphoreType.DMA((count,))],
        compiler_params=pltpu.CompilerParams(vmem_limit_bytes=58 * 1024 * 1024),
        name="pack",
    )(*seqs)
    own_turns = [*range(half // 2, half), *range(1, half // 2)]
    other_turns = [half + k for k in own_turns]
    arrived = swap(sent, [*other_turns[:3], half, *other_turns[3:], *own_turns], [half, *other_turns, *own_turns])

    owned, coded = (2 * STATE + 2 * ROWS, width), (STATE + TILE, width)
    data_shapes = [bf16(half, place.rows_in, LANES), f32(half, ROWS, tokens)] + [bf16(2, half * tokens, width)] * 2
    carry_shapes = [f32(STATE, width), f32(STATE, width), f32(ROWS, width)]

    def totals(turn, blocks, others, shapes):
        return pl.pallas_call(
            functools.partial(totals_kernel, place, turn),
            in_specs=[vmem] * (1 + half + len(others)),
            out_specs=[vmem] * (4 + len(shapes)),
            out_shape=data_shapes + shapes,
            compiler_params=params,
            name="totals",
        )(rate, *blocks, *others)

    def cross(send, middle, early):
        pairs = [(0, 2), (3, 1)] if early else [(1, 3), (2, 0)]
        return lax.ppermute(send, "hi", [(0, 1), (1, 0)]), lax.ppermute(middle, ("hi", "ctx"), pairs)

    sends = [bf16(*coded)] * 2
    *data1, other_s, other_g, other_log, send, middle_send = totals(1, arrived[half:], [], carry_shapes + sends)
    first_send = send
    first, first_middle = cross(send, middle_send, True)
    *data0, own, send, middle_send = totals(0, [after(block, first_send) for block in arrived[:half]], [other_s, other_g, other_log], [f32(*owned)] + sends)
    second, second_middle = cross(send, middle_send, False)

    within = [f32(half, tokens, width), f32(half, ROWS, tokens), f32(half, tokens, STATE), f32(half, tokens, STATE)]
    def middle(data):
        return pl.pallas_call(
            functools.partial(middle_kernel, place),
            in_specs=[vmem] * 2,
            out_specs=[vmem] * 4,
            out_shape=within,
            compiler_params=params,
            cost_estimate=pl.CostEstimate(flops=3_000_000_000, bytes_accessed=10_000_000, transcendentals=1_000_000),
            name="middle",
        )(rate, data[0])

    def finish(turn, data, parts, others, shapes):
        return pl.pallas_call(
            functools.partial(finish_kernel, place, turn),
            in_specs=[vmem] * (9 + len(others)),
            out_specs=[vmem] * (half + len(shapes)),
            out_shape=shapes + [bf16(place.rows_out, LANES)] * half,
            scratch_shapes=[pltpu.VMEM((half, place.rows_out, LANES), BF16)],
            compiler_params=params,
            name="finish",
        )(rate, *data, *parts, *others)

    parts1, parts0 = middle(data1), middle(data0)
    second = after(second, parts1[0])
    state, grad, through, *outs0 = finish(0, data0, parts0, [own, first, first_middle, second, second_middle], carry_shapes)
    outs1 = finish(1, data1, parts1, [state, grad, through], [])
    turns = [*range(1, half), *range(half + 1, count), half]
    homes = swap([*outs0, *outs1], turns, turns)

    dx, ddt, db, dc = pl.pallas_call(
        functools.partial(unpack_kernel, place, count, copies),
        in_specs=[vmem] * count,
        out_specs=[hbm] * 4,
        out_shape=[bf16(*x_seq.shape), bf16(HEADS, tokens), bf16(*b_seq.shape), bf16(*c_seq.shape)],
        scratch_shapes=by_partner
        + [pltpu.VMEM(b_seq.shape, BF16), pltpu.VMEM(c_seq.shape, BF16), pltpu.VMEM((HEADS, tokens), BF16)]
        + wides
        + [pltpu.SemaphoreType.DMA((count + 3,))],
        compiler_params=params,
        name="unpack",
    )(*homes)
    return dx, ddt.T, db, dc


def solution(mesh):
    parts, head, ctx = (mesh.shape[name] for name in ("grp", "head", "ctx"))
    split = jax.sharding.Mesh(mesh.devices.reshape(parts, 2, head // 2, ctx), ("grp", "hi", "lo", "ctx"))
    spec = P(("grp", "ctx", "hi", "lo"))
    return jax.shard_map(
        on_device,
        mesh=split,
        in_specs=(spec, spec, spec, P(), spec, spec),
        out_specs=(spec, spec, spec, spec),
        check_vma=False,
    )
```

```python
import functools
from typing import NamedTuple

import jax
import jax.numpy as jnp
from jax import lax
from jax.experimental import pallas as pl
from jax.experimental.pallas import tpu as pltpu
from jax.sharding import PartitionSpec as P

HEADS = 64
HEAD_DIM = 64
STATE = 128
GROUPS = 8
LANES = 128
ROWS = 8
TILE = 16
LOG2E = 1.4426950408889634
CODE_SPAN = 250.0
IN_FLIGHT = 5
F32 = jnp.float32
BF16 = jnp.bfloat16


def split2(value):
    hi = value.astype(BF16)
    return hi, (value - hi.astype(F32)).astype(BF16)


def split3(value):
    hi = value.astype(BF16)
    rest = value - hi.astype(F32)
    mid = rest.astype(BF16)
    return hi, mid, (rest - mid.astype(F32)).astype(BF16)


def dot(a, b):
    return lax.dot_general(a, b, (((1,), (0,)), ((), ())), preferred_element_type=F32)


def dot_nt(a, b):
    return lax.dot_general(a, b, (((1,), (1,)), ((), ())), preferred_element_type=F32)


def dot_tn(a, b):
    return lax.dot_general(a, b, (((0,), (0,)), ((), ())), preferred_element_type=F32)


def cat(parts, axis):
    return jnp.concatenate(parts, axis=axis)


def upper(size, strict):
    row = lax.broadcasted_iota(jnp.int32, (size, size), 0)
    col = lax.broadcasted_iota(jnp.int32, (size, size), 1)
    return row < col if strict else row <= col


def cumulate(rows, strict):
    tri = upper(rows.shape[1], strict).astype(F32).astype(BF16)
    sums = dot(cat([part.astype(F32) for part in split3(rows)], 0).astype(BF16), tri)
    size = rows.shape[0]
    return sums[:size] + sums[size : 2 * size] + sums[2 * size :]


def spread_matrix(terms, width):
    row = lax.broadcasted_iota(jnp.int32, (terms * ROWS, width), 0)
    col = lax.broadcasted_iota(jnp.int32, (terms * ROWS, width), 1)
    return (row % ROWS == col // HEAD_DIM).astype(F32).astype(BF16)


def spread_rows(rows, width):
    hi, lo = split2(rows)
    terms = cat([hi.astype(F32), lo.astype(F32)], 0).astype(BF16)
    return dot_tn(terms, spread_matrix(2, width))


def columns(rows):
    return jnp.transpose(cat([rows, jnp.zeros((LANES - rows.shape[0], rows.shape[1]), F32)], 0))


def widen(cols, first, width):
    lane = lax.broadcasted_iota(jnp.int32, cols.shape, 1)
    heads = [first + lane // HEAD_DIM + 2 * block for block in range(width // LANES)]
    return cat([jnp.take_along_axis(cols, head, axis=1) for head in heads], 1)


def head_products(values, factors):
    rows = values[0].shape[0]
    both = dot_nt(cat(list(values), 0), cat(list(factors), 0))
    size = factors[0].shape[0]
    return (both[:rows, :size] + (both[:rows, size:] + both[rows:, :size])) + both[rows:, size:]


class Place(NamedTuple):
    tokens: int
    half: int
    blocks: int

    @property
    def width(self):
        return self.blocks * LANES

    @property
    def b_row(self):
        return 2 * self.blocks * self.tokens

    @property
    def dt_row(self):
        return self.b_row + 2 * self.tokens

    @property
    def rows_in(self):
        return self.dt_row + TILE

    @property
    def rows_out(self):
        return (self.blocks + 2) * self.tokens + TILE

    def x(self, buf):
        return [buf[i * self.tokens : (i + 1) * self.tokens, :] for i in range(self.blocks)]

    def dy(self, buf):
        return [buf[i * self.tokens : (i + 1) * self.tokens, :] for i in range(self.blocks, 2 * self.blocks)]

    def b(self, buf):
        return buf[self.b_row : self.b_row + self.tokens, :]

    def c(self, buf):
        return buf[self.b_row + self.tokens : self.b_row + 2 * self.tokens, :]

    def dt(self, buf):
        return buf[self.dt_row : self.dt_row + TILE, :].astype(F32)[:ROWS]


def partner(place, k):
    return (lax.axis_index("ctx") ^ (k // place.half)) * place.half + (lax.axis_index("lo") ^ (k % place.half))


def pack_kernel(place, count, copies, *refs):
    (b_hbm, c_hbm, dt_hbm, x_hbm, dy_hbm), outs, refs = refs[:5], refs[5 : 5 + count], refs[5 + count :]
    b_ref, c_ref, dt_ref, b_wide, c_wide, dt_wide, x_ref, dy_ref, ready, sems, out_sems = refs
    tokens, blocks, width = place.tokens, place.blocks, place.width
    heads = HEADS // count
    dests = [partner(place, k) for k in range(count)]
    loads = [(b_hbm, b_ref), (c_hbm, c_ref), (dt_hbm, dt_ref)]
    for k, dest in enumerate(dests):
        columns = pl.ds(pl.multiple_of(dest * width, LANES), width)
        loads += [(x_hbm.at[:, columns], x_ref.at[k]), (dy_hbm.at[:, columns], dy_ref.at[k])]
    loads = [pltpu.make_async_copy(source, target, sems.at[i]) for i, (source, target) in enumerate(loads)]
    for load in loads:
        load.start()
    for load in loads[:3]:
        load.wait()
    every = tokens * GROUPS
    b_wide[:every] = b_ref[...].astype(F32).reshape(every, STATE)
    c_wide[:every] = c_ref[...].astype(F32).reshape(every, STATE)
    dt_wide[...] = dt_ref[...].astype(F32)
    stores = []
    for k, (dest, out) in enumerate(zip(dests, outs)):
        mine = pl.ds(lax.div(dest, copies), tokens, stride=GROUPS)
        ready[k, place.b_row : place.b_row + tokens] = b_wide[mine, :].astype(BF16)
        ready[k, place.b_row + tokens : place.dt_row] = c_wide[mine, :].astype(BF16)
        dt = dt_wide[pl.ds(dest * heads, heads), :]
        ready[k, place.dt_row :] = cat([dt, jnp.zeros((TILE - heads, tokens), F32)], 0).astype(BF16)
        for load in loads[3 + 2 * k : 5 + 2 * k]:
            load.wait()
        for part, ref in enumerate((x_ref, dy_ref)):
            for i in range(blocks):
                row = (part * blocks + i) * tokens
                ready[k, row : row + tokens] = ref[k, :, i * LANES : (i + 1) * LANES]
        stores.append(pltpu.make_async_copy(ready.at[k], out, out_sems.at[k]))
        stores[-1].start()
    for store in stores:
        store.wait()


def unpack_kernel(place, count, copies, *refs):
    homes, refs = refs[:count], refs[count:]
    dx_hbm, ddt_hbm, db_hbm, dc_hbm, dx_ref, db_ref, dc_ref, ddt_ref, db_wide, dc_wide, ddt_wide, sems = refs
    tokens, blocks, width = place.tokens, place.blocks, place.width
    heads = HEADS // count
    first = blocks * tokens
    moves = []

    def move(source, target):
        moves.append(pltpu.make_async_copy(source, target, sems.at[len(moves)]))
        moves[-1].start()

    if copies > 1:
        db_wide[...] = jnp.zeros_like(db_wide)
        dc_wide[...] = jnp.zeros_like(dc_wide)
    for k, home in enumerate(homes):
        source = partner(place, k)
        mine = pl.ds(lax.div(source, copies), tokens, stride=GROUPS)
        for to, at in ((db_wide, first), (dc_wide, first + tokens)):
            part = home[at : at + tokens, :].astype(F32)
            to[mine, :] = part if copies == 1 else to[mine, :] + part
        ddt_wide[pl.ds(source * heads, heads), :] = home[place.rows_out - TILE :, :].astype(F32)[:heads]
        for i in range(blocks):
            dx_ref[k, :, i * LANES : (i + 1) * LANES] = home[i * tokens : (i + 1) * tokens, :]
        move(dx_ref.at[k], dx_hbm.at[:, pl.ds(pl.multiple_of(source * width, LANES), width)])
    every = tokens * GROUPS
    db_ref[...] = db_wide[:every].reshape(db_ref.shape).astype(BF16)
    dc_ref[...] = dc_wide[:every].reshape(dc_ref.shape).astype(BF16)
    ddt_ref[...] = ddt_wide[...].astype(BF16)
    for source, target in ((db_ref, db_hbm), (dc_ref, dc_hbm), (ddt_ref, ddt_hbm)):
        move(source, target)
    for one in moves:
        one.wait()


def segment_decays(place, bufs, rate):
    dts = [place.dt(buf) for buf in bufs]
    cums = cumulate(cat([dt * rate for dt in dts], 0), False)
    cums = [cums[i * ROWS : (i + 1) * ROWS] for i in range(len(bufs))]
    starts, start = [], jnp.zeros((ROWS, 1), F32)
    for cum in cums:
        starts.append(start + cum)
        start = start + cum[:, place.tokens - 1 :]
    return dts, [start - one for one in starts], starts


def encode(value, scale):
    size = jnp.exp2(jnp.abs(value) * (CODE_SPAN / scale) - CODE_SPAN / 2)
    return jnp.where(value < 0.0, -size, size).astype(BF16)


def decode(code, scale):
    code = code.astype(F32)
    size = jnp.log(jnp.abs(code)) * (scale * (LOG2E / CODE_SPAN)) + scale / 2
    return jnp.where(code < 0.0, -size, size)


def encode_into(send_ref, value, logs):
    top = jnp.maximum(jnp.max(jnp.abs(value), axis=0, keepdims=True), 1e-30)
    scale = (top * 1.01).astype(BF16).astype(F32)
    send_ref[:STATE] = encode(value, scale)
    notes = [scale] + [part.astype(F32) for log in logs for part in split2(log[:1])]
    notes += [jnp.zeros((TILE - len(notes), value.shape[1]), F32)]
    send_ref[STATE:] = cat(notes, 0).astype(BF16)


def totals_kernel(place, turn, rate_ref, *refs):
    blocks, refs = refs[: place.half], refs[place.half :]
    others, refs = ([], refs) if turn else (refs[:3], refs[3:])
    buf, u_rows, v_rows, u_parts, v_parts, *refs = refs
    width, tokens = place.width, place.tokens
    for k, block in enumerate(blocks):
        lo = lax.axis_index("lo") ^ k
        for at in range(0, place.rows_in, tokens):
            rows = slice(at, min(at + tokens, place.rows_in))
            buf[lo, rows] = block[rows]
    chunks = [buf.at[i] for i in range(place.half)]
    dts, ends, starts = segment_decays(place, chunks, rate_ref[...])
    for i, chunk in enumerate(chunks):
        u_rows[i] = dts[i] * jnp.exp(ends[i])
        rows = slice(i * tokens, (i + 1) * tokens)
        hi, lo = split2(spread_rows(u_rows[i], width) * cat(place.x(chunk), 1).astype(F32))
        u_parts[0, rows], u_parts[1, rows] = hi, lo
        v_rows[i] = jnp.exp(starts[i])
        start_wide = spread_rows(v_rows[i], width)
        hi, lo = split2(start_wide * cat(place.dy(chunk), 1).astype(F32))
        v_parts[0, rows], v_parts[1, rows] = hi, lo
    b_turned = jnp.transpose(cat([place.b(chunk) for chunk in chunks], 0).astype(F32)).astype(BF16)
    c_turned = jnp.transpose(cat([place.c(chunk) for chunk in chunks], 0).astype(F32)).astype(BF16)
    total_s = dot(b_turned, u_parts[0]) + dot(b_turned, u_parts[1])
    total_g = dot(c_turned, v_parts[0]) + dot(c_turned, v_parts[1])
    log = jnp.broadcast_to(start_wide[tokens - 1 :, :], (ROWS, width))
    front, early = lax.axis_index("hi") == 0, lax.axis_index("ctx") == 0
    middle = jnp.where(front, total_s, total_g)
    if turn:
        encode_into(refs[3], jnp.where(early, total_g, total_s), [])
        encode_into(refs[4], middle, [])
        for ref, value in zip(refs, (total_s, total_g, log)):
            ref[...] = value
        return
    own_ref, send_ref, middle_ref = refs
    other_s, other_g, other_log = (ref[...] for ref in others)
    logs = [jnp.where(early, log, other_log), jnp.where(early, other_log, log)]
    encode_into(send_ref, jnp.where(early, total_s, total_g), logs)
    encode_into(middle_ref, middle, [])
    own_ref[:STATE] = jnp.where(early, total_s, other_s)
    own_ref[STATE : 2 * STATE] = jnp.where(early, other_g, total_g)
    own_ref[2 * STATE :] = cat(logs, 0)


def head_sums(values, width):
    hi, lo = split2(values)
    picker = spread_matrix(2, width)
    return (dot_nt(picker, hi) + dot_nt(picker, lo))[:ROWS]


def fold(value):
    total = value[:ROWS]
    for i in range(1, value.shape[0] // ROWS):
        total = total + value[i * ROWS : (i + 1) * ROWS]
    return total


def middle_kernel(place, rate_ref, buf, dx_ref, ddt_ref, db_ref, dc_ref):
    rate, tokens, width = rate_ref[...], place.tokens, place.width
    chunks = [buf.at[i] for i in range(place.half)]
    dts = [place.dt(chunk) for chunk in chunks]
    cums = cumulate(cat([dt * rate for dt in dts], 0), False)
    cums = [cums[i * ROWS : (i + 1) * ROWS] for i in range(len(chunks))]
    ends = [cum[:, tokens - 1 :] for cum in cums]
    starts = [jnp.exp(cum) for cum in cums]

    us, vs, end_wides, adds_s, adds_g, through = [], [], [], [], [], []
    for i, chunk in enumerate(chunks):
        cols = columns(cat([dts[i] * jnp.exp(ends[i] - cums[i]), starts[i]], 0))
        end_wide, start_wide = widen(cols, 0, width), widen(cols, ROWS, width)
        u, v = split2(end_wide * cat(place.x(chunk), 1).astype(F32)), split2(start_wide * cat(place.dy(chunk), 1).astype(F32))
        b_here, c_here = place.b(chunk), place.c(chunk)
        adds_s.append(dot_tn(cat([b_here, b_here], 0), cat(list(u), 0)))
        adds_g.append(dot_tn(cat([c_here, c_here], 0), cat(list(v), 0)))
        through.append(start_wide[tokens - 1 :, :])
        us.append(u)
        vs.append(v)
        end_wides.append(end_wide)
    states, grads = [jnp.zeros((STATE, width), F32)], [jnp.zeros((STATE, width), F32)]
    for i in range(len(chunks) - 1):
        states.append(through[i] * states[-1] + adds_s[i])
        grads.append(through[-1 - i] * grads[-1] + adds_g[-1 - i])
    grads = grads[::-1]
    corners = head_sums(cat([fold(through[i] * (states[i] * grads[i])) for i in range(len(chunks))], 0), width)

    mask = upper(tokens, False)
    left = lax.broadcasted_iota(jnp.int32, (tokens, LANES), 1) < HEAD_DIM
    left, right = left.astype(F32).astype(BF16), (~left).astype(F32).astype(BF16)
    for i, chunk in enumerate(chunks):
        b_here, c_here = place.b(chunk), place.c(chunk)
        cum = cums[i] * LOG2E
        cols = jnp.transpose(cum - jnp.log(jnp.where(dts[i] > 0.0, dts[i], 1.0)) * LOG2E)
        k_two = dot_nt(b_here, c_here)
        s_hi, s_lo = split2(states[i])
        g_hi, g_lo = split2(grads[i])
        b_grad = end_wides[i] * dot(cat([b_here, b_here], 1), cat([g_hi, g_lo], 0))
        c_state = dot(cat([c_here, c_here], 1), cat([s_hi, s_lo], 0))
        one_sum = jnp.zeros((tokens, tokens), F32)
        rows, alongs = [], []
        for block, (x_here, dy_here) in enumerate(zip(place.x(chunk), place.dy(chunk))):
            lanes = slice(block * LANES, (block + 1) * LANES)
            sides = cat([dy_here * left, dy_here * right], 0)
            k_one = dot_nt(x_here, sides)
            tops, bottoms = [], []
            for side in range(2):
                head = 2 * block + side
                gap = jnp.where(mask, cum[head : head + 1, :] - cols[:, head : head + 1], -1e30)
                decay = jnp.exp2(gap)
                a_one = decay * k_one[:, side * tokens : (side + 1) * tokens]
                a_two = decay * k_two
                one_sum = one_sum + a_one
                rows.append(jnp.sum(a_one * k_two, axis=0, keepdims=True))
                hi_two, lo_two = split2(a_two)
                tops.append(hi_two)
                bottoms.append(lo_two)
            both = dot(cat([cat(tops, 1), cat(bottoms, 1)], 0), sides)
            dx = both[:tokens] + both[tokens:] + b_grad[:, lanes]
            dx_ref[i, :, lanes] = dx
            alongs.append(dx * x_here.astype(F32))
        if len(rows) < ROWS:
            rows.append(jnp.zeros((ROWS - len(rows), tokens), F32))
        db = dot(cat(list(split2(one_sum)), 1), cat([c_here, c_here], 0))
        dc = dot(cat(list(split2(jnp.transpose(one_sum))), 1), cat([b_here, b_here], 0))
        db_ref[i] = db + head_products(us[i], (g_hi, g_lo))
        dc_ref[i] = dc + head_products(vs[i], (s_hi, s_lo))
        sums = head_sums(cat([cat(alongs, 1), cat(place.dy(chunk), 1).astype(F32) * c_state], 0), width)
        along = sums[:, :tokens]
        later = starts[i] * sums[:, tokens:]
        corner = jnp.sum(corners[:, i * ROWS : (i + 1) * ROWS], axis=1, keepdims=True)
        flow = along - cat(rows, 0) - later
        dlog = corner + jnp.sum(later, axis=1, keepdims=True) + cumulate(flow, True)
        ddt_ref[i] = along / jnp.where(dts[i] > 0.0, dts[i], 1.0) + rate * dlog


def carried_in(own, first, first_middle, second, second_middle, seg, front):
    sent0, sent2, logs = own[:STATE], own[STATE : 2 * STATE], (own[2 * STATE : 2 * STATE + 1], own[2 * STATE + ROWS : 2 * STATE + ROWS + 1])
    early = lax.axis_index("ctx") == 0
    crossed, late = (decode(part[:STATE], part[STATE:].astype(F32)[:1]) for part in (first, second))
    got0, got2 = jnp.where(early, late, crossed), jnp.where(early, crossed, late)
    middle = jnp.where(front == early, second_middle[...].astype(F32), first_middle[...].astype(F32))
    got1 = decode(middle[:STATE], middle[STATE : STATE + 1])
    notes = second[STATE:].astype(F32)
    mine = jnp.where(front, logs[1], logs[0])
    other = jnp.where(front, notes[1:2] + notes[2:3], notes[3:4] + notes[4:5])
    far = got1 + other * (jnp.where(front, sent2, sent0) + mine * jnp.where(front, got2, got0))
    near = jnp.where(front, got0, got2) + other * jnp.where(front, sent0, sent2)
    none = jnp.zeros_like(far)
    states = [jnp.where(front, none, got0), jnp.where(front, near, far)]
    grads = [jnp.where(front, far, near), jnp.where(front, got2, none)]
    return [[jnp.where(here == 0, pair[0], pair[1]) for pair in (states, grads, logs)] for here in (seg, 1 - seg)]


def finish_kernel(place, turn, rate_ref, buf, u_rows, v_rows, u_parts, v_parts, dx_in, ddt_in, db_in, dc_in, *refs):
    rate, tokens, width = rate_ref[...], place.tokens, place.width
    if turn == 0:
        got, refs = refs[:5], refs[5:]
        (state, grad, through), rest = carried_in(*got, lax.axis_index("ctx"), lax.axis_index("hi") == 0)
        for ref, value in zip(refs, rest):
            ref[...] = jnp.broadcast_to(value, ref.shape)
    else:
        state, grad, through = (ref[...] for ref in refs[:3])
        through = through[:1]
    *outs, out = refs[3:]
    s_hi, s_lo = split2(state)
    g_hi, g_lo = split2(grad)
    corner = jnp.sum(head_sums(fold(through * (grad * state)), width), axis=1, keepdims=True)
    chunks = [buf.at[i] for i in range(place.half)]
    b_all, c_all = cat([place.b(chunk) for chunk in chunks], 0), cat([place.c(chunk) for chunk in chunks], 0)
    b_grad = dot(cat([b_all, b_all], 1), cat([g_hi, g_lo], 0))
    c_state = dot(cat([c_all, c_all], 1), cat([s_hi, s_lo], 0))
    db = head_products((u_parts[0], u_parts[1]), (g_hi, g_lo))
    dc = head_products((v_parts[0], v_parts[1]), (s_hi, s_lo))
    ins = []
    for i, chunk in enumerate(chunks):
        rows = slice(i * tokens, (i + 1) * tokens)
        extra = widen(columns(u_rows[i]), 0, width) * b_grad[rows]
        dx = (dx_in[i] + extra).astype(BF16)
        for block in range(place.blocks):
            out[i, block * tokens : (block + 1) * tokens, :] = dx[:, block * LANES : (block + 1) * LANES]
        ins.append(extra * cat(place.x(chunk), 1).astype(F32))
        first = place.blocks * tokens
        out[i, first : first + tokens, :] = (db_in[i] + db[rows]).astype(BF16)
        out[i, first + tokens : first + 2 * tokens, :] = (dc_in[i] + dc[rows]).astype(BF16)
    ins = head_sums(cat(ins, 0), width)
    laters = head_sums(cat([cat(place.dy(chunk), 1) for chunk in chunks], 0).astype(F32) * c_state, width)
    ins, laters = ([sums[:, i * tokens : (i + 1) * tokens] for i in range(place.half)] for sums in (ins, laters))
    laters = [v_rows[i] * later for i, later in enumerate(laters)]
    over = cumulate(cat([one - other for one, other in zip(ins, laters)], 0), True)
    rest = corner
    for later in laters:
        rest = rest + jnp.sum(later, axis=1, keepdims=True)
    for i, chunk in enumerate(chunks):
        dlog = rest + over[i * ROWS : (i + 1) * ROWS]
        rest = rest + jnp.sum(ins[i] - laters[i], axis=1, keepdims=True)
        dt = place.dt(chunk)
        ddt = ddt_in[i] + ins[i] / jnp.where(dt > 0.0, dt, 1.0) + rate * dlog
        out[i, place.rows_out - TILE :, :] = cat([ddt, jnp.zeros_like(ddt)], 0).astype(BF16)
    for k, target in enumerate(outs):
        lo = lax.axis_index("lo") ^ k
        for at in range(0, place.rows_out, tokens):
            part = slice(at, min(at + tokens, place.rows_out))
            target[part] = out[lo, part]


def on_device(x_seq, dy_seq, dt_seq, a_log, b_seq, c_seq):
    tokens = x_seq.shape[0]
    half = lax.axis_size("lo")
    count = 2 * half
    heads = HEADS // count
    copies = count // GROUPS
    place = Place(tokens, half, heads * HEAD_DIM // LANES)
    width = place.width

    def after(value, *others):
        return lax.optimization_barrier((value, *others))[0]

    def swap(blocks, order, done):
        got = {0: blocks[0]}
        for i, k in enumerate(order):
            turn = (k % half) * 2 + k // half
            block = blocks[k]
            if i >= IN_FLIGHT:
                block = after(block, got[done[i - IN_FLIGHT]])
            got[k] = lax.ppermute(block, ("lo", "ctx"), [(j, j ^ turn) for j in range(count)])
        return [got[k] for k in range(count)]

    rates = -jnp.exp(lax.dynamic_slice_in_dim(a_log, lax.axis_index(("ctx", "lo")) * heads, heads))
    rate = jnp.broadcast_to(jnp.pad(rates, (0, ROWS - heads))[:, None], (ROWS, LANES))

    def f32(*shape):
        return jax.ShapeDtypeStruct(shape, F32)

    def bf16(*shape):
        return jax.ShapeDtypeStruct(shape, BF16)

    hbm, vmem = pl.BlockSpec(memory_space=pltpu.HBM), pl.BlockSpec(memory_space=pltpu.VMEM)
    params = pltpu.CompilerParams(vmem_limit_bytes=24 * 1024 * 1024)
    spaced = pltpu.VMEM((tokens * GROUPS + GROUPS, STATE), F32)
    wides = [spaced, spaced, pltpu.VMEM((HEADS, tokens), F32)]
    seqs = (b_seq, c_seq, dt_seq.T, x_seq, dy_seq)
    by_partner = [pltpu.VMEM((count, tokens, width), BF16)]

    sent = pl.pallas_call(
        functools.partial(pack_kernel, place, count, copies),
        in_specs=[hbm] * 5,
        out_specs=[hbm] * count,
        out_shape=[bf16(place.rows_in, LANES)] * count,
        scratch_shapes=[pltpu.VMEM(seq.shape, BF16) for seq in seqs[:3]]
        + wides
        + by_partner * 2
        + [pltpu.VMEM((count, place.rows_in, LANES), BF16), pltpu.SemaphoreType.DMA((3 + 2 * count,)), pltpu.SemaphoreType.DMA((count,))],
        compiler_params=pltpu.CompilerParams(vmem_limit_bytes=58 * 1024 * 1024),
        name="pack",
    )(*seqs)
    own_turns = [*range(half // 2, half), *range(1, half // 2)]
    other_turns = [half + k for k in own_turns]
    arrived = swap(sent, [*other_turns[:3], half, *other_turns[3:], *own_turns], [half, *other_turns, *own_turns])

    owned, coded = (2 * STATE + 2 * ROWS, width), (STATE + TILE, width)
    data_shapes = [bf16(half, place.rows_in, LANES)] + [f32(half, ROWS, tokens)] * 2 + [bf16(2, half * tokens, width)] * 2
    carry_shapes = [f32(STATE, width), f32(STATE, width), f32(ROWS, width)]

    def totals(turn, blocks, others, shapes):
        return pl.pallas_call(
            functools.partial(totals_kernel, place, turn),
            in_specs=[vmem] * (1 + half + len(others)),
            out_specs=[vmem] * (5 + len(shapes)),
            out_shape=data_shapes + shapes,
            compiler_params=params,
            name="totals",
        )(rate, *blocks, *others)

    def cross(send, middle, early):
        pairs = [(0, 2), (3, 1)] if early else [(1, 3), (2, 0)]
        return lax.ppermute(send, "hi", [(0, 1), (1, 0)]), lax.ppermute(middle, ("hi", "ctx"), pairs)

    sends = [bf16(*coded)] * 2
    *data1, other_s, other_g, other_log, send, middle_send = totals(1, arrived[half:], [], carry_shapes + sends)
    first_send = send
    first, first_middle = cross(send, middle_send, True)
    *data0, own, send, middle_send = totals(0, [after(block, first_send) for block in arrived[:half]], [other_s, other_g, other_log], [f32(*owned)] + sends)
    second, second_middle = cross(send, middle_send, False)

    within = [f32(half, tokens, width), f32(half, ROWS, tokens), f32(half, tokens, STATE), f32(half, tokens, STATE)]
    def middle(data):
        return pl.pallas_call(
            functools.partial(middle_kernel, place),
            in_specs=[vmem] * 2,
            out_specs=[vmem] * 4,
            out_shape=within,
            compiler_params=params,
            cost_estimate=pl.CostEstimate(flops=3_000_000_000, bytes_accessed=10_000_000, transcendentals=1_000_000),
            name="middle",
        )(rate, data[0])

    def finish(turn, data, parts, others, shapes):
        return pl.pallas_call(
            functools.partial(finish_kernel, place, turn),
            in_specs=[vmem] * (10 + len(others)),
            out_specs=[vmem] * (half + len(shapes)),
            out_shape=shapes + [bf16(place.rows_out, LANES)] * half,
            scratch_shapes=[pltpu.VMEM((half, place.rows_out, LANES), BF16)],
            compiler_params=params,
            name="finish",
        )(rate, *data, *parts, *others)

    parts1, parts0 = middle(data1), middle(data0)
    second = after(second, parts1[0])
    state, grad, through, *outs0 = finish(0, data0, parts0, [own, first, first_middle, second, second_middle], carry_shapes)
    outs1 = finish(1, data1, parts1, [state, grad, through], [])
    turns = [*range(1, half), *range(half + 1, count), half]
    homes = swap([*outs0, *outs1], turns, turns)

    dx, ddt, db, dc = pl.pallas_call(
        functools.partial(unpack_kernel, place, count, copies),
        in_specs=[vmem] * count,
        out_specs=[hbm] * 4,
        out_shape=[bf16(*x_seq.shape), bf16(HEADS, tokens), bf16(*b_seq.shape), bf16(*c_seq.shape)],
        scratch_shapes=by_partner
        + [pltpu.VMEM(b_seq.shape, BF16), pltpu.VMEM(c_seq.shape, BF16), pltpu.VMEM((HEADS, tokens), BF16)]
        + wides
        + [pltpu.SemaphoreType.DMA((count + 3,))],
        compiler_params=params,
        name="unpack",
    )(*homes)
    return dx, ddt.T, db, dc


def solution(mesh):
    parts, head, ctx = (mesh.shape[name] for name in ("grp", "head", "ctx"))
    split = jax.sharding.Mesh(mesh.devices.reshape(parts, 2, head // 2, ctx), ("grp", "hi", "lo", "ctx"))
    spec = P(("grp", "ctx", "hi", "lo"))
    return jax.shard_map(
        on_device,
        mesh=split,
        in_specs=(spec, spec, spec, P(), spec, spec),
        out_specs=(spec, spec, spec, spec),
        check_vma=False,
    )
```
